32 devices in a mesh: parts: 2 (over y), patch: 4 (over z), grp: 2 (over x), col: 2 (over core).
Axes of the slice: x: 2, y: 2, z: 4, core: 2. Of those that a mesh axis runs over, the one named last changes fastest.
Arguments:
- query_vectors: bfloat16 [2048, 1024], P(('parts', 'patch', 'grp'), 'col'), parts along dimension 0, may hold values from -180 to 180
- key_vectors: bfloat16 [2048, 1024], P(('parts', 'patch', 'grp'), 'col'), parts along dimension 0, may hold values from -6 to 6
- value_vectors: bfloat16 [2048, 1024], P(('parts', 'patch', 'grp'), 'col'), parts along dimension 0, may hold values from -6 to 6
- residual: bfloat16 [2048, 1024], P(('parts', 'patch', 'grp'), 'col'), parts along dimension 0, may hold values from -6 to 6
- neighbor_ids: int32 [16, 2], P(('parts', 'patch', 'grp')), parts along dimension 0, may hold values from 0 to 1, as said below
- neighbor_count: int32 [16], P(('parts', 'patch', 'grp')), parts along dimension 0, may hold values from 1 to 2
- output_weight: bfloat16 [1024, 1024], P('col'), may hold values from -0.1875 to 0.1875
- norm_gain: float32 [1024], P('col'), may hold values from 0.25 to 1.75
- up_weight: bfloat16 [1024, 4096], P(None, ('grp', 'col')), may hold values from -0.1875 to 0.1875
- down_weight: bfloat16 [4096, 1024], P(('grp', 'col')), may hold values from -0.09375 to 0.09375
- cotangent: bfloat16 [2048, 1024], P(('parts', 'patch', 'grp'), 'col'), parts along dimension 0, may hold values from -6 to 6
Outputs:
- layer_out: bfloat16 [2048, 1024], P(('parts', 'patch', 'grp'), 'col'), parts along dimension 0
- up_grad: float32 [2048, 4096], P('parts', ('grp', 'col')), parts along dimension 0
- down_grad: float32 [8192, 1024], P(('parts', 'grp', 'col')), parts along dimension 0
The draws below stay inside these ranges and needn't reach their ends.
There are 2 independent parts, one for each index of `parts`. The reference program is written for one: setup_inputs(seed, part) draws one part's arguments, and reference() takes and returns one part's arrays. A program takes and returns all parts, laid end to end along the dimension named above; an argument that names none is the same for every part. Nothing has to cross between parts.
Inputs may be any that keep to these rules, and one draw needn't show every extreme that they name: `neighbor_ids`: entry 0 of row b is b % 2; the other entries of a row are distinct other indices of the group; entries past neighbor_count[b] are valid indices but unused.
All inputs are finite; a program needn't handle non-finite values.
Results may differ from the reference program's by a relative error of at most 0.012.
Values may be sent and summed in bfloat16 or wider, within the bound.
No kernel may reach another device: no remote copies, remote signals or barrier semaphores. Data moves between devices by JAX's collectives and lax.ppermute only.
A program may use at most 64 MiB of HBM per device.

```python
import jax
import jax.numpy as jnp
from jax import lax

HEADS = 16
HEAD = 64
D = 1024
FF = 4096
BLK = 128
TOKENS = 1024
BLOCKS = 8
GROUP_BLOCKS = 2
MAXN = 2
PANEL = 1024


def shared_keys(key):
    return jnp.clip(jax.random.normal(jax.random.fold_in(key, 11), (TOKENS, D), jnp.float32), -6.0, 6.0)


def draw_key_vectors(key, part):
    return shared_keys(key).astype(jnp.bfloat16)


def draw_query_vectors(key, part):
    drawn = jnp.clip(jax.random.normal(jax.random.fold_in(key, 12), (TOKENS, D), jnp.float32), -6.0, 6.0)
    return drawn.astype(jnp.bfloat16)


def draw_neighbor_ids(key, part):
    own_index = jnp.arange(BLOCKS, dtype=jnp.int32) % GROUP_BLOCKS
    row_keys = jax.random.split(jax.random.fold_in(key, 21), BLOCKS)
    offsets = jax.vmap(lambda row_key: jax.random.permutation(row_key, GROUP_BLOCKS - 1)[:MAXN - 1] + 1)(row_keys)
    others = (own_index[:, None] + offsets.astype(jnp.int32)) % GROUP_BLOCKS
    return jnp.concatenate([own_index[:, None], others], axis=1).astype(jnp.int32)


def draw_neighbor_count(key, part):
    counts = jax.random.randint(jax.random.fold_in(key, 22), (BLOCKS,), 1, MAXN + 1).astype(jnp.int32)
    return counts.at[0].set(MAXN).astype(jnp.int32)


def block_levels(rng, dims, shards, smallest, high):
    def one(position, blocks):
        heights = jax.random.uniform(jax.random.fold_in(jax.random.fold_in(rng, 6), position), (blocks,), jnp.float32, smallest / len(shards), high / len(shards))
        return jnp.repeat(jnp.exp(heights), dims[position] // blocks).reshape((-1,) + (1,) * (len(dims) - position - 1))

    loudness = one(*shards[0])
    for cut in shards[1:]:
        loudness = loudness * one(*cut)
    return loudness


def bell_draw(stream_key, dims, deviation, limit, cuts=(), held_as=jnp.bfloat16):
    gain = block_levels(stream_key, dims, cuts, -0.22, 0.18) if cuts else 1.0
    entries = jax.random.normal(stream_key, dims, jnp.float32) * deviation * gain
    return jnp.minimum(jnp.maximum(entries, -limit), limit).astype(held_as)


def setup_inputs(seed: int = 0, part: int = 0) -> dict:
    key_of = jax.random.split(jax.random.key(seed), 12)
    own_keys = jax.random.split(jax.random.fold_in(key_of[11], part), 12)
    return {
        "query_vectors": draw_query_vectors(jax.random.fold_in(jax.random.fold_in(key_of[11], part), 71), part),
        "key_vectors": draw_key_vectors(jax.random.fold_in(jax.random.fold_in(key_of[11], part), 71), part),
        "value_vectors": bell_draw(own_keys[2], (TOKENS, D), 1.0, 6.0, ((0, 8), (1, 2))),
        "residual": bell_draw(own_keys[3], (TOKENS, D), 1.0, 6.0, ((0, 8), (1, 2))),
        "neighbor_ids": draw_neighbor_ids(jax.random.fold_in(jax.random.fold_in(key_of[11], part), 71), part),
        "neighbor_count": draw_neighbor_count(jax.random.fold_in(jax.random.fold_in(key_of[11], part), 71), part),
        "output_weight": bell_draw(key_of[6], (D, D), D ** -0.5, 0.1875, ((0, 2),)),
        "norm_gain": jnp.clip(1.0 + 0.15 * jax.random.normal(key_of[7], (D,), jnp.float32), 0.25, 1.75),
        "up_weight": bell_draw(key_of[8], (D, FF), D ** -0.5, 0.1875, ((1, 4),)),
        "down_weight": bell_draw(key_of[9], (FF, D), FF ** -0.5, 0.09375, ((0, 4),)),
        "cotangent": bell_draw(own_keys[10], (TOKENS, D), 1.0, 6.0, ((0, 8), (1, 2))),
    }


def attend_group(query_group, key_group, value_group, ids_group, count_group):
    group_count = ids_group.shape[0]
    column_ids = jnp.arange(group_count, dtype=jnp.int32)
    slot_ids = jnp.arange(ids_group.shape[1], dtype=jnp.int32)
    listed = (ids_group[:, :, None] == column_ids[None, None, :]) & (slot_ids[None, :, None] < count_group[:, None, None])
    allowed = jnp.any(listed, axis=1)
    token_mask = jnp.repeat(jnp.repeat(allowed, BLK, axis=0), BLK, axis=1)
    query_heads = query_group.astype(jnp.float32).reshape(-1, HEADS, HEAD)
    key_heads = key_group.astype(jnp.float32).reshape(-1, HEADS, HEAD)
    value_heads = value_group.astype(jnp.float32).reshape(-1, HEADS, HEAD)
    scores = jnp.einsum('qhd,khd->hqk', query_heads, key_heads) * HEAD ** (-0.5)
    scores = jnp.where(token_mask[None], scores, -1e+30)
    largest = lax.optimization_barrier(jnp.max(scores, axis=2, keepdims=True))
    weights = jnp.exp(scores - largest)
    probs = (weights / lax.optimization_barrier(jnp.sum(weights, axis=2, keepdims=True))).astype(jnp.bfloat16)
    attended = jnp.einsum('hqk,khd->qhd', probs.astype(jnp.float32), value_heads)
    return attended.reshape(-1, D).astype(jnp.bfloat16)

def reference(query_vectors, key_vectors, value_vectors, residual, neighbor_ids, neighbor_count, output_weight, norm_gain, up_weight, down_weight, cotangent):
    group_total = BLOCKS // GROUP_BLOCKS
    group_tokens = GROUP_BLOCKS * BLK

    def one_group(index):
        start = index * group_tokens
        query_group = lax.dynamic_slice_in_dim(query_vectors, start, group_tokens, 0)
        key_group = lax.dynamic_slice_in_dim(key_vectors, start, group_tokens, 0)
        value_group = lax.dynamic_slice_in_dim(value_vectors, start, group_tokens, 0)
        ids_group = lax.dynamic_slice_in_dim(neighbor_ids, index * GROUP_BLOCKS, GROUP_BLOCKS, 0)
        count_group = lax.dynamic_slice_in_dim(neighbor_count, index * GROUP_BLOCKS, GROUP_BLOCKS, 0)
        return attend_group(query_group, key_group, value_group, ids_group, count_group)
    attended = lax.map(one_group, jnp.arange(group_total, dtype=jnp.int32)).reshape(TOKENS, D)
    stream = residual.astype(jnp.float32) + jnp.dot(attended, output_weight, preferred_element_type=jnp.float32)
    center = lax.optimization_barrier(jnp.mean(stream, axis=1, keepdims=True))
    shifted = stream - center
    spread_sq = lax.optimization_barrier(jnp.mean(shifted * shifted, axis=1, keepdims=True))
    normed = (shifted * lax.rsqrt(spread_sq + 1e-05) * norm_gain.astype(jnp.float32)[None, :]).astype(jnp.bfloat16)
    pre = jnp.dot(normed, up_weight, preferred_element_type=jnp.float32)
    hidden = jax.nn.gelu(pre).astype(jnp.bfloat16)

    def add_panel(total, index):
        hidden_part = lax.dynamic_slice_in_dim(hidden, index * PANEL, PANEL, 1)
        weight_part = lax.dynamic_slice_in_dim(down_weight, index * PANEL, PANEL, 0)
        term = jnp.dot(hidden_part, weight_part, preferred_element_type=jnp.float32).astype(jnp.bfloat16)
        term = lax.optimization_barrier(term)
        return (total + term.astype(jnp.float32), None)
    panel_total = FF // PANEL
    ff_out, _ = lax.scan(add_panel, jnp.zeros((TOKENS, D), jnp.float32), jnp.arange(panel_total, dtype=jnp.int32))
    layer_out = (stream + ff_out).astype(jnp.bfloat16)
    back_hidden = jnp.dot(cotangent, down_weight.T, preferred_element_type=jnp.float32)
    _, gelu_back = jax.vjp(jax.nn.gelu, pre)
    back_pre = gelu_back(back_hidden)[0].astype(jnp.bfloat16)
    up_grad = jnp.dot(normed.T, back_pre, preferred_element_type=jnp.float32)
    down_grad = jnp.dot(hidden.T, cotangent, preferred_element_type=jnp.float32)
    return (layer_out, up_grad, down_grad)
```

```python
import jax
import jax.numpy as jnp
from jax import lax
from jax.sharding import PartitionSpec as P

HEAD = 64
D = 1024
BLK = 128


def spread_rows(part_rows):
    stacked = lax.all_gather(part_rows[None], ("grp", "col"), axis=0, tiled=True)
    grp_count = lax.axis_size("grp")
    col_count = lax.axis_size("col")
    row_count = part_rows.shape[0]
    half_width = part_rows.shape[1]
    arranged = stacked.reshape(grp_count, col_count, row_count, half_width).transpose(0, 2, 1, 3)
    return arranged.reshape(grp_count * row_count, col_count * half_width)


def shards(
    query_vectors,
    key_vectors,
    value_vectors,
    residual,
    neighbor_ids,
    neighbor_count,
    output_weight,
    norm_gain,
    up_weight,
    down_weight,
    cotangent,
):
    key_all, value_all = (
        lax.all_gather(key_vectors, "grp", axis=0, tiled=True),
        lax.all_gather(value_vectors, "grp", axis=0, tiled=True),
    )
    row_count = query_vectors.shape[0]
    local_heads = query_vectors.shape[1] // HEAD
    group_count = key_all.shape[0] // BLK
    column_ids = jnp.arange(group_count, dtype=jnp.int32)
    slot_ids = jnp.arange(neighbor_ids.shape[1], dtype=jnp.int32)
    listed = (neighbor_ids[:, :, None] == column_ids[None, None, :]) & (
        slot_ids[None, :, None] < neighbor_count[:, None, None]
    )
    allowed = jnp.any(listed, axis=1)
    token_mask = jnp.repeat(jnp.repeat(allowed, BLK, axis=0), BLK, axis=1)
    query_heads = query_vectors.reshape(row_count, local_heads, HEAD)
    key_heads = key_all.reshape(-1, local_heads, HEAD)
    value_heads = value_all.reshape(-1, local_heads, HEAD)
    scores = jnp.einsum(
        "qhd,khd->hqk", query_heads, key_heads, preferred_element_type=jnp.float32
    ) * HEAD ** (-0.5)
    scores = jnp.where(token_mask[None], scores, -1e30)
    largest = jnp.max(scores, axis=2, keepdims=True)
    weights = jnp.exp(scores - largest)
    probs = (weights / jnp.sum(weights, axis=2, keepdims=True)).astype(jnp.bfloat16)
    attended = jnp.einsum("hqk,khd->qhd", probs, value_heads, preferred_element_type=jnp.float32)
    attended = attended.astype(jnp.bfloat16).reshape(row_count, -1)
    projected = jnp.dot(attended, output_weight, preferred_element_type=jnp.float32)
    stream = residual.astype(jnp.float32) + lax.psum_scatter(
        projected.astype(jnp.bfloat16), "col", scatter_dimension=1, tiled=True
    ).astype(jnp.float32)
    first_sum, second_sum = lax.psum(
        (jnp.sum(stream, axis=1), jnp.sum(stream * stream, axis=1)), "col"
    )
    center = first_sum[:, None] / D
    shifted = stream - center
    spread_sq = second_sum[:, None] / D - center * center
    normed = (shifted * lax.rsqrt(spread_sq + 1e-05) * norm_gain[None, :]).astype(jnp.bfloat16)
    normed_rows = spread_rows(normed)
    pre = jnp.dot(normed_rows, up_weight, preferred_element_type=jnp.float32)
    hidden = jax.nn.gelu(pre).astype(jnp.bfloat16)
    grp_count = lax.axis_size("grp")
    col_count = lax.axis_size("col")
    partial_out = jnp.dot(hidden, down_weight, preferred_element_type=jnp.float32)
    half_width = partial_out.shape[1] // col_count
    partial_out = partial_out.reshape(grp_count, row_count, col_count, half_width).transpose(
        0, 2, 1, 3
    )
    partial_out = partial_out.reshape(grp_count * col_count * row_count, half_width)
    ff_out = lax.psum_scatter(
        partial_out.astype(jnp.bfloat16), ("grp", "col"), scatter_dimension=0, tiled=True
    ).astype(jnp.float32)
    layer_out = (stream + ff_out).astype(jnp.bfloat16)
    back_rows = spread_rows(cotangent)
    back_hidden = lax.dot_general(
        back_rows, down_weight, (((1,), (1,)), ((), ())), preferred_element_type=jnp.float32
    )
    _, gelu_back = jax.vjp(jax.nn.gelu, pre)
    back_pre = gelu_back(back_hidden)[0].astype(jnp.bfloat16)
    up_local = lax.dot_general(
        normed_rows, back_pre, (((0,), (0,)), ((), ())), preferred_element_type=jnp.float32
    )
    down_local = lax.dot_general(
        hidden, back_rows, (((0,), (0,)), ((), ())), preferred_element_type=jnp.float32
    )
    up_grad, down_grad = (
        lax.psum(up_local.astype(jnp.bfloat16), "patch").astype(jnp.float32),
        lax.psum(down_local.astype(jnp.bfloat16), "patch").astype(jnp.float32),
    )
    return (layer_out, up_grad, down_grad)


def shift(x, axis, k):
    n = lax.axis_size(axis)
    return lax.ppermute(x, axis, [(i, (i + k) % n) for i in range(n)])


def spread(piece):
    chunks = []
    held = piece
    for s in range(lax.axis_size("patch")):
        if s:
            held = shift(held, "patch", 1)
        chunks.append([held] + [shift(held, "grp", k) for k in range(1, lax.axis_size("grp"))])
    return chunks


def join(pieces, dim):
    n = len(pieces)
    me = lax.axis_index("col")
    size = pieces[0].shape[dim]
    shape = list(pieces[0].shape)
    shape[dim] = size * n
    whole = jnp.zeros(shape, pieces[0].dtype)
    for j, piece in enumerate(pieces):
        start = [0] * len(shape)
        start[dim] = (me - j + n) % n * size
        whole = lax.dynamic_update_slice(whole, piece, start)
    return whole


def over_cores(piece, dim):
    return join([piece] + [shift(piece, "col", j) for j in range(1, lax.axis_size("col"))], dim)


def gather_plan(
    query_vectors,
    key_vectors,
    value_vectors,
    residual,
    neighbor_ids,
    neighbor_count,
    output_weight,
    norm_gain,
    up_weight,
    down_weight,
    cotangent,
):
    cores = lax.axis_size("col")
    grps = lax.axis_size("grp")
    me = lax.axis_index("col")
    row_count = query_vectors.shape[0]
    half = query_vectors.shape[1]
    keys = [key_vectors] + [shift(key_vectors, "grp", k) for k in range(1, grps)]
    values = [value_vectors] + [shift(value_vectors, "grp", k) for k in range(1, grps)]
    cot_chunks = spread(cotangent)
    out_weight = over_cores(output_weight, 0)
    res_rows = over_cores(residual, 1)
    gain = over_cores(norm_gain, 0)

    local_heads = half // HEAD
    own = lax.axis_index("grp")
    slot_ids = jnp.arange(neighbor_ids.shape[1], dtype=jnp.int32)
    query_heads = query_vectors.reshape(row_count, local_heads, HEAD)
    scores = []
    for k in range(grps):
        seen = jnp.any((neighbor_ids[0] == (own - k + grps) % grps) & (slot_ids < neighbor_count[0]))
        part = jnp.einsum(
            "qhd,khd->hqk",
            query_heads,
            keys[k].reshape(row_count, local_heads, HEAD),
            preferred_element_type=jnp.float32,
        ) * HEAD ** (-0.5)
        scores.append(jnp.where(seen, part, -1e30))
    scores = jnp.concatenate(scores, axis=2)
    largest = jnp.max(scores, axis=2, keepdims=True)
    weights = jnp.exp(scores - largest)
    probs = (weights / jnp.sum(weights, axis=2, keepdims=True)).astype(jnp.bfloat16)
    value_heads = jnp.concatenate(values, axis=0).reshape(-1, local_heads, HEAD)
    attended = jnp.einsum("hqk,khd->qhd", probs, value_heads, preferred_element_type=jnp.float32)
    attended = over_cores(attended.astype(jnp.bfloat16).reshape(row_count, -1), 1)
    stream = res_rows.astype(jnp.float32) + jnp.dot(
        attended, out_weight, preferred_element_type=jnp.float32
    )
    center = jnp.mean(stream, axis=1, keepdims=True)
    shifted = stream - center
    spread_sq = jnp.mean(shifted * shifted, axis=1, keepdims=True)
    normed = (shifted * lax.rsqrt(spread_sq + 1e-05) * gain[None, :]).astype(jnp.bfloat16)
    own_stream = lax.dynamic_slice(stream, (0, me * half), (row_count, half))

    share = row_count // cores
    norm_chunks = spread(lax.dynamic_slice(normed, (me * share, 0), (share, normed.shape[1])))

    rows, backs, hiddens, back_pres = [], [], [], []
    layer_out = None
    for s, (norm_pieces, cot_pieces) in enumerate(zip(norm_chunks, cot_chunks)):
        normed_rows = jnp.concatenate(
            [normed if s == 0 and k == 0 else over_cores(p, 0) for k, p in enumerate(norm_pieces)], 0
        )
        back_rows = over_cores(jnp.concatenate(cot_pieces, 0), 1)
        pre = jnp.dot(normed_rows, up_weight, preferred_element_type=jnp.float32)
        hidden = jax.nn.gelu(pre).astype(jnp.bfloat16)
        if s == 0:
            partial_out = jnp.dot(hidden, down_weight, preferred_element_type=jnp.float32)
            partial_out = partial_out.astype(jnp.bfloat16)
            layer_out = own_stream
            for k in range(grps):
                for j in range(cores):
                    piece = lax.dynamic_slice(
                        partial_out, (k * row_count, (me - j + cores) % cores * half), (row_count, half)
                    )
                    if k or j:
                        piece = lax.ppermute(
                            piece,
                            ("grp", "col"),
                            [
                                (a * cores + b, (a - k) % grps * cores + (b - j) % cores)
                                for a in range(grps)
                                for b in range(cores)
                            ],
                        )
                    layer_out = layer_out + piece.astype(jnp.float32)
            layer_out = layer_out.astype(jnp.bfloat16)
        back_hidden = lax.dot_general(
            back_rows, down_weight, (((1,), (1,)), ((), ())), preferred_element_type=jnp.float32
        )
        _, gelu_back = jax.vjp(jax.nn.gelu, pre)
        back_pres.append(gelu_back(back_hidden)[0].astype(jnp.bfloat16))
        rows.append(normed_rows)
        backs.append(back_rows)
        hiddens.append(hidden)
    rows, backs, hiddens, back_pres = (
        jnp.concatenate(a, 0) for a in (rows, backs, hiddens, back_pres)
    )
    up_grad = lax.dot_general(
        rows, back_pres, (((0,), (0,)), ((), ())), preferred_element_type=jnp.float32
    )
    down_grad = lax.dot_general(
        hiddens, backs, (((0,), (0,)), ((), ())), preferred_element_type=jnp.float32
    )
    return (layer_out, up_grad, down_grad)


def layer(*args):
    query_vectors, up_weight = args[0], args[8]
    tokens = query_vectors.shape[0] * lax.axis_size("grp") * lax.axis_size("patch")
    if tokens <= 2 * up_weight.shape[1]:
        return gather_plan(*args)
    return shards(*args)


def solution(mesh):
    return jax.shard_map(
        layer,
        mesh=mesh,
        in_specs=(
            P(("parts", "patch", "grp"), "col"),
            P(("parts", "patch", "grp"), "col"),
            P(("parts", "patch", "grp"), "col"),
            P(("parts", "patch", "grp"), "col"),
            P(("parts", "patch", "grp"), None),
            P(("parts", "patch", "grp")),
            P("col", None),
            P("col"),
            P(None, ("grp", "col")),
            P(("grp", "col"), None),
            P(("parts", "patch", "grp"), "col"),
        ),
        out_specs=(
            P(("parts", "patch", "grp"), "col"),
            P("parts", ("grp", "col")),
            P(("parts", "grp", "col"), None),
        ),
        check_vma=False,
    )
```

```python
import jax
import jax.numpy as jnp
from jax import lax
from jax.experimental import pallas as pl
from jax.experimental.pallas import tpu as pltpu
from jax.sharding import PartitionSpec as P

HEAD = 64
D = 1024
BLK = 128


def spread_rows(part_rows):
    stacked = lax.all_gather(part_rows[None], ("grp", "col"), axis=0, tiled=True)
    grp_count = lax.axis_size("grp")
    col_count = lax.axis_size("col")
    row_count = part_rows.shape[0]
    half_width = part_rows.shape[1]
    arranged = stacked.reshape(grp_count, col_count, row_count, half_width).transpose(0, 2, 1, 3)
    return arranged.reshape(grp_count * row_count, col_count * half_width)


def shards(
    query_vectors,
    key_vectors,
    value_vectors,
    residual,
    neighbor_ids,
    neighbor_count,
    output_weight,
    norm_gain,
    up_weight,
    down_weight,
    cotangent,
):
    key_all, value_all = (
        lax.all_gather(key_vectors, "grp", axis=0, tiled=True),
        lax.all_gather(value_vectors, "grp", axis=0, tiled=True),
    )
    row_count = query_vectors.shape[0]
    local_heads = query_vectors.shape[1] // HEAD
    group_count = key_all.shape[0] // BLK
    column_ids = jnp.arange(group_count, dtype=jnp.int32)
    slot_ids = jnp.arange(neighbor_ids.shape[1], dtype=jnp.int32)
    listed = (neighbor_ids[:, :, None] == column_ids[None, None, :]) & (
        slot_ids[None, :, None] < neighbor_count[:, None, None]
    )
    allowed = jnp.any(listed, axis=1)
    token_mask = jnp.repeat(jnp.repeat(allowed, BLK, axis=0), BLK, axis=1)
    query_heads = query_vectors.reshape(row_count, local_heads, HEAD)
    key_heads = key_all.reshape(-1, local_heads, HEAD)
    value_heads = value_all.reshape(-1, local_heads, HEAD)
    scores = jnp.einsum(
        "qhd,khd->hqk", query_heads, key_heads, preferred_element_type=jnp.float32
    ) * HEAD ** (-0.5)
    scores = jnp.where(token_mask[None], scores, -1e30)
    largest = jnp.max(scores, axis=2, keepdims=True)
    weights = jnp.exp(scores - largest)
    probs = (weights / jnp.sum(weights, axis=2, keepdims=True)).astype(jnp.bfloat16)
    attended = jnp.einsum("hqk,khd->qhd", probs, value_heads, preferred_element_type=jnp.float32)
    attended = attended.astype(jnp.bfloat16).reshape(row_count, -1)
    projected = jnp.dot(attended, output_weight, preferred_element_type=jnp.float32)
    stream = residual.astype(jnp.float32) + lax.psum_scatter(
        projected.astype(jnp.bfloat16), "col", scatter_dimension=1, tiled=True
    ).astype(jnp.float32)
    first_sum, second_sum = lax.psum(
        (jnp.sum(stream, axis=1), jnp.sum(stream * stream, axis=1)), "col"
    )
    center = first_sum[:, None] / D
    shifted = stream - center
    spread_sq = second_sum[:, None] / D - center * center
    normed = (shifted * lax.rsqrt(spread_sq + 1e-05) * norm_gain[None, :]).astype(jnp.bfloat16)
    normed_rows = spread_rows(normed)
    pre = jnp.dot(normed_rows, up_weight, preferred_element_type=jnp.float32)
    hidden = jax.nn.gelu(pre).astype(jnp.bfloat16)
    grp_count = lax.axis_size("grp")
    col_count = lax.axis_size("col")
    partial_out = jnp.dot(hidden, down_weight, preferred_element_type=jnp.float32)
    half_width = partial_out.shape[1] // col_count
    partial_out = partial_out.reshape(grp_count, row_count, col_count, half_width).transpose(
        0, 2, 1, 3
    )
    partial_out = partial_out.reshape(grp_count * col_count * row_count, half_width)
    ff_out = lax.psum_scatter(
        partial_out.astype(jnp.bfloat16), ("grp", "col"), scatter_dimension=0, tiled=True
    ).astype(jnp.float32)
    layer_out = (stream + ff_out).astype(jnp.bfloat16)
    back_rows = spread_rows(cotangent)
    back_hidden = lax.dot_general(
        back_rows, down_weight, (((1,), (1,)), ((), ())), preferred_element_type=jnp.float32
    )
    _, gelu_back = jax.vjp(jax.nn.gelu, pre)
    back_pre = gelu_back(back_hidden)[0].astype(jnp.bfloat16)
    up_local = lax.dot_general(
        normed_rows, back_pre, (((0,), (0,)), ((), ())), preferred_element_type=jnp.float32
    )
    down_local = lax.dot_general(
        hidden, back_rows, (((0,), (0,)), ((), ())), preferred_element_type=jnp.float32
    )
    up_grad, down_grad = (
        lax.psum(up_local.astype(jnp.bfloat16), "patch").astype(jnp.float32),
        lax.psum(down_local.astype(jnp.bfloat16), "patch").astype(jnp.float32),
    )
    return (layer_out, up_grad, down_grad)


def shift(x, axis, k):
    n = lax.axis_size(axis)
    return lax.ppermute(x, axis, [(i, (i + k) % n) for i in range(n)])


def after(x, *others):
    return lax.optimization_barrier((x,) + others)[0]


def others(x, axis):
    return [shift(x, axis, k) for k in range(1, lax.axis_size(axis))]


def attend(seen_ref, query_ref, *refs):
    grps = seen_ref.shape[0]
    keys, values, out_ref = refs[:grps], refs[grps : 2 * grps], refs[2 * grps]
    lane = lax.broadcasted_iota(jnp.int32, (BLK, 2 * HEAD), 1)
    nt = (((1,), (1,)), ((), ()))
    for pair in range(query_ref.shape[1] // (2 * HEAD)):
        cols = pl.ds(pair * 2 * HEAD, 2 * HEAD)
        query = query_ref[:, cols]
        found = []
        for head in range(2):
            one = jnp.where((lane < HEAD) == (head == 0), query, jnp.zeros_like(query))
            scores = []
            for k in range(grps):
                part = lax.dot_general(
                    one, keys[k][:, cols], nt, preferred_element_type=jnp.float32
                ) * HEAD ** (-0.5)
                scores.append(jnp.where(seen_ref[k] > 0, part, -1e30))
            largest = scores[0]
            for part in scores[1:]:
                largest = jnp.maximum(largest, part)
            largest = jnp.max(largest, axis=1, keepdims=True)
            weights = [jnp.exp(part - largest) for part in scores]
            total = weights[0]
            for part in weights[1:]:
                total = total + part
            total = jnp.sum(total, axis=1, keepdims=True)
            result = 0.0
            for k in range(grps):
                probs = (weights[k] / total).astype(jnp.bfloat16)
                result = result + jnp.dot(
                    probs, values[k][:, cols], preferred_element_type=jnp.float32
                )
            found.append(result)
        out_ref[:, cols] = jnp.where(lane < HEAD, found[0], found[1]).astype(jnp.bfloat16)


def project(me_ref, gain_ref, *refs):
    cores = (len(refs) - 3) // 3
    attended, weights, residuals = refs[:cores], refs[cores : 2 * cores], refs[2 * cores : 3 * cores]
    stream_ref, normed_ref, full = refs[3 * cores :]
    half = stream_ref.shape[1]
    me = me_ref[0]
    total = jnp.dot(attended[0][...], weights[0][...], preferred_element_type=jnp.float32)
    for j in range(1, cores):
        total = total + jnp.dot(
            attended[j][...], weights[j][...], preferred_element_type=jnp.float32
        )
    full[...] = total
    parts = []
    for j in range(cores):
        cols = pl.ds(pl.multiple_of(lax.rem(me - j + cores, cores) * half, half), half)
        parts.append(full[:, cols] + residuals[j][...].astype(jnp.float32))
    width = half * cores
    center = sum(jnp.sum(part, axis=1, keepdims=True) for part in parts) / width
    spread_sq = sum(
        jnp.sum((part - center) * (part - center), axis=1, keepdims=True) for part in parts
    ) / width
    stream_ref[...] = parts[0]
    normed_ref[...] = (
        (parts[0] - center) * lax.rsqrt(spread_sq + 1e-05) * gain_ref[...]
    ).astype(jnp.bfloat16)


def call(kernel, out_shape, smem, args, flops, scratch=()):
    moved = sum(a.size * a.dtype.itemsize for a in args) + sum(
        o.size * o.dtype.itemsize for o in jax.tree.leaves(out_shape)
    )
    return pl.pallas_call(
        kernel,
        out_shape=out_shape,
        in_specs=[pl.BlockSpec(memory_space=pltpu.SMEM)] * smem
        + [pl.BlockSpec(memory_space=pltpu.VMEM)] * (len(args) - smem),
        scratch_shapes=scratch,
        cost_estimate=pl.CostEstimate(flops=flops, bytes_accessed=moved, transcendentals=0),
        compiler_params=pltpu.CompilerParams(vmem_limit_bytes=24 * 2**20),
    )(*args)


def join(pieces, dim):
    n = len(pieces)
    me = lax.axis_index("col")
    size = pieces[0].shape[dim]
    shape = list(pieces[0].shape)
    shape[dim] = size * n
    whole = jnp.zeros(shape, pieces[0].dtype)
    for j, piece in enumerate(pieces):
        start = [0] * len(shape)
        start[dim] = (me - j + n) % n * size
        whole = lax.dynamic_update_slice(whole, piece, start)
    return whole


def over_cores(piece, dim):
    return join([piece] + others(piece, "col"), dim)


def gather_plan(
    query_vectors,
    key_vectors,
    value_vectors,
    residual,
    neighbor_ids,
    neighbor_count,
    output_weight,
    norm_gain,
    up_weight,
    down_weight,
    cotangent,
):
    cores = lax.axis_size("col")
    grps = lax.axis_size("grp")
    patches = lax.axis_size("patch")
    me = lax.axis_index("col")
    rows, half = query_vectors.shape
    width = half * cores

    keys = [key_vectors] + others(key_vectors, "grp")
    values = [value_vectors] + others(value_vectors, "grp")
    cots = [cotangent, shift(cotangent, "patch", 1)]
    weights = [output_weight] + others(output_weight, "col")
    residuals = [residual] + others(residual, "col")

    own = lax.axis_index("grp")
    source = (own - jnp.arange(grps, dtype=jnp.int32) + grps) % grps
    slots = jnp.arange(neighbor_ids.shape[1], dtype=jnp.int32) < neighbor_count[0]
    seen = jnp.any((neighbor_ids[0][None] == source[:, None]) & slots[None], axis=1)
    attended = call(
        attend,
        jax.ShapeDtypeStruct((rows, half), jnp.bfloat16),
        1,
        [seen.astype(jnp.int32), query_vectors] + keys + values,
        4 * rows * rows * grps * width,
    )
    attended_all = [attended] + others(attended, "col")
    cots.append(shift(after(cots[1], attended), "patch", 1))
    stream, normed = call(
        project,
        (
            jax.ShapeDtypeStruct((rows, half), jnp.float32),
            jax.ShapeDtypeStruct((rows, half), jnp.bfloat16),
        ),
        1,
        [me[None], norm_gain[None]] + attended_all + weights + residuals,
        2 * rows * width * width,
        [pltpu.VMEM((rows, width), jnp.float32)],
    )
    cots[0], cots[1], cots[2] = (after(c, normed) for c in cots)
    for s in range(3, patches):
        cots.append(shift(cots[s - 1], "patch", 1))

    norms = [normed]
    for s in range(1, patches):
        norms.append(shift(norms[-1], "patch", 1))

    saved = []
    layer_out = None
    for s in range(patches):
        norm_pieces = [norms[s]] + others(norms[s], "grp")
        cot_pieces = [cots[s]] + others(cots[s], "grp")
        normed_rows = jnp.concatenate([over_cores(p, 1) for p in norm_pieces], 0)
        back_rows = over_cores(jnp.concatenate(cot_pieces, 0), 1)
        pre = jnp.dot(normed_rows, up_weight, preferred_element_type=jnp.float32)
        hidden = jax.nn.gelu(pre).astype(jnp.bfloat16)
        if s == 0:
            partial_out = jnp.dot(hidden, down_weight, preferred_element_type=jnp.float32)
            partial_out = partial_out.astype(jnp.bfloat16)
            layer_out = stream
            for k in range(grps):
                for j in range(cores):
                    piece = lax.dynamic_slice(
                        partial_out, (k * rows, (me - j + cores) % cores * half), (rows, half)
                    )
                    if k or j:
                        piece = lax.ppermute(
                            piece,
                            ("grp", "col"),
                            [
                                (a * cores + b, (a - k) % grps * cores + (b - j) % cores)
                                for a in range(grps)
                                for b in range(cores)
                            ],
                        )
                    layer_out = layer_out + piece.astype(jnp.float32)
            layer_out = layer_out.astype(jnp.bfloat16)
        back_hidden = lax.dot_general(
            back_rows, down_weight, (((1,), (1,)), ((), ())), preferred_element_type=jnp.float32
        )
        _, gelu_back = jax.vjp(jax.nn.gelu, pre)
        back_pre = gelu_back(back_hidden)[0].astype(jnp.bfloat16)
        saved.append((normed_rows, back_rows, hidden, back_pre))
    all_normed, all_back, all_hidden, all_pre = (jnp.concatenate(a, 0) for a in zip(*saved))
    up_grad = lax.dot_general(
        all_normed, all_pre, (((0,), (0,)), ((), ())), preferred_element_type=jnp.float32
    )
    down_grad = lax.dot_general(
        all_hidden, all_back, (((0,), (0,)), ((), ())), preferred_element_type=jnp.float32
    )
    return (layer_out, up_grad, down_grad)


def layer(*args):
    query_vectors, up_weight = args[0], args[8]
    tokens = query_vectors.shape[0] * lax.axis_size("grp") * lax.axis_size("patch")
    if tokens <= 2 * up_weight.shape[1]:
        return gather_plan(*args)
    return shards(*args)


def solution(mesh):
    return jax.shard_map(
        layer,
        mesh=mesh,
        in_specs=(
            P(("parts", "patch", "grp"), "col"),
            P(("parts", "patch", "grp"), "col"),
            P(("parts", "patch", "grp"), "col"),
            P(("parts", "patch", "grp"), "col"),
            P(("parts", "patch", "grp"), None),
            P(("parts", "patch", "grp")),
            P("col", None),
            P("col"),
            P(None, ("grp", "col")),
            P(("grp", "col"), None),
            P(("parts", "patch", "grp"), "col"),
        ),
        out_specs=(
            P(("parts", "patch", "grp"), "col"),
            P("parts", ("grp", "col")),
            P(("parts", "grp", "col"), None),
        ),
        check_vma=False,
    )
```

```python
import functools

import jax
import jax.numpy as jnp
from jax import lax
from jax.experimental import pallas as pl
from jax.experimental.pallas import tpu as pltpu
from jax.sharding import PartitionSpec as P

HEAD = 64
D = 1024
BLK = 128


def spread_rows(part_rows):
    stacked = lax.all_gather(part_rows[None], ("grp", "col"), axis=0, tiled=True)
    grp_count = lax.axis_size("grp")
    col_count = lax.axis_size("col")
    row_count = part_rows.shape[0]
    half_width = part_rows.shape[1]
    arranged = stacked.reshape(grp_count, col_count, row_count, half_width).transpose(0, 2, 1, 3)
    return arranged.reshape(grp_count * row_count, col_count * half_width)


def shards(
    query_vectors,
    key_vectors,
    value_vectors,
    residual,
    neighbor_ids,
    neighbor_count,
    output_weight,
    norm_gain,
    up_weight,
    down_weight,
    cotangent,
):
    key_all, value_all = (
        lax.all_gather(key_vectors, "grp", axis=0, tiled=True),
        lax.all_gather(value_vectors, "grp", axis=0, tiled=True),
    )
    row_count = query_vectors.shape[0]
    local_heads = query_vectors.shape[1] // HEAD
    group_count = key_all.shape[0] // BLK
    column_ids = jnp.arange(group_count, dtype=jnp.int32)
    slot_ids = jnp.arange(neighbor_ids.shape[1], dtype=jnp.int32)
    listed = (neighbor_ids[:, :, None] == column_ids[None, None, :]) & (
        slot_ids[None, :, None] < neighbor_count[:, None, None]
    )
    allowed = jnp.any(listed, axis=1)
    token_mask = jnp.repeat(jnp.repeat(allowed, BLK, axis=0), BLK, axis=1)
    query_heads = query_vectors.reshape(row_count, local_heads, HEAD)
    key_heads = key_all.reshape(-1, local_heads, HEAD)
    value_heads = value_all.reshape(-1, local_heads, HEAD)
    scores = jnp.einsum(
        "qhd,khd->hqk", query_heads, key_heads, preferred_element_type=jnp.float32
    ) * HEAD ** (-0.5)
    scores = jnp.where(token_mask[None], scores, -1e30)
    largest = jnp.max(scores, axis=2, keepdims=True)
    weights = jnp.exp(scores - largest)
    probs = (weights / jnp.sum(weights, axis=2, keepdims=True)).astype(jnp.bfloat16)
    attended = jnp.einsum("hqk,khd->qhd", probs, value_heads, preferred_element_type=jnp.float32)
    attended = attended.astype(jnp.bfloat16).reshape(row_count, -1)
    projected = jnp.dot(attended, output_weight, preferred_element_type=jnp.float32)
    stream = residual.astype(jnp.float32) + lax.psum_scatter(
        projected.astype(jnp.bfloat16), "col", scatter_dimension=1, tiled=True
    ).astype(jnp.float32)
    first_sum, second_sum = lax.psum(
        (jnp.sum(stream, axis=1), jnp.sum(stream * stream, axis=1)), "col"
    )
    center = first_sum[:, None] / D
    shifted = stream - center
    spread_sq = second_sum[:, None] / D - center * center
    normed = (shifted * lax.rsqrt(spread_sq + 1e-05) * norm_gain[None, :]).astype(jnp.bfloat16)
    normed_rows = spread_rows(normed)
    pre = jnp.dot(normed_rows, up_weight, preferred_element_type=jnp.float32)
    hidden = jax.nn.gelu(pre).astype(jnp.bfloat16)
    grp_count = lax.axis_size("grp")
    col_count = lax.axis_size("col")
    partial_out = jnp.dot(hidden, down_weight, preferred_element_type=jnp.float32)
    half_width = partial_out.shape[1] // col_count
    partial_out = partial_out.reshape(grp_count, row_count, col_count, half_width).transpose(
        0, 2, 1, 3
    )
    partial_out = partial_out.reshape(grp_count * col_count * row_count, half_width)
    ff_out = lax.psum_scatter(
        partial_out.astype(jnp.bfloat16), ("grp", "col"), scatter_dimension=0, tiled=True
    ).astype(jnp.float32)
    layer_out = (stream + ff_out).astype(jnp.bfloat16)
    back_rows = spread_rows(cotangent)
    back_hidden = lax.dot_general(
        back_rows, down_weight, (((1,), (1,)), ((), ())), preferred_element_type=jnp.float32
    )
    _, gelu_back = jax.vjp(jax.nn.gelu, pre)
    back_pre = gelu_back(back_hidden)[0].astype(jnp.bfloat16)
    up_local = lax.dot_general(
        normed_rows, back_pre, (((0,), (0,)), ((), ())), preferred_element_type=jnp.float32
    )
    down_local = lax.dot_general(
        hidden, back_rows, (((0,), (0,)), ((), ())), preferred_element_type=jnp.float32
    )
    up_grad, down_grad = (
        lax.psum(up_local.astype(jnp.bfloat16), "patch").astype(jnp.float32),
        lax.psum(down_local.astype(jnp.bfloat16), "patch").astype(jnp.float32),
    )
    return (layer_out, up_grad, down_grad)


def shift(x, axis, k):
    n = lax.axis_size(axis)
    return lax.ppermute(x, axis, [(i, (i + k) % n) for i in range(n)])


def after(x, *others):
    return lax.optimization_barrier((x,) + others)[0]


def others(x, axis):
    n = lax.axis_size(axis)
    if n & (n - 1):
        return [shift(x, axis, k) for k in range(1, n)]
    return [lax.ppermute(x, axis, [(i, i ^ k) for i in range(n)]) for k in range(1, n)]


def member(axis, k):
    n = lax.axis_size(axis)
    me = lax.axis_index(axis)
    return (me - k + n) % n if n & (n - 1) else me ^ k


def one_head(query, lane, head):
    return jnp.where((lane < HEAD) == (head == 0), query, jnp.zeros_like(query))


def pair_scores(query, key):
    return lax.dot_general(
        query, key, (((1,), (1,)), ((), ())), preferred_element_type=jnp.float32
    ) * HEAD ** (-0.5)


def stage(count, *refs):
    sources, targets, score_ref, sems = refs[:count], refs[count : 2 * count], refs[-2], refs[-1]
    copies = [
        pltpu.make_async_copy(source, target, sems.at[i])
        for i, (source, target) in enumerate(zip(sources, targets))
    ]
    for copy in copies:
        copy.start()
    copies[0].wait()
    copies[1].wait()
    query_ref, key_ref = targets[:2]
    rows = query_ref.shape[0]
    lane = lax.broadcasted_iota(jnp.int32, (rows, 2 * HEAD), 1)
    for pair in range(query_ref.shape[1] // (2 * HEAD)):
        cols = pl.ds(pair * 2 * HEAD, 2 * HEAD)
        query, key = query_ref[:, cols], key_ref[:, cols]
        for head in range(2):
            score_ref[2 * pair + head] = pair_scores(one_head(query, lane, head), key)
    for copy in copies[2:]:
        copy.wait()


def attend(seen_ref, score_ref, query_ref, *refs):
    grps = seen_ref.shape[0]
    keys, values, out_ref = refs[: grps - 1], refs[grps - 1 : 2 * grps - 1], refs[2 * grps - 1]
    rows = query_ref.shape[0]
    lane = lax.broadcasted_iota(jnp.int32, (rows, 2 * HEAD), 1)
    for pair in range(query_ref.shape[1] // (2 * HEAD)):
        cols = pl.ds(pair * 2 * HEAD, 2 * HEAD)
        query = query_ref[:, cols]
        found = []
        for head in range(2):
            one = one_head(query, lane, head)
            scores = [score_ref[2 * pair + head]] + [
                pair_scores(one, keys[k][:, cols]) for k in range(grps - 1)
            ]
            scores = [
                jnp.where(seen_ref[k] > 0, part, -1e30) for k, part in enumerate(scores)
            ]
            largest = scores[0]
            for part in scores[1:]:
                largest = jnp.maximum(largest, part)
            largest = jnp.max(largest, axis=1, keepdims=True)
            weights = [jnp.exp(part - largest) for part in scores]
            total = weights[0]
            for part in weights[1:]:
                total = total + part
            total = jnp.sum(total, axis=1, keepdims=True)
            result = 0.0
            for k in range(grps):
                probs = (weights[k] / total).astype(jnp.bfloat16)
                result = result + jnp.dot(
                    probs, values[k][:, cols], preferred_element_type=jnp.float32
                )
            found.append(result)
        out_ref[:, cols] = jnp.where(lane < HEAD, found[0], found[1]).astype(jnp.bfloat16)


def project(place_ref, gain_ref, *refs):
    cores = (len(refs) - 3) // 3
    attended, weights, residuals = refs[:cores], refs[cores : 2 * cores], refs[2 * cores : 3 * cores]
    stream_ref, normed_ref, full = refs[3 * cores :]
    half = stream_ref.shape[1]
    total = jnp.dot(attended[0][...], weights[0][...], preferred_element_type=jnp.float32)
    for j in range(1, cores):
        total = total + jnp.dot(
            attended[j][...], weights[j][...], preferred_element_type=jnp.float32
        )
    full[...] = total
    parts = []
    for j in range(cores):
        cols = pl.ds(pl.multiple_of(place_ref[j] * half, half), half)
        parts.append(full[:, cols] + residuals[j][...].astype(jnp.float32))
    width = half * cores
    center = sum(jnp.sum(part, axis=1, keepdims=True) for part in parts) / width
    spread_sq = sum(
        jnp.sum((part - center) * (part - center), axis=1, keepdims=True) for part in parts
    ) / width
    stream_ref[...] = parts[0]
    normed_ref[...] = (
        (parts[0] - center) * lax.rsqrt(spread_sq + 1e-05) * gain_ref[...]
    ).astype(jnp.bfloat16)


def call(kernel, out_shape, smem, args, flops, scratch=()):
    moved = sum(a.size * a.dtype.itemsize for a in args) + sum(
        o.size * o.dtype.itemsize for o in jax.tree.leaves(out_shape)
    )
    return pl.pallas_call(
        kernel,
        out_shape=out_shape,
        in_specs=[pl.BlockSpec(memory_space=pltpu.SMEM)] * smem
        + [pl.BlockSpec(memory_space=pltpu.VMEM)] * (len(args) - smem),
        scratch_shapes=scratch,
        cost_estimate=pl.CostEstimate(flops=flops, bytes_accessed=moved, transcendentals=0),
        compiler_params=pltpu.CompilerParams(vmem_limit_bytes=24 * 2**20),
    )(*args)


def join(pieces, dim):
    n = len(pieces)
    size = pieces[0].shape[dim]
    shape = list(pieces[0].shape)
    shape[dim] = size * n
    whole = jnp.zeros(shape, pieces[0].dtype)
    for j, piece in enumerate(pieces):
        start = [0] * len(shape)
        start[dim] = member("col", j) * size
        whole = lax.dynamic_update_slice(whole, piece, start)
    return whole


def over_cores(piece, dim):
    return join([piece] + others(piece, "col"), dim)


def send_back(piece, k, j):
    if not (k or j):
        return piece
    grps, cores = lax.axis_size("grp"), lax.axis_size("col")
    pairs = []
    for a in range(grps):
        for b in range(cores):
            to_grp = (a - k) % grps if grps & (grps - 1) else a ^ k
            to_core = (b - j) % cores if cores & (cores - 1) else b ^ j
            pairs.append((a * cores + b, to_grp * cores + to_core))
    return lax.ppermute(piece, ("grp", "col"), pairs)


def gather_plan(
    query_vectors,
    key_vectors,
    value_vectors,
    residual,
    neighbor_ids,
    neighbor_count,
    output_weight,
    norm_gain,
    up_weight,
    down_weight,
    cotangent,
):
    cores = lax.axis_size("col")
    grps = lax.axis_size("grp")
    patches = lax.axis_size("patch")
    rows, half = query_vectors.shape
    width = half * cores

    key_others = others(key_vectors, "grp")
    value_others = others(value_vectors, "grp")
    cot_others = others(cotangent, "grp")
    weight_others = others(output_weight, "col")
    residual_others = others(residual, "col")

    source = jnp.stack([member("grp", k) for k in range(grps)])
    slots = jnp.arange(neighbor_ids.shape[1], dtype=jnp.int32) < neighbor_count[0]
    seen = jnp.any((neighbor_ids[0][None] == source[:, None]) & slots[None], axis=1)
    held = [query_vectors, key_vectors, value_vectors, output_weight, residual, norm_gain[None], cotangent]
    heads = half // HEAD
    *held, scores = pl.pallas_call(
        functools.partial(stage, len(held)),
        out_shape=[jax.ShapeDtypeStruct(a.shape, a.dtype) for a in held]
        + [jax.ShapeDtypeStruct((heads, rows, rows), jnp.float32)],
        in_specs=[pl.BlockSpec(memory_space=pl.ANY)] * len(held),
        out_specs=[pl.BlockSpec(memory_space=pltpu.VMEM)] * (len(held) + 1),
        scratch_shapes=[pltpu.SemaphoreType.DMA((len(held),))],
        cost_estimate=pl.CostEstimate(
            flops=2 * rows * rows * width, bytes_accessed=4 * 2**20, transcendentals=0
        ),
        compiler_params=pltpu.CompilerParams(vmem_limit_bytes=24 * 2**20),
    )(*held)
    query, _, value, weight, residual, gain, cot = held
    attended = call(
        attend,
        jax.ShapeDtypeStruct((rows, half), jnp.bfloat16),
        1,
        [seen.astype(jnp.int32), scores, query] + key_others + [value] + value_others,
        4 * rows * rows * grps * width,
    )
    attended_others = others(attended, "col")
    cots = [jnp.concatenate([cot] + [after(c, attended) for c in cot_others], 0)]
    cots += others(cots[0], "patch")
    stream, normed = call(
        project,
        (
            jax.ShapeDtypeStruct((rows, half), jnp.float32),
            jax.ShapeDtypeStruct((rows, half), jnp.bfloat16),
        ),
        1,
        [jnp.stack([member("col", j) for j in range(cores)]), gain, attended]
        + attended_others
        + [weight]
        + weight_others
        + [residual]
        + residual_others,
        2 * rows * width * width,
        [pltpu.VMEM((rows, width), jnp.float32)],
    )
    norms = [jnp.concatenate([normed] + others(normed, "grp"), 0)]
    norms += others(norms[0], "patch")

    saved = []
    layer_out = None
    for s in range(patches):
        normed_rows = over_cores(norms[s], 1)
        back_rows = over_cores(cots[s], 1)
        pre = jnp.dot(normed_rows, up_weight, preferred_element_type=jnp.float32)
        hidden = jax.nn.gelu(pre).astype(jnp.bfloat16)
        if s == 0:
            partial_out = jnp.dot(hidden, down_weight, preferred_element_type=jnp.float32)
            partial_out = partial_out.astype(jnp.bfloat16)
            layer_out = stream
            for k in range(grps):
                for j in range(cores):
                    piece = lax.dynamic_slice(
                        partial_out, (k * rows, member("col", j) * half), (rows, half)
                    )
                    layer_out = layer_out + send_back(piece, k, j).astype(jnp.float32)
            layer_out = layer_out.astype(jnp.bfloat16)
        back_hidden = lax.dot_general(
            back_rows, down_weight, (((1,), (1,)), ((), ())), preferred_element_type=jnp.float32
        )
        _, gelu_back = jax.vjp(jax.nn.gelu, pre)
        back_pre = gelu_back(back_hidden)[0].astype(jnp.bfloat16)
        saved.append((normed_rows, back_rows, hidden, back_pre))
    all_normed, all_back, all_hidden, all_pre = (jnp.concatenate(a, 0) for a in zip(*saved))
    up_grad = lax.dot_general(
        all_normed, all_pre, (((0,), (0,)), ((), ())), preferred_element_type=jnp.float32
    )
    down_grad = lax.dot_general(
        all_hidden, all_back, (((0,), (0,)), ((), ())), preferred_element_type=jnp.float32
    )
    return (layer_out, up_grad, down_grad)


def layer(*args):
    query_vectors, up_weight = args[0], args[8]
    tokens = query_vectors.shape[0] * lax.axis_size("grp") * lax.axis_size("patch")
    if tokens <= 2 * up_weight.shape[1]:
        return gather_plan(*args)
    return shards(*args)


def solution(mesh):
    return jax.shard_map(
        layer,
        mesh=mesh,
        in_specs=(
            P(("parts", "patch", "grp"), "col"),
            P(("parts", "patch", "grp"), "col"),
            P(("parts", "patch", "grp"), "col"),
            P(("parts", "patch", "grp"), "col"),
            P(("parts", "patch", "grp"), None),
            P(("parts", "patch", "grp")),
            P("col", None),
            P("col"),
            P(None, ("grp", "col")),
            P(("grp", "col"), None),
            P(("parts", "patch", "grp"), "col"),
        ),
        out_specs=(
            P(("parts", "patch", "grp"), "col"),
            P("parts", ("grp", "col")),
            P(("parts", "grp", "col"), None),
        ),
        check_vma=False,
    )
```

```python
import functools

import jax
import jax.numpy as jnp
from jax import lax
from jax.experimental import pallas as pl
from jax.experimental.pallas import tpu as pltpu
from jax.sharding import PartitionSpec as P

HEAD = 64
D = 1024
BLK = 128


def spread_rows(part_rows):
    stacked = lax.all_gather(part_rows[None], ("grp", "col"), axis=0, tiled=True)
    grp_count = lax.axis_size("grp")
    col_count = lax.axis_size("col")
    row_count = part_rows.shape[0]
    half_width = part_rows.shape[1]
    arranged = stacked.reshape(grp_count, col_count, row_count, half_width).transpose(0, 2, 1, 3)
    return arranged.reshape(grp_count * row_count, col_count * half_width)


def shards(
    query_vectors,
    key_vectors,
    value_vectors,
    residual,
    neighbor_ids,
    neighbor_count,
    output_weight,
    norm_gain,
    up_weight,
    down_weight,
    cotangent,
):
    key_all, value_all = (
        lax.all_gather(key_vectors, "grp", axis=0, tiled=True),
        lax.all_gather(value_vectors, "grp", axis=0, tiled=True),
    )
    row_count = query_vectors.shape[0]
    local_heads = query_vectors.shape[1] // HEAD
    group_count = key_all.shape[0] // BLK
    column_ids = jnp.arange(group_count, dtype=jnp.int32)
    slot_ids = jnp.arange(neighbor_ids.shape[1], dtype=jnp.int32)
    listed = (neighbor_ids[:, :, None] == column_ids[None, None, :]) & (
        slot_ids[None, :, None] < neighbor_count[:, None, None]
    )
    allowed = jnp.any(listed, axis=1)
    token_mask = jnp.repeat(jnp.repeat(allowed, BLK, axis=0), BLK, axis=1)
    query_heads = query_vectors.reshape(row_count, local_heads, HEAD)
    key_heads = key_all.reshape(-1, local_heads, HEAD)
    value_heads = value_all.reshape(-1, local_heads, HEAD)
    scores = jnp.einsum(
        "qhd,khd->hqk", query_heads, key_heads, preferred_element_type=jnp.float32
    ) * HEAD ** (-0.5)
    scores = jnp.where(token_mask[None], scores, -1e30)
    largest = jnp.max(scores, axis=2, keepdims=True)
    weights = jnp.exp(scores - largest)
    probs = (weights / jnp.sum(weights, axis=2, keepdims=True)).astype(jnp.bfloat16)
    attended = jnp.einsum("hqk,khd->qhd", probs, value_heads, preferred_element_type=jnp.float32)
    attended = attended.astype(jnp.bfloat16).reshape(row_count, -1)
    projected = jnp.dot(attended, output_weight, preferred_element_type=jnp.float32)
    stream = residual.astype(jnp.float32) + lax.psum_scatter(
        projected.astype(jnp.bfloat16), "col", scatter_dimension=1, tiled=True
    ).astype(jnp.float32)
    first_sum, second_sum = lax.psum(
        (jnp.sum(stream, axis=1), jnp.sum(stream * stream, axis=1)), "col"
    )
    center = first_sum[:, None] / D
    shifted = stream - center
    spread_sq = second_sum[:, None] / D - center * center
    normed = (shifted * lax.rsqrt(spread_sq + 1e-05) * norm_gain[None, :]).astype(jnp.bfloat16)
    normed_rows = spread_rows(normed)
    pre = jnp.dot(normed_rows, up_weight, preferred_element_type=jnp.float32)
    hidden = jax.nn.gelu(pre).astype(jnp.bfloat16)
    grp_count = lax.axis_size("grp")
    col_count = lax.axis_size("col")
    partial_out = jnp.dot(hidden, down_weight, preferred_element_type=jnp.float32)
    half_width = partial_out.shape[1] // col_count
    partial_out = partial_out.reshape(grp_count, row_count, col_count, half_width).transpose(
        0, 2, 1, 3
    )
    partial_out = partial_out.reshape(grp_count * col_count * row_count, half_width)
    ff_out = lax.psum_scatter(
        partial_out.astype(jnp.bfloat16), ("grp", "col"), scatter_dimension=0, tiled=True
    ).astype(jnp.float32)
    layer_out = (stream + ff_out).astype(jnp.bfloat16)
    back_rows = spread_rows(cotangent)
    back_hidden = lax.dot_general(
        back_rows, down_weight, (((1,), (1,)), ((), ())), preferred_element_type=jnp.float32
    )
    _, gelu_back = jax.vjp(jax.nn.gelu, pre)
    back_pre = gelu_back(back_hidden)[0].astype(jnp.bfloat16)
    up_local = lax.dot_general(
        normed_rows, back_pre, (((0,), (0,)), ((), ())), preferred_element_type=jnp.float32
    )
    down_local = lax.dot_general(
        hidden, back_rows, (((0,), (0,)), ((), ())), preferred_element_type=jnp.float32
    )
    up_grad, down_grad = (
        lax.psum(up_local.astype(jnp.bfloat16), "patch").astype(jnp.float32),
        lax.psum(down_local.astype(jnp.bfloat16), "patch").astype(jnp.float32),
    )
    return (layer_out, up_grad, down_grad)

GAIN_ROWS = 16
STAGE_LIMIT = 56 * 2**20


def shift(x, axis, k):
    n = lax.axis_size(axis)
    return lax.ppermute(x, axis, [(i, (i + k) % n) for i in range(n)])


def after(x, *others):
    return lax.optimization_barrier((x,) + others)[0]


def others(x, axis):
    n = lax.axis_size(axis)
    if n & (n - 1):
        return [shift(x, axis, k) for k in range(1, n)]
    return [lax.ppermute(x, axis, [(i, i ^ k) for i in range(n)]) for k in range(1, n)]


def member(axis, k):
    n = lax.axis_size(axis)
    me = lax.axis_index(axis)
    return (me - k + n) % n if n & (n - 1) else me ^ k


def one_head(query, lane, head):
    return jnp.where((lane < HEAD) == (head == 0), query, jnp.zeros_like(query))


def pair_scores(query, key):
    return lax.dot_general(
        query, key, (((1,), (1,)), ((), ())), preferred_element_type=jnp.float32
    ) * HEAD ** (-0.5)


def stage(place_ref, gain_ref, query_src, key_src, value_src, weight_src, residual_src, *refs):
    cores = place_ref.shape[0]
    cots = refs[:cores]
    query_ref, key_ref, value_ref, weight_ref, packed_ref, cot_ref, score_ref, sems = refs[cores:]
    rows, half = query_ref.shape
    pairs = [
        (query_src, query_ref),
        (key_src, key_ref),
        (value_src, value_ref),
        (weight_src, weight_ref),
        (residual_src, packed_ref.at[pl.ds(0, rows)]),
    ]
    for j, source in enumerate(cots):
        cols = pl.ds(pl.multiple_of(place_ref[j] * half, half), half)
        pairs.append((source, cot_ref.at[:, cols]))
    copies = [
        pltpu.make_async_copy(source, target, sems.at[i]) for i, (source, target) in enumerate(pairs)
    ]
    for copy in copies:
        copy.start()
    gain = gain_ref[...]
    high = gain.astype(jnp.bfloat16)
    rest = gain - high.astype(jnp.float32)
    middle = rest.astype(jnp.bfloat16)
    low = rest - middle.astype(jnp.float32)
    row = lax.broadcasted_iota(jnp.int32, (GAIN_ROWS, half), 0)
    parts = jnp.where(
        row == 0,
        high.astype(jnp.float32),
        jnp.where(row == 1, middle.astype(jnp.float32), jnp.where(row == 2, low, 0.0)),
    )
    packed_ref[pl.ds(rows, GAIN_ROWS), :] = parts.astype(jnp.bfloat16)
    copies[0].wait()
    copies[1].wait()
    lane = lax.broadcasted_iota(jnp.int32, (rows, 2 * HEAD), 1)
    for pair in range(half // (2 * HEAD)):
        cols = pl.ds(pair * 2 * HEAD, 2 * HEAD)
        query, key = query_ref[:, cols], key_ref[:, cols]
        for head in range(2):
            score_ref[2 * pair + head] = pair_scores(one_head(query, lane, head), key)
    for copy in copies[2:]:
        copy.wait()


def attend(seen_ref, score_ref, query_ref, *refs):
    grps = seen_ref.shape[0]
    keys, values, out_ref = refs[: grps - 1], refs[grps - 1 : 2 * grps - 1], refs[2 * grps - 1]
    rows = query_ref.shape[0]
    lane = lax.broadcasted_iota(jnp.int32, (rows, 2 * HEAD), 1)
    for pair in range(query_ref.shape[1] // (2 * HEAD)):
        cols = pl.ds(pair * 2 * HEAD, 2 * HEAD)
        query = query_ref[:, cols]
        found = []
        for head in range(2):
            one = one_head(query, lane, head)
            scores = [score_ref[2 * pair + head]] + [
                pair_scores(one, keys[k][:, cols]) for k in range(grps - 1)
            ]
            scores = [
                jnp.where(seen_ref[k] > 0, part, -1e30) for k, part in enumerate(scores)
            ]
            largest = scores[0]
            for part in scores[1:]:
                largest = jnp.maximum(largest, part)
            largest = jnp.max(largest, axis=1, keepdims=True)
            weights = [jnp.exp(part - largest) for part in scores]
            total = weights[0]
            for part in weights[1:]:
                total = total + part
            total = jnp.sum(total, axis=1, keepdims=True)
            result = 0.0
            for k in range(grps):
                probs = (weights[k] / total).astype(jnp.bfloat16)
                result = result + jnp.dot(
                    probs, values[k][:, cols], preferred_element_type=jnp.float32
                )
            found.append(result)
        out_ref[:, cols] = jnp.where(lane < HEAD, found[0], found[1]).astype(jnp.bfloat16)


def project(place_ref, *refs):
    cores = place_ref.shape[0]
    attended, weights, packed = refs[:cores], refs[cores : 2 * cores], refs[2 * cores : 3 * cores]
    stream_ref, normed_ref, full, gain = refs[3 * cores :]
    rows, half = stream_ref.shape
    width = half * cores
    total = jnp.dot(attended[0][...], weights[0][...], preferred_element_type=jnp.float32)
    for j in range(1, cores):
        total = total + jnp.dot(
            attended[j][...], weights[j][...], preferred_element_type=jnp.float32
        )
    full[...] = total
    for j in range(cores):
        cols = pl.ds(pl.multiple_of(place_ref[j] * half, half), half)
        part = full[:, cols] + packed[j][pl.ds(0, rows), :].astype(jnp.float32)
        full[:, cols] = part
        if j == 0:
            stream_ref[...] = part
        gains = packed[j][pl.ds(rows, GAIN_ROWS), :].astype(jnp.float32)
        gain[0:1, cols] = (gains[1:2] + gains[2:3]) + gains[0:1]
    stream = full[...]
    center = jnp.sum(stream, axis=1, keepdims=True) / width
    shifted = stream - center
    spread_sq = jnp.sum(shifted * shifted, axis=1, keepdims=True) / width
    normed_ref[...] = (shifted * lax.rsqrt(spread_sq + 1e-05) * gain[0:1, :]).astype(jnp.bfloat16)


def call(kernel, out_shape, smem, args, flops, scratch=()):
    moved = sum(a.size * a.dtype.itemsize for a in args) + sum(
        o.size * o.dtype.itemsize for o in jax.tree.leaves(out_shape)
    )
    return pl.pallas_call(
        kernel,
        out_shape=out_shape,
        in_specs=[pl.BlockSpec(memory_space=pltpu.SMEM)] * smem
        + [pl.BlockSpec(memory_space=pltpu.VMEM)] * (len(args) - smem),
        scratch_shapes=scratch,
        cost_estimate=pl.CostEstimate(flops=flops, bytes_accessed=moved, transcendentals=0),
        compiler_params=pltpu.CompilerParams(vmem_limit_bytes=24 * 2**20),
    )(*args)


def send(x, routes):
    patches, grps, cores = (lax.axis_size(a) for a in ("patch", "grp", "col"))
    pairs = []
    for p in range(patches):
        for g in range(grps):
            for c, route in enumerate(routes):
                if route is not None:
                    to = ((p ^ route[0]) * grps + (g ^ route[1])) * cores + c
                    pairs.append(((p * grps + g) * cores + c, to))
    return lax.ppermute(x, ("patch", "grp", "col"), pairs)


def swap(x):
    return lax.ppermute(x, "col", [(0, 1), (1, 0)])


def hand_over(x):
    return lax.ppermute(x, "col", [(0, 1)])


def gather_plan(
    query_vectors,
    key_vectors,
    value_vectors,
    residual,
    neighbor_ids,
    neighbor_count,
    output_weight,
    norm_gain,
    up_weight,
    down_weight,
    cotangent,
):
    cores = lax.axis_size("col")
    grps = lax.axis_size("grp")
    rows, half = query_vectors.shape
    width = half * cores

    key_others = others(key_vectors, "grp")
    value_others = others(value_vectors, "grp")
    cot_others = others(cotangent, "col")
    weight_others = others(output_weight, "col")

    source = jnp.stack([member("grp", k) for k in range(grps)])
    slots = jnp.arange(neighbor_ids.shape[1], dtype=jnp.int32) < neighbor_count[0]
    seen = jnp.any((neighbor_ids[0][None] == source[:, None]) & slots[None], axis=1)
    place = jnp.stack([member("col", j) for j in range(cores)])
    heads = half // HEAD
    bf16 = jnp.bfloat16
    query, _, value, weight, packed, cot, scores = pl.pallas_call(
        stage,
        out_shape=[jax.ShapeDtypeStruct((rows, half), bf16)] * 3
        + [
            jax.ShapeDtypeStruct(output_weight.shape, bf16),
            jax.ShapeDtypeStruct((rows + GAIN_ROWS, half), bf16),
            jax.ShapeDtypeStruct((rows, width), bf16),
            jax.ShapeDtypeStruct((heads, rows, rows), jnp.float32),
        ],
        in_specs=[
            pl.BlockSpec(memory_space=pltpu.SMEM),
            pl.BlockSpec((1, half), lambda i: (0, 0)),
        ]
        + [pl.BlockSpec(memory_space=pl.ANY)] * (5 + cores),
        out_specs=[pl.BlockSpec(memory_space=pltpu.VMEM)] * 7,
        grid=(1,),
        scratch_shapes=[pltpu.SemaphoreType.DMA((5 + cores,))],
        cost_estimate=pl.CostEstimate(
            flops=2 * rows * rows * width, bytes_accessed=4 * 2**20, transcendentals=0
        ),
        compiler_params=pltpu.CompilerParams(vmem_limit_bytes=STAGE_LIMIT),
    )(
        place,
        norm_gain[None],
        query_vectors,
        key_vectors,
        value_vectors,
        output_weight,
        residual,
        cotangent,
        *cot_others,
    )
    packed_others = others(packed, "col")
    cot12 = send(cot, [(1, 0), (2, 0)])
    cot3x = send(cot, [(3, 0), (0, 1)])
    attended = call(
        attend,
        jax.ShapeDtypeStruct((rows, half), jnp.bfloat16),
        1,
        [seen.astype(jnp.int32), scores, query] + key_others + [value] + value_others,
        4 * rows * rows * grps * width,
    )
    attended_others = others(attended, "col")
    stream, normed = call(
        project,
        (
            jax.ShapeDtypeStruct((rows, half), jnp.float32),
            jax.ShapeDtypeStruct((rows, width), bf16),
        ),
        1,
        [place, attended]
        + attended_others
        + [weight]
        + weight_others
        + [packed]
        + packed_others,
        2 * rows * width * width,
        [pltpu.VMEM((rows, width), jnp.float32), pltpu.VMEM((8, width), jnp.float32)],
    )
    first = lax.axis_index("col") == 0

    def passed_on(own, by12, by3x):
        swap12, swap3x = swap(by12), swap(by3x)
        over12 = send(by12, [(0, 1), (0, 1)])
        over3 = send(by3x, [(0, 1), None])
        group = jnp.concatenate([own, jnp.where(first, swap3x, by3x)], 0)
        third = jnp.concatenate(
            [jnp.where(first, by3x, swap3x), jnp.where(first, over3, hand_over(over3))], 0
        )
        return [
            group,
            jnp.concatenate([by12, swap12], 0),
            jnp.concatenate([over12, swap(over12)], 0),
            third,
        ]

    norm12 = send(normed, [(1, 0), (2, 0)])
    norm3x = send(normed, [(3, 0), (0, 1)])
    cots = passed_on(cot, after(cot12, normed), after(cot3x, normed))
    norms = passed_on(normed, norm12, norm3x)

    saved = []
    layer_out = None
    for s, (normed_rows, back_rows) in enumerate(zip(norms, cots)):
        pre = jnp.dot(normed_rows, up_weight, preferred_element_type=jnp.float32)
        hidden = jax.nn.gelu(pre).astype(bf16)
        if s == 0:
            partial_out = jnp.dot(hidden, down_weight, preferred_element_type=jnp.float32)
            partial_out = partial_out.astype(bf16)
            mine, theirs = (
                lax.dynamic_slice(partial_out, (0, place[j] * half), (2 * rows, half)) for j in (0, 1)
            )
            both = mine.astype(jnp.float32) + swap(theirs).astype(jnp.float32)
            rest = lax.ppermute(both[rows:].astype(bf16), "grp", [(0, 1), (1, 0)])
            layer_out = (stream + both[:rows] + rest.astype(jnp.float32)).astype(bf16)
        back_hidden = lax.dot_general(
            back_rows, down_weight, (((1,), (1,)), ((), ())), preferred_element_type=jnp.float32
        )
        _, gelu_back = jax.vjp(jax.nn.gelu, pre)
        back_pre = gelu_back(back_hidden)[0].astype(bf16)
        saved.append((normed_rows, back_rows, hidden, back_pre))
    all_normed, all_back, all_hidden, all_pre = (jnp.concatenate(a, 0) for a in zip(*saved))
    up_grad = lax.dot_general(
        all_normed, all_pre, (((0,), (0,)), ((), ())), preferred_element_type=jnp.float32
    )
    down_grad = lax.dot_general(
        all_hidden, all_back, (((0,), (0,)), ((), ())), preferred_element_type=jnp.float32
    )
    return (layer_out, up_grad, down_grad)


def layer(*args):
    query_vectors, up_weight = args[0], args[8]
    patches, grps, cores = (lax.axis_size(a) for a in ("patch", "grp", "col"))
    tokens = query_vectors.shape[0] * grps * patches
    if (patches, grps, cores) == (4, 2, 2) and tokens <= 2 * up_weight.shape[1]:
        return gather_plan(*args)
    return shards(*args)


def solution(mesh):
    return jax.shard_map(
        layer,
        mesh=mesh,
        in_specs=(
            P(("parts", "patch", "grp"), "col"),
            P(("parts", "patch", "grp"), "col"),
            P(("parts", "patch", "grp"), "col"),
            P(("parts", "patch", "grp"), "col"),
            P(("parts", "patch", "grp"), None),
            P(("parts", "patch", "grp")),
            P("col", None),
            P("col"),
            P(None, ("grp", "col")),
            P(("grp", "col"), None),
            P(("parts", "patch", "grp"), "col"),
        ),
        out_specs=(
            P(("parts", "patch", "grp"), "col"),
            P("parts", ("grp", "col")),
            P(("parts", "grp", "col"), None),
        ),
        check_vma=False,
    )
```

```python
import functools

import jax
import jax.numpy as jnp
from jax import lax
from jax.experimental import pallas as pl
from jax.experimental.pallas import tpu as pltpu
from jax.sharding import PartitionSpec as P

HEAD = 64
D = 1024
BLK = 128


def spread_rows(part_rows):
    stacked = lax.all_gather(part_rows[None], ("grp", "col"), axis=0, tiled=True)
    grp_count = lax.axis_size("grp")
    col_count = lax.axis_size("col")
    row_count = part_rows.shape[0]
    half_width = part_rows.shape[1]
    arranged = stacked.reshape(grp_count, col_count, row_count, half_width).transpose(0, 2, 1, 3)
    return arranged.reshape(grp_count * row_count, col_count * half_width)


def shards(
    query_vectors,
    key_vectors,
    value_vectors,
    residual,
    neighbor_ids,
    neighbor_count,
    output_weight,
    norm_gain,
    up_weight,
    down_weight,
    cotangent,
):
    key_all, value_all = (
        lax.all_gather(key_vectors, "grp", axis=0, tiled=True),
        lax.all_gather(value_vectors, "grp", axis=0, tiled=True),
    )
    row_count = query_vectors.shape[0]
    local_heads = query_vectors.shape[1] // HEAD
    group_count = key_all.shape[0] // BLK
    column_ids = jnp.arange(group_count, dtype=jnp.int32)
    slot_ids = jnp.arange(neighbor_ids.shape[1], dtype=jnp.int32)
    listed = (neighbor_ids[:, :, None] == column_ids[None, None, :]) & (
        slot_ids[None, :, None] < neighbor_count[:, None, None]
    )
    allowed = jnp.any(listed, axis=1)
    token_mask = jnp.repeat(jnp.repeat(allowed, BLK, axis=0), BLK, axis=1)
    query_heads = query_vectors.reshape(row_count, local_heads, HEAD)
    key_heads = key_all.reshape(-1, local_heads, HEAD)
    value_heads = value_all.reshape(-1, local_heads, HEAD)
    scores = jnp.einsum(
        "qhd,khd->hqk", query_heads, key_heads, preferred_element_type=jnp.float32
    ) * HEAD ** (-0.5)
    scores = jnp.where(token_mask[None], scores, -1e30)
    largest = jnp.max(scores, axis=2, keepdims=True)
    weights = jnp.exp(scores - largest)
    probs = (weights / jnp.sum(weights, axis=2, keepdims=True)).astype(jnp.bfloat16)
    attended = jnp.einsum("hqk,khd->qhd", probs, value_heads, preferred_element_type=jnp.float32)
    attended = attended.astype(jnp.bfloat16).reshape(row_count, -1)
    projected = jnp.dot(attended, output_weight, preferred_element_type=jnp.float32)
    stream = residual.astype(jnp.float32) + lax.psum_scatter(
        projected.astype(jnp.bfloat16), "col", scatter_dimension=1, tiled=True
    ).astype(jnp.float32)
    first_sum, second_sum = lax.psum(
        (jnp.sum(stream, axis=1), jnp.sum(stream * stream, axis=1)), "col"
    )
    center = first_sum[:, None] / D
    shifted = stream - center
    spread_sq = second_sum[:, None] / D - center * center
    normed = (shifted * lax.rsqrt(spread_sq + 1e-05) * norm_gain[None, :]).astype(jnp.bfloat16)
    normed_rows = spread_rows(normed)
    pre = jnp.dot(normed_rows, up_weight, preferred_element_type=jnp.float32)
    hidden = jax.nn.gelu(pre).astype(jnp.bfloat16)
    grp_count = lax.axis_size("grp")
    col_count = lax.axis_size("col")
    partial_out = jnp.dot(hidden, down_weight, preferred_element_type=jnp.float32)
    half_width = partial_out.shape[1] // col_count
    partial_out = partial_out.reshape(grp_count, row_count, col_count, half_width).transpose(
        0, 2, 1, 3
    )
    partial_out = partial_out.reshape(grp_count * col_count * row_count, half_width)
    ff_out = lax.psum_scatter(
        partial_out.astype(jnp.bfloat16), ("grp", "col"), scatter_dimension=0, tiled=True
    ).astype(jnp.float32)
    layer_out = (stream + ff_out).astype(jnp.bfloat16)
    back_rows = spread_rows(cotangent)
    back_hidden = lax.dot_general(
        back_rows, down_weight, (((1,), (1,)), ((), ())), preferred_element_type=jnp.float32
    )
    _, gelu_back = jax.vjp(jax.nn.gelu, pre)
    back_pre = gelu_back(back_hidden)[0].astype(jnp.bfloat16)
    up_local = lax.dot_general(
        normed_rows, back_pre, (((0,), (0,)), ((), ())), preferred_element_type=jnp.float32
    )
    down_local = lax.dot_general(
        hidden, back_rows, (((0,), (0,)), ((), ())), preferred_element_type=jnp.float32
    )
    up_grad, down_grad = (
        lax.psum(up_local.astype(jnp.bfloat16), "patch").astype(jnp.float32),
        lax.psum(down_local.astype(jnp.bfloat16), "patch").astype(jnp.float32),
    )
    return (layer_out, up_grad, down_grad)


GAIN_ROWS = 16
TILE = 256
OWN_LIMIT = 56 * 2**20


def shift(x, axis, k):
    n = lax.axis_size(axis)
    return lax.ppermute(x, axis, [(i, (i + k) % n) for i in range(n)])


def after(x, *others):
    return lax.optimization_barrier((x,) + others)[0]


def others(x, axis):
    n = lax.axis_size(axis)
    if n & (n - 1):
        return [shift(x, axis, k) for k in range(1, n)]
    return [lax.ppermute(x, axis, [(i, i ^ k) for i in range(n)]) for k in range(1, n)]


def member(axis, k):
    n = lax.axis_size(axis)
    me = lax.axis_index(axis)
    return (me - k + n) % n if n & (n - 1) else me ^ k


def one_head(query, lane, head):
    return jnp.where((lane < HEAD) == (head == 0), query, jnp.zeros_like(query))


def pair_scores(query, key):
    return lax.dot_general(
        query, key, (((1,), (1,)), ((), ())), preferred_element_type=jnp.float32
    ) * HEAD ** (-0.5)


def core_columns(j, half):
    return pl.ds(pl.multiple_of(member("col", j) * half, half), half)


def join_cores(weight_ref, *refs):
    parts, (kept_ref, out_ref) = refs[:-2], refs[-2:]
    half = parts[0].shape[1]
    for j, part in enumerate(parts):
        out_ref[:, core_columns(j, half)] = part[...]
    kept_ref[...] = weight_ref[...]


def attend(grps, ids_ref, count_ref, gain_ref, residual_ref, query_ref, *refs):
    seen = []
    for k in range(grps):
        listed = [
            (ids_ref[0, m] == member("grp", k)) & (m < count_ref[0]) for m in range(ids_ref.shape[1])
        ]
        seen.append(functools.reduce(jnp.logical_or, listed))
    keys, values, (out_ref, score_ref) = refs[:grps], refs[grps : 2 * grps], refs[2 * grps :]
    rows, half = query_ref.shape
    heads = half // HEAD
    lane = lax.broadcasted_iota(jnp.int32, (rows, 2 * HEAD), 1)
    for head in range(heads):
        cols = pl.ds(head // 2 * 2 * HEAD, 2 * HEAD)
        query = one_head(query_ref[:, cols], lane, head % 2)
        for k in range(grps):
            part = pair_scores(query, keys[k][:, cols])
            score_ref[head * grps + k] = jnp.where(seen[k], part, -1e30)
    for pair in range(heads // 2):
        cols = pl.ds(pair * 2 * HEAD, 2 * HEAD)
        value = [ref[:, cols] for ref in values]
        found = []
        for head in (2 * pair, 2 * pair + 1):
            scores = [score_ref[head * grps + k] for k in range(grps)]
            largest = scores[0]
            for part in scores[1:]:
                largest = jnp.maximum(largest, part)
            largest = jnp.max(largest, axis=1, keepdims=True)
            weights = [jnp.exp(part - largest) for part in scores]
            total = weights[0]
            for part in weights[1:]:
                total = total + part
            total = jnp.sum(total, axis=1, keepdims=True)
            result = 0.0
            for k in range(grps):
                probs = (weights[k] / total).astype(jnp.bfloat16)
                result = result + jnp.dot(probs, value[k], preferred_element_type=jnp.float32)
            found.append(result)
        out_ref[pl.ds(0, rows), cols] = jnp.where(lane < HEAD, found[0], found[1]).astype(
            jnp.bfloat16
        )
    gain = gain_ref[...]
    high = gain.astype(jnp.bfloat16).astype(jnp.float32)
    middle = (gain - high).astype(jnp.bfloat16).astype(jnp.float32)
    low = gain - high - middle
    row = lax.broadcasted_iota(jnp.int32, (GAIN_ROWS, half), 0)
    parts = jnp.where(
        row == 0, high, jnp.where(row == 1, middle, jnp.where(row == 2, low, 0.0))
    )
    out_ref[pl.ds(rows, GAIN_ROWS), :] = parts.astype(jnp.bfloat16)
    out_ref[pl.ds(rows + GAIN_ROWS, rows), :] = residual_ref[...]


def project(cores, *refs):
    packs, weights, (stream_ref, normed_ref, full, gain) = refs[:cores], refs[cores:-4], refs[-4:]
    rows, half = stream_ref.shape
    width = half * cores
    full[...] = sum(
        jnp.dot(pack[pl.ds(0, rows), :], weight[...], preferred_element_type=jnp.float32)
        for pack, weight in zip(packs, weights)
    )
    for j, pack in enumerate(packs):
        cols = core_columns(j, half)
        part = full[:, cols] + pack[pl.ds(rows + GAIN_ROWS, rows), :].astype(jnp.float32)
        full[:, cols] = part
        if j == 0:
            stream_ref[...] = part
        gains = pack[pl.ds(rows, GAIN_ROWS), :].astype(jnp.float32)
        gain[0:1, cols] = (gains[1:2] + gains[2:3]) + gains[0:1]
    stream = full[...]
    center = jnp.sum(stream, axis=1, keepdims=True) / width
    shifted = stream - center
    spread_sq = jnp.sum(shifted * shifted, axis=1, keepdims=True) / width
    normed_ref[...] = (shifted * lax.rsqrt(spread_sq + 1e-05) * gain[0:1, :]).astype(jnp.bfloat16)


def add_products(*refs):
    pairs, (up_ref, down_ref) = refs[:-2], refs[-2:]
    count = len(pairs) // 4
    for start in range(0, up_ref.shape[0], TILE):
        tile = pl.ds(start, TILE)
        for k, out_ref in ((0, up_ref), (2, down_ref)):
            out_ref[tile, :] = sum(
                lax.dot_general(
                    pairs[4 * i + k][:, tile],
                    pairs[4 * i + k + 1][...],
                    (((0,), (0,)), ((), ())),
                    preferred_element_type=jnp.float32,
                )
                for i in range(count)
            )


def finish_products(*refs):
    up_sum, down_sum = refs[:2]
    up_ref, down_ref, buffer, sems = refs[-4:]
    pairs = refs[2:-4]
    count = len(pairs) // 4
    copies = []
    for start in range(0, up_ref.shape[0], TILE):
        tile = pl.ds(start, TILE)
        for k, sum_ref, out_ref in ((0, up_sum, up_ref), (2, down_sum, down_ref)):
            slot = len(copies) % buffer.shape[0]
            if len(copies) >= buffer.shape[0]:
                copies[-buffer.shape[0]].wait()
            buffer[slot] = sum_ref[tile, :] + sum(
                lax.dot_general(
                    pairs[4 * i + k][:, tile],
                    pairs[4 * i + k + 1][...],
                    (((0,), (0,)), ((), ())),
                    preferred_element_type=jnp.float32,
                )
                for i in range(count)
            )
            copies.append(
                pltpu.make_async_copy(buffer.at[slot], out_ref.at[tile], sems.at[slot])
            )
            copies[-1].start()
    for copy in copies[-buffer.shape[0] :]:
        copy.wait()


def call(kernel, out_shape, smem, args, flops, scratch=(), limit=16 * 2**20):
    moved = sum(a.size * a.dtype.itemsize for a in args) + sum(
        o.size * o.dtype.itemsize for o in jax.tree.leaves(out_shape)
    )
    return pl.pallas_call(
        kernel,
        out_shape=out_shape,
        in_specs=[pl.BlockSpec(memory_space=pltpu.SMEM)] * smem
        + [pl.BlockSpec(memory_space=pltpu.VMEM)] * (len(args) - smem),
        scratch_shapes=scratch,
        cost_estimate=pl.CostEstimate(flops=flops, bytes_accessed=moved, transcendentals=0),
        compiler_params=pltpu.CompilerParams(vmem_limit_bytes=limit),
    )(*args)


def send(x, routes):
    patches, grps, cores = (lax.axis_size(a) for a in ("patch", "grp", "col"))
    pairs = []
    for p in range(patches):
        for g in range(grps):
            for c, route in enumerate(routes):
                if route is not None:
                    to = ((p ^ route[0]) * grps + (g ^ route[1])) * cores + c
                    pairs.append(((p * grps + g) * cores + c, to))
    return lax.ppermute(x, ("patch", "grp", "col"), pairs)


def swap(x):
    return lax.ppermute(x, "col", [(0, 1), (1, 0)])


def hand_over(x):
    return lax.ppermute(x, "col", [(0, 1)])


def gather_plan(
    query_vectors,
    key_vectors,
    value_vectors,
    residual,
    neighbor_ids,
    neighbor_count,
    output_weight,
    norm_gain,
    up_weight,
    down_weight,
    cotangent,
):
    cores = lax.axis_size("col")
    grps = lax.axis_size("grp")
    rows, half = query_vectors.shape
    width = half * cores

    bf16 = jnp.bfloat16
    cot_parts = [cotangent] + others(cotangent, "col")
    keys = [key_vectors] + others(key_vectors, "grp")
    values = [value_vectors] + others(value_vectors, "grp")
    weights = [output_weight] + others(output_weight, "col")
    weights[0], cot = call(
        join_cores,
        (
            jax.ShapeDtypeStruct(output_weight.shape, bf16),
            jax.ShapeDtypeStruct((rows, width), bf16),
        ),
        0,
        [output_weight] + cot_parts,
        0,
    )
    cot12 = send(cot, [(1, 0), (2, 0)])
    cot3x = send(cot, [(3, 0), (0, 1)])

    packed = call(
        functools.partial(attend, grps),
        jax.ShapeDtypeStruct((2 * rows + GAIN_ROWS, half), bf16),
        2,
        [neighbor_ids, neighbor_count, norm_gain[None], residual, after(query_vectors, cot)]
        + keys
        + values,
        4 * rows * rows * grps * width,
        [pltpu.VMEM((half // HEAD * grps, rows, rows), jnp.float32)],
        OWN_LIMIT,
    )
    stream, normed = call(
        functools.partial(project, cores),
        (
            jax.ShapeDtypeStruct((rows, half), jnp.float32),
            jax.ShapeDtypeStruct((rows, width), bf16),
        ),
        0,
        [packed] + others(packed, "col") + weights,
        2 * rows * width * width,
        [pltpu.VMEM((rows, width), jnp.float32), pltpu.VMEM((8, width), jnp.float32)],
    )
    first = lax.axis_index("col") == 0

    def pairs_of(own, by12, by3x, swapped, over12, over3, swapped_over):
        swap12, swap3x = swapped[:rows], swapped[rows:]
        return [
            jnp.concatenate([own, jnp.where(first, swap3x, by3x)], 0),
            jnp.concatenate([by12, swap12], 0),
            jnp.concatenate([over12, swapped_over[:rows]], 0),
            jnp.concatenate(
                [jnp.where(first, by3x, swap3x), jnp.where(first, over3, swapped_over[rows:])], 0
            ),
        ]

    def forward(by12, by3x):
        return send(by12, [(0, 1), (0, 1)]), send(by3x, [(0, 1), None])

    norm12 = send(normed, [(1, 0), (2, 0)])
    norm3x = send(normed, [(3, 0), (0, 1)])
    own_pre = jnp.dot(normed, up_weight, preferred_element_type=jnp.float32)
    cot12, cot3x = after(cot12, own_pre), after(cot3x, norm12)
    over12, over3 = forward(cot12, cot3x)
    late = swap(jnp.concatenate([cot3x, over12], 0))
    cots = pairs_of(
        cot,
        cot12,
        cot3x,
        jnp.concatenate([swap(cot12), late[:rows]], 0),
        over12,
        over3,
        jnp.concatenate([late[rows:], hand_over(over3)], 0),
    )
    over12, over3 = forward(norm12, norm3x)
    norms = pairs_of(
        normed,
        norm12,
        norm3x,
        jnp.concatenate([swap(norm12), swap(norm3x)], 0),
        over12,
        over3,
        jnp.concatenate([swap(over12), hand_over(over3)], 0),
    )

    saved = []
    layer_out = None
    for s, (normed_rows, back_rows) in enumerate(zip(norms, cots)):
        if s == 0:
            pre = jnp.dot(normed_rows[rows:], up_weight, preferred_element_type=jnp.float32)
            pre = jnp.concatenate([own_pre, pre], 0)
        else:
            pre = jnp.dot(normed_rows, up_weight, preferred_element_type=jnp.float32)
        hidden = jax.nn.gelu(pre).astype(bf16)
        if s == 0:
            partial_out = jnp.dot(hidden, down_weight, preferred_element_type=jnp.float32)
            partial_out = partial_out.astype(bf16)
            mine, theirs = (
                lax.dynamic_slice(partial_out, (0, member("col", j) * half), (2 * rows, half)) for j in (0, 1)
            )
            both = mine.astype(jnp.float32) + swap(theirs).astype(jnp.float32)
            rest = lax.ppermute(both[rows:].astype(bf16), "grp", [(0, 1), (1, 0)])
            layer_out = (stream + both[:rows] + rest.astype(jnp.float32)).astype(bf16)
        back_hidden = lax.dot_general(
            back_rows, down_weight, (((1,), (1,)), ((), ())), preferred_element_type=jnp.float32
        )
        _, gelu_back = jax.vjp(jax.nn.gelu, pre)
        back_pre = gelu_back(back_hidden)[0].astype(bf16)
        saved.append([normed_rows, back_pre, hidden, back_rows])
    panel = up_weight.shape[1]
    grads = (
        jax.ShapeDtypeStruct((width, panel), jnp.float32),
        jax.ShapeDtypeStruct((panel, width), jnp.float32),
    )
    early, last = saved[0] + saved[1], saved[2] + saved[3]
    flops = 8 * 2 * rows * panel * width
    sums = call(add_products, grads, 0, early, flops)
    up_grad, down_grad = pl.pallas_call(
        finish_products,
        out_shape=grads,
        in_specs=[pl.BlockSpec(memory_space=pltpu.VMEM)] * (2 + len(last)),
        out_specs=[pl.BlockSpec(memory_space=pl.ANY)] * 2,
        scratch_shapes=[
            pltpu.VMEM((4, TILE, width), jnp.float32),
            pltpu.SemaphoreType.DMA((4,)),
        ],
        cost_estimate=pl.CostEstimate(
            flops=flops, bytes_accessed=16 * panel * width, transcendentals=0
        ),
        compiler_params=pltpu.CompilerParams(vmem_limit_bytes=16 * 2**20),
    )(*sums, *last)
    return (layer_out, up_grad, down_grad)


def layer(*args):
    query_vectors, up_weight = args[0], args[8]
    patches, grps, cores = (lax.axis_size(a) for a in ("patch", "grp", "col"))
    tokens = query_vectors.shape[0] * grps * patches
    if (patches, grps, cores) == (4, 2, 2) and tokens <= 2 * up_weight.shape[1]:
        return gather_plan(*args)
    return shards(*args)


def solution(mesh):
    return jax.shard_map(
        layer,
        mesh=mesh,
        in_specs=(
            P(("parts", "patch", "grp"), "col"),
            P(("parts", "patch", "grp"), "col"),
            P(("parts", "patch", "grp"), "col"),
            P(("parts", "patch", "grp"), "col"),
            P(("parts", "patch", "grp"), None),
            P(("parts", "patch", "grp")),
            P("col", None),
            P("col"),
            P(None, ("grp", "col")),
            P(("grp", "col"), None),
            P(("parts", "patch", "grp"), "col"),
        ),
        out_specs=(
            P(("parts", "patch", "grp"), "col"),
            P("parts", ("grp", "col")),
            P(("parts", "grp", "col"), None),
        ),
        check_vma=False,
    )
```

```python
import functools

import jax
import jax.numpy as jnp
from jax import lax
from jax.experimental import pallas as pl
from jax.experimental.pallas import tpu as pltpu
from jax.sharding import PartitionSpec as P

HEAD = 64
D = 1024
BLK = 128


def spread_rows(part_rows):
    stacked = lax.all_gather(part_rows[None], ("grp", "col"), axis=0, tiled=True)
    grp_count = lax.axis_size("grp")
    col_count = lax.axis_size("col")
    row_count = part_rows.shape[0]
    half_width = part_rows.shape[1]
    arranged = stacked.reshape(grp_count, col_count, row_count, half_width).transpose(0, 2, 1, 3)
    return arranged.reshape(grp_count * row_count, col_count * half_width)


def shards(
    query_vectors,
    key_vectors,
    value_vectors,
    residual,
    neighbor_ids,
    neighbor_count,
    output_weight,
    norm_gain,
    up_weight,
    down_weight,
    cotangent,
):
    key_all, value_all = (
        lax.all_gather(key_vectors, "grp", axis=0, tiled=True),
        lax.all_gather(value_vectors, "grp", axis=0, tiled=True),
    )
    row_count = query_vectors.shape[0]
    local_heads = query_vectors.shape[1] // HEAD
    group_count = key_all.shape[0] // BLK
    column_ids = jnp.arange(group_count, dtype=jnp.int32)
    slot_ids = jnp.arange(neighbor_ids.shape[1], dtype=jnp.int32)
    listed = (neighbor_ids[:, :, None] == column_ids[None, None, :]) & (
        slot_ids[None, :, None] < neighbor_count[:, None, None]
    )
    allowed = jnp.any(listed, axis=1)
    token_mask = jnp.repeat(jnp.repeat(allowed, BLK, axis=0), BLK, axis=1)
    query_heads = query_vectors.reshape(row_count, local_heads, HEAD)
    key_heads = key_all.reshape(-1, local_heads, HEAD)
    value_heads = value_all.reshape(-1, local_heads, HEAD)
    scores = jnp.einsum(
        "qhd,khd->hqk", query_heads, key_heads, preferred_element_type=jnp.float32
    ) * HEAD ** (-0.5)
    scores = jnp.where(token_mask[None], scores, -1e30)
    largest = jnp.max(scores, axis=2, keepdims=True)
    weights = jnp.exp(scores - largest)
    probs = (weights / jnp.sum(weights, axis=2, keepdims=True)).astype(jnp.bfloat16)
    attended = jnp.einsum("hqk,khd->qhd", probs, value_heads, preferred_element_type=jnp.float32)
    attended = attended.astype(jnp.bfloat16).reshape(row_count, -1)
    projected = jnp.dot(attended, output_weight, preferred_element_type=jnp.float32)
    stream = residual.astype(jnp.float32) + lax.psum_scatter(
        projected.astype(jnp.bfloat16), "col", scatter_dimension=1, tiled=True
    ).astype(jnp.float32)
    first_sum, second_sum = lax.psum(
        (jnp.sum(stream, axis=1), jnp.sum(stream * stream, axis=1)), "col"
    )
    center = first_sum[:, None] / D
    shifted = stream - center
    spread_sq = second_sum[:, None] / D - center * center
    normed = (shifted * lax.rsqrt(spread_sq + 1e-05) * norm_gain[None, :]).astype(jnp.bfloat16)
    normed_rows = spread_rows(normed)
    pre = jnp.dot(normed_rows, up_weight, preferred_element_type=jnp.float32)
    hidden = jax.nn.gelu(pre).astype(jnp.bfloat16)
    grp_count = lax.axis_size("grp")
    col_count = lax.axis_size("col")
    partial_out = jnp.dot(hidden, down_weight, preferred_element_type=jnp.float32)
    half_width = partial_out.shape[1] // col_count
    partial_out = partial_out.reshape(grp_count, row_count, col_count, half_width).transpose(
        0, 2, 1, 3
    )
    partial_out = partial_out.reshape(grp_count * col_count * row_count, half_width)
    ff_out = lax.psum_scatter(
        partial_out.astype(jnp.bfloat16), ("grp", "col"), scatter_dimension=0, tiled=True
    ).astype(jnp.float32)
    layer_out = (stream + ff_out).astype(jnp.bfloat16)
    back_rows = spread_rows(cotangent)
    back_hidden = lax.dot_general(
        back_rows, down_weight, (((1,), (1,)), ((), ())), preferred_element_type=jnp.float32
    )
    _, gelu_back = jax.vjp(jax.nn.gelu, pre)
    back_pre = gelu_back(back_hidden)[0].astype(jnp.bfloat16)
    up_local = lax.dot_general(
        normed_rows, back_pre, (((0,), (0,)), ((), ())), preferred_element_type=jnp.float32
    )
    down_local = lax.dot_general(
        hidden, back_rows, (((0,), (0,)), ((), ())), preferred_element_type=jnp.float32
    )
    up_grad, down_grad = (
        lax.psum(up_local.astype(jnp.bfloat16), "patch").astype(jnp.float32),
        lax.psum(down_local.astype(jnp.bfloat16), "patch").astype(jnp.float32),
    )
    return (layer_out, up_grad, down_grad)


GAIN_ROWS = 16
TILE = 256
PANEL_TILE = 512
ROOT, CUBIC = 0.7978845608028654, 0.044715
OWN_LIMIT = 56 * 2**20


def shift(x, axis, k):
    n = lax.axis_size(axis)
    return lax.ppermute(x, axis, [(i, (i + k) % n) for i in range(n)])


def after(x, *others):
    return lax.optimization_barrier((x,) + others)[0]


def others(x, axis):
    n = lax.axis_size(axis)
    if n & (n - 1):
        return [shift(x, axis, k) for k in range(1, n)]
    return [lax.ppermute(x, axis, [(i, i ^ k) for i in range(n)]) for k in range(1, n)]


def member(axis, k):
    n = lax.axis_size(axis)
    me = lax.axis_index(axis)
    return (me - k + n) % n if n & (n - 1) else me ^ k


def one_head(query, lane, head):
    return jnp.where((lane < HEAD) == (head == 0), query, jnp.zeros_like(query))


def pair_scores(query, key):
    return lax.dot_general(
        query, key, (((1,), (1,)), ((), ())), preferred_element_type=jnp.float32
    ) * HEAD ** (-0.5)


def core_columns(j, half):
    return pl.ds(pl.multiple_of(member("col", j) * half, half), half)


def join_cores(*refs):
    parts, out_ref = refs[:-1], refs[-1]
    half = parts[0].shape[1]
    for j, part in enumerate(parts):
        out_ref[:, core_columns(j, half)] = part[...]


def keep(*refs):
    count = len(refs) // 2
    for source, target in zip(refs[:count], refs[count:]):
        target[...] = source[...]


def gelu_and_slope(pre):
    square = pre * pre
    curve = jnp.tanh(ROOT * (pre + CUBIC * (square * pre)))
    half = 0.5 * (1.0 + curve)
    slope = half + 0.5 * pre * (1.0 - curve * curve) * (ROOT * (1.0 + 3.0 * CUBIC * square))
    return pre * half, slope


def feed_forward(choices, share, *refs):
    count = 2 * sum(choices)
    blocks, (up_ref, down_ref), outs = refs[:count], refs[count : count + 2], refs[count + 2 :]
    rows_ref, back_pre_ref, hidden_ref, back_ref = outs[:4]
    first = lax.axis_index("col") == 0
    at = 0
    for out_ref in (rows_ref, back_ref):
        for i, width in enumerate(choices):
            rows = blocks[at].shape[0]
            block = blocks[at][...]
            if width == 2:
                block = jnp.where(first, block, blocks[at + 1][...])
            out_ref[pl.ds(i * rows, rows), :] = block
            at += width
    rows, back = rows_ref[...], back_ref[...]
    for start in range(0, up_ref.shape[1], PANEL_TILE):
        tile = pl.ds(start, PANEL_TILE)
        pre = jnp.dot(rows, up_ref[:, tile], preferred_element_type=jnp.float32)
        back_hidden = lax.dot_general(
            back, down_ref[tile, :], (((1,), (1,)), ((), ())), preferred_element_type=jnp.float32
        )
        hidden, slope = gelu_and_slope(pre)
        hidden_ref[:, tile] = hidden.astype(jnp.bfloat16)
        back_pre_ref[:, tile] = (back_hidden * slope).astype(jnp.bfloat16)
    if share:
        for j, out_ref in enumerate(outs[4:]):
            part = jnp.dot(
                hidden_ref[...],
                down_ref[:, core_columns(j, out_ref.shape[1])],
                preferred_element_type=jnp.float32,
            )
            out_ref[...] = part.astype(out_ref.dtype)


def attend(grps, ids_ref, count_ref, gain_ref, query_ref, *refs):
    seen = []
    for k in range(grps):
        listed = [
            (ids_ref[0, m] == member("grp", k)) & (m < count_ref[0]) for m in range(ids_ref.shape[1])
        ]
        seen.append(functools.reduce(jnp.logical_or, listed))
    keys, values, (out_ref, score_ref) = refs[:grps], refs[grps : 2 * grps], refs[2 * grps :]
    rows, half = query_ref.shape
    heads = half // HEAD
    lane = lax.broadcasted_iota(jnp.int32, (rows, 2 * HEAD), 1)
    for head in range(heads):
        cols = pl.ds(head // 2 * 2 * HEAD, 2 * HEAD)
        query = one_head(query_ref[:, cols], lane, head % 2)
        for k in range(grps):
            part = pair_scores(query, keys[k][:, cols])
            score_ref[head * grps + k] = jnp.where(seen[k], part, -1e30)
    for pair in range(heads // 2):
        cols = pl.ds(pair * 2 * HEAD, 2 * HEAD)
        value = [ref[:, cols] for ref in values]
        found = []
        for head in (2 * pair, 2 * pair + 1):
            scores = [score_ref[head * grps + k] for k in range(grps)]
            largest = scores[0]
            for part in scores[1:]:
                largest = jnp.maximum(largest, part)
            largest = jnp.max(largest, axis=1, keepdims=True)
            weights = [jnp.exp(part - largest) for part in scores]
            total = weights[0]
            for part in weights[1:]:
                total = total + part
            total = jnp.sum(total, axis=1, keepdims=True)
            result = 0.0
            for k in range(grps):
                probs = (weights[k] / total).astype(jnp.bfloat16)
                result = result + jnp.dot(probs, value[k], preferred_element_type=jnp.float32)
            found.append(result)
        out_ref[pl.ds(0, rows), cols] = jnp.where(lane < HEAD, found[0], found[1]).astype(
            jnp.bfloat16
        )
    gain = gain_ref[...]
    high = gain.astype(jnp.bfloat16).astype(jnp.float32)
    middle = (gain - high).astype(jnp.bfloat16).astype(jnp.float32)
    low = gain - high - middle
    row = lax.broadcasted_iota(jnp.int32, (GAIN_ROWS, half), 0)
    parts = jnp.where(
        row == 0, high, jnp.where(row == 1, middle, jnp.where(row == 2, low, 0.0))
    )
    out_ref[pl.ds(rows, GAIN_ROWS), :] = parts.astype(jnp.bfloat16)


def project(cores, *refs):
    packs, weights, residuals = refs[:cores], refs[cores : 2 * cores], refs[2 * cores : 3 * cores]
    stream_ref, normed_ref, full, gain = refs[3 * cores :]
    rows, half = stream_ref.shape
    width = half * cores
    full[...] = sum(
        jnp.dot(pack[pl.ds(0, rows), :], weight[...], preferred_element_type=jnp.float32)
        for pack, weight in zip(packs, weights)
    )
    for j, pack in enumerate(packs):
        cols = core_columns(j, half)
        part = full[:, cols] + residuals[j][...].astype(jnp.float32)
        full[:, cols] = part
        if j == 0:
            stream_ref[...] = part
        gains = pack[pl.ds(rows, GAIN_ROWS), :].astype(jnp.float32)
        gain[0:1, cols] = (gains[1:2] + gains[2:3]) + gains[0:1]
    stream = full[...]
    center = jnp.sum(stream, axis=1, keepdims=True) / width
    shifted = stream - center
    spread_sq = jnp.sum(shifted * shifted, axis=1, keepdims=True) / width
    normed_ref[...] = (shifted * lax.rsqrt(spread_sq + 1e-05) * gain[0:1, :]).astype(jnp.bfloat16)


def add_products(*refs):
    pairs, (up_ref, down_ref) = refs[:-2], refs[-2:]
    count = len(pairs) // 4
    for start in range(0, up_ref.shape[0], TILE):
        tile = pl.ds(start, TILE)
        for k, out_ref in ((0, up_ref), (2, down_ref)):
            out_ref[tile, :] = sum(
                lax.dot_general(
                    pairs[4 * i + k][:, tile],
                    pairs[4 * i + k + 1][...],
                    (((0,), (0,)), ((), ())),
                    preferred_element_type=jnp.float32,
                )
                for i in range(count)
            )


def finish_products(*refs):
    up_sum, down_sum = refs[:2]
    up_ref, down_ref, buffer, sems = refs[-4:]
    pairs = refs[2:-4]
    count = len(pairs) // 4
    copies = []
    for start in range(0, up_ref.shape[0], TILE):
        tile = pl.ds(start, TILE)
        for k, sum_ref, out_ref in ((0, up_sum, up_ref), (2, down_sum, down_ref)):
            slot = len(copies) % buffer.shape[0]
            if len(copies) >= buffer.shape[0]:
                copies[-buffer.shape[0]].wait()
            buffer[slot] = sum_ref[tile, :] + sum(
                lax.dot_general(
                    pairs[4 * i + k][:, tile],
                    pairs[4 * i + k + 1][...],
                    (((0,), (0,)), ((), ())),
                    preferred_element_type=jnp.float32,
                )
                for i in range(count)
            )
            copies.append(
                pltpu.make_async_copy(buffer.at[slot], out_ref.at[tile], sems.at[slot])
            )
            copies[-1].start()
    for copy in copies[-buffer.shape[0] :]:
        copy.wait()


SMALL = pl.CostEstimate(flops=1, bytes_accessed=1, transcendentals=0)


def call(kernel, out_shape, smem, args, scratch=(), limit=16 * 2**20):
    return pl.pallas_call(
        kernel,
        out_shape=out_shape,
        in_specs=[pl.BlockSpec(memory_space=pltpu.SMEM)] * smem
        + [pl.BlockSpec(memory_space=pltpu.VMEM)] * (len(args) - smem),
        scratch_shapes=scratch,
        cost_estimate=SMALL,
        compiler_params=pltpu.CompilerParams(vmem_limit_bytes=limit),
    )(*args)


def send(x, routes):
    patches, grps, cores = (lax.axis_size(a) for a in ("patch", "grp", "col"))
    pairs = []
    for p in range(patches):
        for g in range(grps):
            for c, route in enumerate(routes):
                if route is not None:
                    to = ((p ^ route[0]) * grps + (g ^ route[1])) * cores + c
                    pairs.append(((p * grps + g) * cores + c, to))
    return lax.ppermute(x, ("patch", "grp", "col"), pairs)


def swap(x):
    return lax.ppermute(x, "col", [(0, 1), (1, 0)])


def hand_over(x):
    return lax.ppermute(x, "col", [(0, 1)])


def gather_plan(
    query_vectors,
    key_vectors,
    value_vectors,
    residual,
    neighbor_ids,
    neighbor_count,
    output_weight,
    norm_gain,
    up_weight,
    down_weight,
    cotangent,
):
    cores = lax.axis_size("col")
    grps = lax.axis_size("grp")
    rows, half = query_vectors.shape
    width = half * cores

    bf16 = jnp.bfloat16
    cot_parts = [cotangent] + others(cotangent, "col")
    residuals = [residual] + others(residual, "col")
    keys = [key_vectors] + others(key_vectors, "grp")
    values = [value_vectors] + others(value_vectors, "grp")
    weights = [output_weight] + others(output_weight, "col")
    cot = call(join_cores, jax.ShapeDtypeStruct((rows, width), bf16), 0, cot_parts)
    cot12 = send(cot, [(1, 0), (2, 0)])
    cot3x = send(cot, [(3, 0), (0, 1)])

    weights[0], residuals[0] = call(
        keep,
        [jax.ShapeDtypeStruct(a.shape, bf16) for a in (output_weight, residual)],
        0,
        [after(output_weight, cot), residual],
    )
    packed = call(
        functools.partial(attend, grps),
        jax.ShapeDtypeStruct((rows + GAIN_ROWS, half), bf16),
        2,
        [neighbor_ids, neighbor_count, norm_gain[None], after(query_vectors, weights[0])]
        + keys
        + values,
        [pltpu.VMEM((half // HEAD * grps, rows, rows), jnp.float32)],
        OWN_LIMIT,
    )
    stream, normed = call(
        functools.partial(project, cores),
        (
            jax.ShapeDtypeStruct((rows, half), jnp.float32),
            jax.ShapeDtypeStruct((rows, width), bf16),
        ),
        0,
        [packed] + others(packed, "col") + [after(weights[0], cot12)] + weights[1:] + residuals,
        [pltpu.VMEM((rows, width), jnp.float32), pltpu.VMEM((8, width), jnp.float32)],
    )

    def forward(by12, by3x):
        return send(by12, [(0, 1), (0, 1)]), send(by3x, [(0, 1), None])

    norm12 = send(normed, [(1, 0), (2, 0)])
    norm3x = send(normed, [(3, 0), (0, 1)])
    cot12, cot3x = after(cot12, normed), after(cot3x, normed)
    cot_over12, cot_over3 = forward(cot12, cot3x)
    cot_swap12, cot_swap3x = swap(cot12), swap(cot3x)
    cot_swap_over, cot_handed = swap(cot_over12), hand_over(cot_over3)
    norm12, norm3x, *_ = lax.optimization_barrier(
        (norm12, norm3x, cot_over12, cot_swap12)
    )
    over12, over3 = forward(norm12, norm3x)
    swap12, swap3x = swap(norm12), swap(norm3x)
    swap_over, handed = swap(over12), hand_over(over3)

    def pair(choices, blocks, shares=()):
        made = jax.ShapeDtypeStruct((2 * rows, width), bf16)
        return call(
            functools.partial(feed_forward, choices, bool(shares)),
            [made] * 4 + [jax.ShapeDtypeStruct((2 * rows, half), t) for t in shares],
            0,
            blocks + [up_weight, down_weight],
        )

    *group, mine, theirs = pair(
        (1, 2), [normed, swap3x, norm3x, cot, cot_swap3x, cot3x], (jnp.float32, bf16)
    )
    near = pair((1, 1), [norm12, swap12, cot12, cot_swap12])
    both = mine + swap(theirs).astype(jnp.float32)
    rest = lax.ppermute(both[rows:].astype(bf16), "grp", [(0, 1), (1, 0)])
    layer_out = (stream + both[:rows] + rest.astype(jnp.float32)).astype(bf16)
    panel = up_weight.shape[1]
    grads = (
        jax.ShapeDtypeStruct((width, panel), jnp.float32),
        jax.ShapeDtypeStruct((panel, width), jnp.float32),
    )
    sums = call(add_products, grads, 0, list(group) + list(near))
    over = pair((1, 1), [over12, swap_over, cot_over12, cot_swap_over])
    third = pair(
        (2, 2),
        [after(norm3x, sums[0]), swap3x, over3, handed]
        + [cot3x, cot_swap3x, cot_over3, cot_handed],
    )
    last = list(over) + list(third)
    up_grad, down_grad = pl.pallas_call(
        finish_products,
        out_shape=grads,
        in_specs=[pl.BlockSpec(memory_space=pltpu.VMEM)] * (2 + len(last)),
        out_specs=[pl.BlockSpec(memory_space=pl.ANY)] * 2,
        scratch_shapes=[
            pltpu.VMEM((4, TILE, width), jnp.float32),
            pltpu.SemaphoreType.DMA((4,)),
        ],
        cost_estimate=SMALL,
        compiler_params=pltpu.CompilerParams(vmem_limit_bytes=16 * 2**20),
    )(*sums, *last)
    return (layer_out, up_grad, down_grad)


def layer(*args):
    query_vectors, up_weight = args[0], args[8]
    patches, grps, cores = (lax.axis_size(a) for a in ("patch", "grp", "col"))
    tokens = query_vectors.shape[0] * grps * patches
    if (patches, grps, cores) == (4, 2, 2) and tokens <= 2 * up_weight.shape[1]:
        return gather_plan(*args)
    return shards(*args)


def solution(mesh):
    return jax.shard_map(
        layer,
        mesh=mesh,
        in_specs=(
            P(("parts", "patch", "grp"), "col"),
            P(("parts", "patch", "grp"), "col"),
            P(("parts", "patch", "grp"), "col"),
            P(("parts", "patch", "grp"), "col"),
            P(("parts", "patch", "grp"), None),
            P(("parts", "patch", "grp")),
            P("col", None),
            P("col"),
            P(None, ("grp", "col")),
            P(("grp", "col"), None),
            P(("parts", "patch", "grp"), "col"),
        ),
        out_specs=(
            P(("parts", "patch", "grp"), "col"),
            P("parts", ("grp", "col")),
            P(("parts", "grp", "col"), None),
        ),
        check_vma=False,
    )
```

```python
import functools

import jax
import jax.numpy as jnp
from jax import lax
from jax.experimental import pallas as pl
from jax.experimental.pallas import tpu as pltpu
from jax.sharding import PartitionSpec as P

HEAD = 64
D = 1024
BLK = 128


def spread_rows(part_rows):
    stacked = lax.all_gather(part_rows[None], ("grp", "col"), axis=0, tiled=True)
    grp_count = lax.axis_size("grp")
    col_count = lax.axis_size("col")
    row_count = part_rows.shape[0]
    half_width = part_rows.shape[1]
    arranged = stacked.reshape(grp_count, col_count, row_count, half_width).transpose(0, 2, 1, 3)
    return arranged.reshape(grp_count * row_count, col_count * half_width)


def shards(
    query_vectors,
    key_vectors,
    value_vectors,
    residual,
    neighbor_ids,
    neighbor_count,
    output_weight,
    norm_gain,
    up_weight,
    down_weight,
    cotangent,
):
    key_all, value_all = (
        lax.all_gather(key_vectors, "grp", axis=0, tiled=True),
        lax.all_gather(value_vectors, "grp", axis=0, tiled=True),
    )
    row_count = query_vectors.shape[0]
    local_heads = query_vectors.shape[1] // HEAD
    group_count = key_all.shape[0] // BLK
    column_ids = jnp.arange(group_count, dtype=jnp.int32)
    slot_ids = jnp.arange(neighbor_ids.shape[1], dtype=jnp.int32)
    listed = (neighbor_ids[:, :, None] == column_ids[None, None, :]) & (
        slot_ids[None, :, None] < neighbor_count[:, None, None]
    )
    allowed = jnp.any(listed, axis=1)
    token_mask = jnp.repeat(jnp.repeat(allowed, BLK, axis=0), BLK, axis=1)
    query_heads = query_vectors.reshape(row_count, local_heads, HEAD)
    key_heads = key_all.reshape(-1, local_heads, HEAD)
    value_heads = value_all.reshape(-1, local_heads, HEAD)
    scores = jnp.einsum(
        "qhd,khd->hqk", query_heads, key_heads, preferred_element_type=jnp.float32
    ) * HEAD ** (-0.5)
    scores = jnp.where(token_mask[None], scores, -1e30)
    largest = jnp.max(scores, axis=2, keepdims=True)
    weights = jnp.exp(scores - largest)
    probs = (weights / jnp.sum(weights, axis=2, keepdims=True)).astype(jnp.bfloat16)
    attended = jnp.einsum("hqk,khd->qhd", probs, value_heads, preferred_element_type=jnp.float32)
    attended = attended.astype(jnp.bfloat16).reshape(row_count, -1)
    projected = jnp.dot(attended, output_weight, preferred_element_type=jnp.float32)
    stream = residual.astype(jnp.float32) + lax.psum_scatter(
        projected.astype(jnp.bfloat16), "col", scatter_dimension=1, tiled=True
    ).astype(jnp.float32)
    first_sum, second_sum = lax.psum(
        (jnp.sum(stream, axis=1), jnp.sum(stream * stream, axis=1)), "col"
    )
    center = first_sum[:, None] / D
    shifted = stream - center
    spread_sq = second_sum[:, None] / D - center * center
    normed = (shifted * lax.rsqrt(spread_sq + 1e-05) * norm_gain[None, :]).astype(jnp.bfloat16)
    normed_rows = spread_rows(normed)
    pre = jnp.dot(normed_rows, up_weight, preferred_element_type=jnp.float32)
    hidden = jax.nn.gelu(pre).astype(jnp.bfloat16)
    grp_count = lax.axis_size("grp")
    col_count = lax.axis_size("col")
    partial_out = jnp.dot(hidden, down_weight, preferred_element_type=jnp.float32)
    half_width = partial_out.shape[1] // col_count
    partial_out = partial_out.reshape(grp_count, row_count, col_count, half_width).transpose(
        0, 2, 1, 3
    )
    partial_out = partial_out.reshape(grp_count * col_count * row_count, half_width)
    ff_out = lax.psum_scatter(
        partial_out.astype(jnp.bfloat16), ("grp", "col"), scatter_dimension=0, tiled=True
    ).astype(jnp.float32)
    layer_out = (stream + ff_out).astype(jnp.bfloat16)
    back_rows = spread_rows(cotangent)
    back_hidden = lax.dot_general(
        back_rows, down_weight, (((1,), (1,)), ((), ())), preferred_element_type=jnp.float32
    )
    _, gelu_back = jax.vjp(jax.nn.gelu, pre)
    back_pre = gelu_back(back_hidden)[0].astype(jnp.bfloat16)
    up_local = lax.dot_general(
        normed_rows, back_pre, (((0,), (0,)), ((), ())), preferred_element_type=jnp.float32
    )
    down_local = lax.dot_general(
        hidden, back_rows, (((0,), (0,)), ((), ())), preferred_element_type=jnp.float32
    )
    up_grad, down_grad = (
        lax.psum(up_local.astype(jnp.bfloat16), "patch").astype(jnp.float32),
        lax.psum(down_local.astype(jnp.bfloat16), "patch").astype(jnp.float32),
    )
    return (layer_out, up_grad, down_grad)


GAIN_ROWS = 16
TILE = 256
PANEL_TILE = 512
ROOT, CUBIC = 0.7978845608028654, 0.044715
OWN_LIMIT = 56 * 2**20


def shift(x, axis, k):
    n = lax.axis_size(axis)
    return lax.ppermute(x, axis, [(i, (i + k) % n) for i in range(n)])


def after(x, *others):
    return lax.optimization_barrier((x,) + others)[0]


def others(x, axis):
    n = lax.axis_size(axis)
    if n & (n - 1):
        return [shift(x, axis, k) for k in range(1, n)]
    return [lax.ppermute(x, axis, [(i, i ^ k) for i in range(n)]) for k in range(1, n)]


def member(axis, k):
    n = lax.axis_size(axis)
    me = lax.axis_index(axis)
    return (me - k + n) % n if n & (n - 1) else me ^ k


def one_head(query, lane, head):
    return jnp.where((lane < HEAD) == (head == 0), query, jnp.zeros_like(query))


def pair_scores(query, key):
    return lax.dot_general(
        query, key, (((1,), (1,)), ((), ())), preferred_element_type=jnp.float32
    ) * HEAD ** (-0.5)


def core_columns(j, half):
    return pl.ds(pl.multiple_of(member("col", j) * half, half), half)


def join_cores(*refs):
    parts, out_ref = refs[:-1], refs[-1]
    half = parts[0].shape[1]
    for j, part in enumerate(parts):
        out_ref[:, core_columns(j, half)] = part[...]


def keep(*refs):
    count = len(refs) // 2
    for source, target in zip(refs[:count], refs[count:]):
        target[...] = source[...]


def gelu_and_slope(pre):
    square = pre * pre
    curve = jnp.tanh(ROOT * (pre + CUBIC * (square * pre)))
    half = 0.5 * (1.0 + curve)
    slope = half + 0.5 * pre * (1.0 - curve * curve) * (ROOT * (1.0 + 3.0 * CUBIC * square))
    return pre * half, slope


def feed_forward(choices, share, *refs):
    count = 2 * sum(choices)
    blocks, (up_ref, down_ref), outs = refs[:count], refs[count : count + 2], refs[count + 2 :]
    rows_ref, back_pre_ref, hidden_ref, back_ref = outs[:4]
    first = lax.axis_index("col") == 0
    at = 0
    for out_ref in (rows_ref, back_ref):
        for i, width in enumerate(choices):
            rows = blocks[at].shape[0]
            block = blocks[at][...]
            if width == 2:
                block = jnp.where(first, block, blocks[at + 1][...])
            out_ref[pl.ds(i * rows, rows), :] = block
            at += width
    rows, back = rows_ref[...], back_ref[...]
    for start in range(0, up_ref.shape[1], PANEL_TILE):
        tile = pl.ds(start, PANEL_TILE)
        pre = jnp.dot(rows, up_ref[:, tile], preferred_element_type=jnp.float32)
        back_hidden = lax.dot_general(
            back, down_ref[tile, :], (((1,), (1,)), ((), ())), preferred_element_type=jnp.float32
        )
        hidden, slope = gelu_and_slope(pre)
        hidden_ref[:, tile] = hidden.astype(jnp.bfloat16)
        back_pre_ref[:, tile] = (back_hidden * slope).astype(jnp.bfloat16)
    if share:
        for j, out_ref in enumerate(outs[4:]):
            part = jnp.dot(
                hidden_ref[...],
                down_ref[:, core_columns(j, out_ref.shape[1])],
                preferred_element_type=jnp.float32,
            )
            out_ref[...] = part.astype(out_ref.dtype)


def attend(grps, ids_ref, count_ref, gain_ref, query_ref, *refs):
    seen = []
    for k in range(grps):
        listed = [
            (ids_ref[0, m] == member("grp", k)) & (m < count_ref[0]) for m in range(ids_ref.shape[1])
        ]
        seen.append(functools.reduce(jnp.logical_or, listed))
    keys, values, (out_ref, score_ref) = refs[:grps], refs[grps : 2 * grps], refs[2 * grps :]
    rows, half = query_ref.shape
    heads = half // HEAD
    lane = lax.broadcasted_iota(jnp.int32, (rows, 2 * HEAD), 1)
    for head in range(heads):
        cols = pl.ds(head // 2 * 2 * HEAD, 2 * HEAD)
        query = one_head(query_ref[:, cols], lane, head % 2)
        for k in range(grps):
            part = pair_scores(query, keys[k][:, cols])
            score_ref[head * grps + k] = jnp.where(seen[k], part, -1e30)
    for pair in range(heads // 2):
        cols = pl.ds(pair * 2 * HEAD, 2 * HEAD)
        value = [ref[:, cols] for ref in values]
        found = []
        for head in (2 * pair, 2 * pair + 1):
            scores = [score_ref[head * grps + k] for k in range(grps)]
            largest = scores[0]
            for part in scores[1:]:
                largest = jnp.maximum(largest, part)
            largest = jnp.max(largest, axis=1, keepdims=True)
            weights = [jnp.exp(part - largest) for part in scores]
            total = weights[0]
            for part in weights[1:]:
                total = total + part
            total = jnp.sum(total, axis=1, keepdims=True)
            result = 0.0
            for k in range(grps):
                probs = (weights[k] / total).astype(jnp.bfloat16)
                result = result + jnp.dot(probs, value[k], preferred_element_type=jnp.float32)
            found.append(result)
        out_ref[pl.ds(0, rows), cols] = jnp.where(lane < HEAD, found[0], found[1]).astype(
            jnp.bfloat16
        )
    gain = gain_ref[...]
    high = gain.astype(jnp.bfloat16).astype(jnp.float32)
    middle = (gain - high).astype(jnp.bfloat16).astype(jnp.float32)
    low = gain - high - middle
    row = lax.broadcasted_iota(jnp.int32, (GAIN_ROWS, half), 0)
    parts = jnp.where(
        row == 0, high, jnp.where(row == 1, middle, jnp.where(row == 2, low, 0.0))
    )
    out_ref[pl.ds(rows, GAIN_ROWS), :] = parts.astype(jnp.bfloat16)


def project(cores, *refs):
    packs, weights, residuals = refs[:cores], refs[cores : 2 * cores], refs[2 * cores : 3 * cores]
    stream_ref, normed_ref, full, gain = refs[3 * cores :]
    rows, half = stream_ref.shape
    width = half * cores
    full[...] = sum(
        jnp.dot(pack[pl.ds(0, rows), :], weight[...], preferred_element_type=jnp.float32)
        for pack, weight in zip(packs, weights)
    )
    for j, pack in enumerate(packs):
        cols = core_columns(j, half)
        part = full[:, cols] + residuals[j][...].astype(jnp.float32)
        full[:, cols] = part
        if j == 0:
            stream_ref[...] = part
        gains = pack[pl.ds(rows, GAIN_ROWS), :].astype(jnp.float32)
        gain[0:1, cols] = (gains[1:2] + gains[2:3]) + gains[0:1]
    stream = full[...]
    center = jnp.sum(stream, axis=1, keepdims=True) / width
    shifted = stream - center
    spread_sq = jnp.sum(shifted * shifted, axis=1, keepdims=True) / width
    normed_ref[...] = (shifted * lax.rsqrt(spread_sq + 1e-05) * gain[0:1, :]).astype(jnp.bfloat16)


def add_products(*refs):
    pairs, (up_ref, down_ref) = refs[:-2], refs[-2:]
    count = len(pairs) // 4
    for start in range(0, up_ref.shape[0], TILE):
        tile = pl.ds(start, TILE)
        for k, out_ref in ((0, up_ref), (2, down_ref)):
            out_ref[tile, :] = sum(
                lax.dot_general(
                    pairs[4 * i + k][:, tile],
                    pairs[4 * i + k + 1][...],
                    (((0,), (0,)), ((), ())),
                    preferred_element_type=jnp.float32,
                )
                for i in range(count)
            )


def finish_products(*refs):
    up_sum, down_sum, stream, own_part, other_part = refs[:5]
    layer_ref, up_ref, down_ref, layer, buffer, sems = refs[-6:]
    pairs = refs[5:-6]
    count = len(pairs) // 4
    total = stream[...] + own_part[...] + other_part[...].astype(jnp.float32)
    layer[...] = total.astype(jnp.bfloat16)
    layer_copy = pltpu.make_async_copy(layer, layer_ref, sems.at[buffer.shape[0]])
    layer_copy.start()
    copies = []
    for start in range(0, up_ref.shape[0], TILE):
        tile = pl.ds(start, TILE)
        for k, sum_ref, out_ref in ((0, up_sum, up_ref), (2, down_sum, down_ref)):
            slot = len(copies) % buffer.shape[0]
            if len(copies) >= buffer.shape[0]:
                copies[-buffer.shape[0]].wait()
            buffer[slot] = sum_ref[tile, :] + sum(
                lax.dot_general(
                    pairs[4 * i + k][:, tile],
                    pairs[4 * i + k + 1][...],
                    (((0,), (0,)), ((), ())),
                    preferred_element_type=jnp.float32,
                )
                for i in range(count)
            )
            copies.append(
                pltpu.make_async_copy(buffer.at[slot], out_ref.at[tile], sems.at[slot])
            )
            copies[-1].start()
    for copy in copies[-buffer.shape[0] :] + [layer_copy]:
        copy.wait()


SMALL = pl.CostEstimate(flops=1, bytes_accessed=1, transcendentals=0)
LARGE = pl.CostEstimate(flops=8 * 10**9, bytes_accessed=1, transcendentals=0)


def call(kernel, out_shape, smem, args, scratch=(), limit=16 * 2**20, cost=SMALL):
    return pl.pallas_call(
        kernel,
        out_shape=out_shape,
        in_specs=[pl.BlockSpec(memory_space=pltpu.SMEM)] * smem
        + [pl.BlockSpec(memory_space=pltpu.VMEM)] * (len(args) - smem),
        scratch_shapes=scratch,
        cost_estimate=cost,
        compiler_params=pltpu.CompilerParams(vmem_limit_bytes=limit),
    )(*args)


def send(x, routes):
    patches, grps, cores = (lax.axis_size(a) for a in ("patch", "grp", "col"))
    pairs = []
    for p in range(patches):
        for g in range(grps):
            for c, route in enumerate(routes):
                if route is not None:
                    to = ((p ^ route[0]) * grps + (g ^ route[1])) * cores + c
                    pairs.append(((p * grps + g) * cores + c, to))
    return lax.ppermute(x, ("patch", "grp", "col"), pairs)


def swap(x):
    return lax.ppermute(x, "col", [(0, 1), (1, 0)])


def hand_over(x):
    return lax.ppermute(x, "col", [(0, 1)])


def gather_plan(
    query_vectors,
    key_vectors,
    value_vectors,
    residual,
    neighbor_ids,
    neighbor_count,
    output_weight,
    norm_gain,
    up_weight,
    down_weight,
    cotangent,
):
    cores = lax.axis_size("col")
    grps = lax.axis_size("grp")
    rows, half = query_vectors.shape
    width = half * cores

    bf16 = jnp.bfloat16
    cot_parts = [cotangent] + others(cotangent, "col")
    residuals = [residual] + others(residual, "col")
    keys = [key_vectors] + others(key_vectors, "grp")
    values = [value_vectors] + others(value_vectors, "grp")
    weights = [output_weight] + others(output_weight, "col")
    cot = call(join_cores, jax.ShapeDtypeStruct((rows, width), bf16), 0, cot_parts)
    cot12 = send(cot, [(1, 0), (2, 0)])
    cot3x = send(cot, [(3, 0), (0, 1)])

    weights[0], residuals[0] = call(
        keep,
        [jax.ShapeDtypeStruct(a.shape, bf16) for a in (output_weight, residual)],
        0,
        [after(output_weight, cot), residual],
    )
    packed = call(
        functools.partial(attend, grps),
        jax.ShapeDtypeStruct((rows + GAIN_ROWS, half), bf16),
        2,
        [neighbor_ids, neighbor_count, norm_gain[None], after(query_vectors, weights[0])]
        + keys
        + values,
        [pltpu.VMEM((half // HEAD * grps, rows, rows), jnp.float32)],
        OWN_LIMIT,
    )
    stream, normed = call(
        functools.partial(project, cores),
        (
            jax.ShapeDtypeStruct((rows, half), jnp.float32),
            jax.ShapeDtypeStruct((rows, width), bf16),
        ),
        0,
        [packed] + others(packed, "col") + [after(weights[0], cot12)] + weights[1:] + residuals,
        [pltpu.VMEM((rows, width), jnp.float32), pltpu.VMEM((8, width), jnp.float32)],
    )

    norm12 = send(normed, [(1, 0), (2, 0)])
    norm3x = send(normed, [(3, 0), (0, 1)])
    first = lax.axis_index("col") == 0
    cot12, cot3x = after(cot12, normed), after(cot3x, normed)
    cot_over12 = send(cot12, [(0, 1), (0, 1)])
    cot_swap12, cot_swap3x = swap(cot12), swap(cot3x)
    norm12, norm3x = call(
        keep, [jax.ShapeDtypeStruct((rows, width), bf16)] * 2, 0, [norm12, norm3x], cost=LARGE
    )
    norm12, norm3x, *_ = lax.optimization_barrier(
        (norm12, norm3x, cot_over12, cot_swap12, cot_swap3x)
    )
    over12 = send(norm12, [(0, 1), (0, 1)])
    over3 = send(jnp.where(first, norm3x, cot_swap3x), [(0, 1), (0, 1)])
    swap12, swap3x = swap(norm12), swap(norm3x)

    def pair(choices, blocks, shares=()):
        made = jax.ShapeDtypeStruct((2 * rows, width), bf16)
        return call(
            functools.partial(feed_forward, choices, bool(shares)),
            [made] * 4 + [jax.ShapeDtypeStruct((2 * rows, half), t) for t in shares],
            0,
            blocks + [up_weight, down_weight],
        )

    *group, mine, theirs = pair(
        (1, 2), [normed, swap3x, norm3x, cot, cot_swap3x, cot3x], (jnp.float32, bf16)
    )
    near = pair((1, 1), [norm12, swap12, cot12, cot_swap12])
    both = mine + swap(theirs).astype(jnp.float32)
    rest = lax.ppermute(both[rows:].astype(bf16), "grp", [(0, 1), (1, 0)])
    panel = up_weight.shape[1]
    grads = (
        jax.ShapeDtypeStruct((width, panel), jnp.float32),
        jax.ShapeDtypeStruct((panel, width), jnp.float32),
    )
    sums = call(add_products, grads, 0, list(group) + list(near))
    over12, over3 = after(over12, sums[0]), after(over3, sums[0])
    swap_over, swap_over3 = swap(over12), swap(over3)
    over = pair((1, 1), [over12, swap_over, cot_over12, swap(cot_over12)])
    third = pair(
        (2, 2),
        [norm3x, swap3x, over3, swap_over3, cot3x, cot_swap3x, swap_over3, over3],
    )
    last = list(over) + list(third)
    parts = [stream, both[:rows], rest]
    return pl.pallas_call(
        finish_products,
        out_shape=(jax.ShapeDtypeStruct((rows, half), bf16),) + grads,
        in_specs=[pl.BlockSpec(memory_space=pltpu.VMEM)] * (5 + len(last)),
        out_specs=[pl.BlockSpec(memory_space=pl.ANY)] * 3,
        scratch_shapes=[
            pltpu.VMEM((rows, half), bf16),
            pltpu.VMEM((4, TILE, width), jnp.float32),
            pltpu.SemaphoreType.DMA((5,)),
        ],
        cost_estimate=SMALL,
        compiler_params=pltpu.CompilerParams(vmem_limit_bytes=16 * 2**20),
    )(*sums, *parts, *last)


def layer(*args):
    query_vectors, up_weight = args[0], args[8]
    patches, grps, cores = (lax.axis_size(a) for a in ("patch", "grp", "col"))
    tokens = query_vectors.shape[0] * grps * patches
    if (patches, grps, cores) == (4, 2, 2) and tokens <= 2 * up_weight.shape[1]:
        return gather_plan(*args)
    return shards(*args)


def solution(mesh):
    return jax.shard_map(
        layer,
        mesh=mesh,
        in_specs=(
            P(("parts", "patch", "grp"), "col"),
            P(("parts", "patch", "grp"), "col"),
            P(("parts", "patch", "grp"), "col"),
            P(("parts", "patch", "grp"), "col"),
            P(("parts", "patch", "grp"), None),
            P(("parts", "patch", "grp")),
            P("col", None),
            P("col"),
            P(None, ("grp", "col")),
            P(("grp", "col"), None),
            P(("parts", "patch", "grp"), "col"),
        ),
        out_specs=(
            P(("parts", "patch", "grp"), "col"),
            P("parts", ("grp", "col")),
            P(("parts", "grp", "col"), None),
        ),
        check_vma=False,
    )
```

```python
import functools

import jax
import jax.numpy as jnp
from jax import lax
from jax.experimental import pallas as pl
from jax.experimental.pallas import tpu as pltpu
from jax.sharding import PartitionSpec as P

HEAD = 64
D = 1024
BLK = 128


def spread_rows(part_rows):
    stacked = lax.all_gather(part_rows[None], ("grp", "col"), axis=0, tiled=True)
    grp_count = lax.axis_size("grp")
    col_count = lax.axis_size("col")
    row_count = part_rows.shape[0]
    half_width = part_rows.shape[1]
    arranged = stacked.reshape(grp_count, col_count, row_count, half_width).transpose(0, 2, 1, 3)
    return arranged.reshape(grp_count * row_count, col_count * half_width)


def shards(
    query_vectors,
    key_vectors,
    value_vectors,
    residual,
    neighbor_ids,
    neighbor_count,
    output_weight,
    norm_gain,
    up_weight,
    down_weight,
    cotangent,
):
    key_all, value_all = (
        lax.all_gather(key_vectors, "grp", axis=0, tiled=True),
        lax.all_gather(value_vectors, "grp", axis=0, tiled=True),
    )
    row_count = query_vectors.shape[0]
    local_heads = query_vectors.shape[1] // HEAD
    group_count = key_all.shape[0] // BLK
    column_ids = jnp.arange(group_count, dtype=jnp.int32)
    slot_ids = jnp.arange(neighbor_ids.shape[1], dtype=jnp.int32)
    listed = (neighbor_ids[:, :, None] == column_ids[None, None, :]) & (
        slot_ids[None, :, None] < neighbor_count[:, None, None]
    )
    allowed = jnp.any(listed, axis=1)
    token_mask = jnp.repeat(jnp.repeat(allowed, BLK, axis=0), BLK, axis=1)
    query_heads = query_vectors.reshape(row_count, local_heads, HEAD)
    key_heads = key_all.reshape(-1, local_heads, HEAD)
    value_heads = value_all.reshape(-1, local_heads, HEAD)
    scores = jnp.einsum(
        "qhd,khd->hqk", query_heads, key_heads, preferred_element_type=jnp.float32
    ) * HEAD ** (-0.5)
    scores = jnp.where(token_mask[None], scores, -1e30)
    largest = jnp.max(scores, axis=2, keepdims=True)
    weights = jnp.exp(scores - largest)
    probs = (weights / jnp.sum(weights, axis=2, keepdims=True)).astype(jnp.bfloat16)
    attended = jnp.einsum("hqk,khd->qhd", probs, value_heads, preferred_element_type=jnp.float32)
    attended = attended.astype(jnp.bfloat16).reshape(row_count, -1)
    projected = jnp.dot(attended, output_weight, preferred_element_type=jnp.float32)
    stream = residual.astype(jnp.float32) + lax.psum_scatter(
        projected.astype(jnp.bfloat16), "col", scatter_dimension=1, tiled=True
    ).astype(jnp.float32)
    first_sum, second_sum = lax.psum(
        (jnp.sum(stream, axis=1), jnp.sum(stream * stream, axis=1)), "col"
    )
    center = first_sum[:, None] / D
    shifted = stream - center
    spread_sq = second_sum[:, None] / D - center * center
    normed = (shifted * lax.rsqrt(spread_sq + 1e-05) * norm_gain[None, :]).astype(jnp.bfloat16)
    normed_rows = spread_rows(normed)
    pre = jnp.dot(normed_rows, up_weight, preferred_element_type=jnp.float32)
    hidden = jax.nn.gelu(pre).astype(jnp.bfloat16)
    grp_count = lax.axis_size("grp")
    col_count = lax.axis_size("col")
    partial_out = jnp.dot(hidden, down_weight, preferred_element_type=jnp.float32)
    half_width = partial_out.shape[1] // col_count
    partial_out = partial_out.reshape(grp_count, row_count, col_count, half_width).transpose(
        0, 2, 1, 3
    )
    partial_out = partial_out.reshape(grp_count * col_count * row_count, half_width)
    ff_out = lax.psum_scatter(
        partial_out.astype(jnp.bfloat16), ("grp", "col"), scatter_dimension=0, tiled=True
    ).astype(jnp.float32)
    layer_out = (stream + ff_out).astype(jnp.bfloat16)
    back_rows = spread_rows(cotangent)
    back_hidden = lax.dot_general(
        back_rows, down_weight, (((1,), (1,)), ((), ())), preferred_element_type=jnp.float32
    )
    _, gelu_back = jax.vjp(jax.nn.gelu, pre)
    back_pre = gelu_back(back_hidden)[0].astype(jnp.bfloat16)
    up_local = lax.dot_general(
        normed_rows, back_pre, (((0,), (0,)), ((), ())), preferred_element_type=jnp.float32
    )
    down_local = lax.dot_general(
        hidden, back_rows, (((0,), (0,)), ((), ())), preferred_element_type=jnp.float32
    )
    up_grad, down_grad = (
        lax.psum(up_local.astype(jnp.bfloat16), "patch").astype(jnp.float32),
        lax.psum(down_local.astype(jnp.bfloat16), "patch").astype(jnp.float32),
    )
    return (layer_out, up_grad, down_grad)


GAIN_ROWS = 16
TILE = 256
PANEL_TILE = 512
ROOT, CUBIC = 0.7978845608028654, 0.044715
OWN_LIMIT = 56 * 2**20


def shift(x, axis, k):
    n = lax.axis_size(axis)
    return lax.ppermute(x, axis, [(i, (i + k) % n) for i in range(n)])


def after(x, *others):
    return lax.optimization_barrier((x,) + others)[0]


def others(x, axis):
    n = lax.axis_size(axis)
    if n & (n - 1):
        return [shift(x, axis, k) for k in range(1, n)]
    return [lax.ppermute(x, axis, [(i, i ^ k) for i in range(n)]) for k in range(1, n)]


def member(axis, k):
    n = lax.axis_size(axis)
    me = lax.axis_index(axis)
    return (me - k + n) % n if n & (n - 1) else me ^ k


def one_head(query, lane, head):
    return jnp.where((lane < HEAD) == (head == 0), query, jnp.zeros_like(query))


def pair_scores(query, key):
    return lax.dot_general(
        query, key, (((1,), (1,)), ((), ())), preferred_element_type=jnp.float32
    ) * HEAD ** (-0.5)


def core_columns(j, half):
    return pl.ds(pl.multiple_of(member("col", j) * half, half), half)


def join_cores(*refs):
    parts, out_ref = refs[:-1], refs[-1]
    half = parts[0].shape[1]
    for j, part in enumerate(parts):
        out_ref[:, core_columns(j, half)] = part[...]


def keep(*refs):
    count = len(refs) // 2
    for source, target in zip(refs[:count], refs[count:]):
        target[...] = source[...]


def pick(first_ref, second_ref, out_ref):
    out_ref[...] = jnp.where(lax.axis_index("col") == 0, first_ref[...], second_ref[...])


def add_halves(mine_ref, other_ref, own_ref, sent_ref):
    rows = own_ref.shape[0]
    total = mine_ref[...] + other_ref[...].astype(jnp.float32)
    own_ref[...] = total[:rows]
    sent_ref[...] = total[rows:].astype(sent_ref.dtype)


def gelu_and_slope(pre):
    square = pre * pre
    curve = jnp.tanh(ROOT * (pre + CUBIC * (square * pre)))
    half = 0.5 * (1.0 + curve)
    slope = half + 0.5 * pre * (1.0 - curve * curve) * (ROOT * (1.0 + 3.0 * CUBIC * square))
    return pre * half, slope


def feed_forward(choices, share, *refs):
    count = 2 * sum(choices)
    blocks, (up_ref, down_ref), outs = refs[:count], refs[count : count + 2], refs[count + 2 :]
    rows_ref, back_pre_ref, hidden_ref, back_ref = outs[:4]
    first = lax.axis_index("col") == 0
    at = 0
    for out_ref in (rows_ref, back_ref):
        for i, width in enumerate(choices):
            rows = blocks[at].shape[0]
            block = blocks[at][...]
            if width == 2:
                block = jnp.where(first, block, blocks[at + 1][...])
            out_ref[pl.ds(i * rows, rows), :] = block
            at += width
    rows, back = rows_ref[...], back_ref[...]
    for start in range(0, up_ref.shape[1], PANEL_TILE):
        tile = pl.ds(start, PANEL_TILE)
        pre = jnp.dot(rows, up_ref[:, tile], preferred_element_type=jnp.float32)
        back_hidden = lax.dot_general(
            back, down_ref[tile, :], (((1,), (1,)), ((), ())), preferred_element_type=jnp.float32
        )
        hidden, slope = gelu_and_slope(pre)
        hidden_ref[:, tile] = hidden.astype(jnp.bfloat16)
        back_pre_ref[:, tile] = (back_hidden * slope).astype(jnp.bfloat16)
    if share:
        for j, out_ref in enumerate(outs[4:]):
            part = jnp.dot(
                hidden_ref[...],
                down_ref[:, core_columns(j, out_ref.shape[1])],
                preferred_element_type=jnp.float32,
            )
            out_ref[...] = part.astype(out_ref.dtype)


def attend(grps, ids_ref, count_ref, gain_ref, query_ref, *refs):
    seen = []
    for k in range(grps):
        listed = [
            (ids_ref[0, m] == member("grp", k)) & (m < count_ref[0]) for m in range(ids_ref.shape[1])
        ]
        seen.append(functools.reduce(jnp.logical_or, listed))
    keys, values, (out_ref, score_ref) = refs[:grps], refs[grps : 2 * grps], refs[2 * grps :]
    rows, half = query_ref.shape
    heads = half // HEAD
    lane = lax.broadcasted_iota(jnp.int32, (rows, 2 * HEAD), 1)
    for head in range(heads):
        cols = pl.ds(head // 2 * 2 * HEAD, 2 * HEAD)
        query = one_head(query_ref[:, cols], lane, head % 2)
        for k in range(grps):
            part = pair_scores(query, keys[k][:, cols])
            score_ref[head * grps + k] = jnp.where(seen[k], part, -1e30)
    for pair in range(heads // 2):
        cols = pl.ds(pair * 2 * HEAD, 2 * HEAD)
        value = [ref[:, cols] for ref in values]
        found = []
        for head in (2 * pair, 2 * pair + 1):
            scores = [score_ref[head * grps + k] for k in range(grps)]
            largest = scores[0]
            for part in scores[1:]:
                largest = jnp.maximum(largest, part)
            largest = jnp.max(largest, axis=1, keepdims=True)
            weights = [jnp.exp(part - largest) for part in scores]
            total = weights[0]
            for part in weights[1:]:
                total = total + part
            total = jnp.sum(total, axis=1, keepdims=True)
            result = 0.0
            for k in range(grps):
                probs = (weights[k] / total).astype(jnp.bfloat16)
                result = result + jnp.dot(probs, value[k], preferred_element_type=jnp.float32)
            found.append(result)
        out_ref[pl.ds(0, rows), cols] = jnp.where(lane < HEAD, found[0], found[1]).astype(
            jnp.bfloat16
        )
    gain = gain_ref[...]
    high = gain.astype(jnp.bfloat16).astype(jnp.float32)
    middle = (gain - high).astype(jnp.bfloat16).astype(jnp.float32)
    low = gain - high - middle
    row = lax.broadcasted_iota(jnp.int32, (GAIN_ROWS, half), 0)
    parts = jnp.where(
        row == 0, high, jnp.where(row == 1, middle, jnp.where(row == 2, low, 0.0))
    )
    out_ref[pl.ds(rows, GAIN_ROWS), :] = parts.astype(jnp.bfloat16)


def project(cores, *refs):
    packs, weights, residuals = refs[:cores], refs[cores : 2 * cores], refs[2 * cores : 3 * cores]
    stream_ref, normed_ref, full, gain = refs[3 * cores :]
    rows, half = stream_ref.shape
    width = half * cores
    full[...] = sum(
        jnp.dot(pack[pl.ds(0, rows), :], weight[...], preferred_element_type=jnp.float32)
        for pack, weight in zip(packs, weights)
    )
    for j, pack in enumerate(packs):
        cols = core_columns(j, half)
        part = full[:, cols] + residuals[j][...].astype(jnp.float32)
        full[:, cols] = part
        if j == 0:
            stream_ref[...] = part
        gains = pack[pl.ds(rows, GAIN_ROWS), :].astype(jnp.float32)
        gain[0:1, cols] = (gains[1:2] + gains[2:3]) + gains[0:1]
    stream = full[...]
    center = jnp.sum(stream, axis=1, keepdims=True) / width
    shifted = stream - center
    spread_sq = jnp.sum(shifted * shifted, axis=1, keepdims=True) / width
    normed_ref[...] = (shifted * lax.rsqrt(spread_sq + 1e-05) * gain[0:1, :]).astype(jnp.bfloat16)


def add_products(*refs):
    pairs, (up_ref, down_ref) = refs[:-2], refs[-2:]
    count = len(pairs) // 4
    for start in range(0, up_ref.shape[0], TILE):
        tile = pl.ds(start, TILE)
        for k, out_ref in ((0, up_ref), (2, down_ref)):
            out_ref[tile, :] = sum(
                lax.dot_general(
                    pairs[4 * i + k][:, tile],
                    pairs[4 * i + k + 1][...],
                    (((0,), (0,)), ((), ())),
                    preferred_element_type=jnp.float32,
                )
                for i in range(count)
            )


def finish_products(*refs):
    up_sum, down_sum, stream, own_part, other_part = refs[:5]
    layer_ref, up_ref, down_ref, layer, buffer, sems = refs[-6:]
    pairs = refs[5:-6]
    count = len(pairs) // 4
    total = stream[...] + own_part[...] + other_part[...].astype(jnp.float32)
    layer[...] = total.astype(jnp.bfloat16)
    layer_copy = pltpu.make_async_copy(layer, layer_ref, sems.at[buffer.shape[0]])
    layer_copy.start()
    copies = []
    for start in range(0, up_ref.shape[0], TILE):
        tile = pl.ds(start, TILE)
        for k, sum_ref, out_ref in ((0, up_sum, up_ref), (2, down_sum, down_ref)):
            slot = len(copies) % buffer.shape[0]
            if len(copies) >= buffer.shape[0]:
                copies[-buffer.shape[0]].wait()
            buffer[slot] = sum_ref[tile, :] + sum(
                lax.dot_general(
                    pairs[4 * i + k][:, tile],
                    pairs[4 * i + k + 1][...],
                    (((0,), (0,)), ((), ())),
                    preferred_element_type=jnp.float32,
                )
                for i in range(count)
            )
            copies.append(
                pltpu.make_async_copy(buffer.at[slot], out_ref.at[tile], sems.at[slot])
            )
            copies[-1].start()
    for copy in copies[-buffer.shape[0] :] + [layer_copy]:
        copy.wait()


SMALL = pl.CostEstimate(flops=1, bytes_accessed=1, transcendentals=0)
LARGE = pl.CostEstimate(flops=10**8, bytes_accessed=1, transcendentals=0)


def call(kernel, out_shape, smem, args, scratch=(), limit=16 * 2**20, cost=SMALL):
    return pl.pallas_call(
        kernel,
        out_shape=out_shape,
        in_specs=[pl.BlockSpec(memory_space=pltpu.SMEM)] * smem
        + [pl.BlockSpec(memory_space=pltpu.VMEM)] * (len(args) - smem),
        scratch_shapes=scratch,
        cost_estimate=cost,
        compiler_params=pltpu.CompilerParams(vmem_limit_bytes=limit),
    )(*args)


def send(x, routes):
    patches, grps, cores = (lax.axis_size(a) for a in ("patch", "grp", "col"))
    pairs = []
    for p in range(patches):
        for g in range(grps):
            for c, route in enumerate(routes):
                if route is not None:
                    to = ((p ^ route[0]) * grps + (g ^ route[1])) * cores + c
                    pairs.append(((p * grps + g) * cores + c, to))
    return lax.ppermute(x, ("patch", "grp", "col"), pairs)


def swap(x):
    return lax.ppermute(x, "col", [(0, 1), (1, 0)])


def hand_over(x):
    return lax.ppermute(x, "col", [(0, 1)])


def gather_plan(
    query_vectors,
    key_vectors,
    value_vectors,
    residual,
    neighbor_ids,
    neighbor_count,
    output_weight,
    norm_gain,
    up_weight,
    down_weight,
    cotangent,
):
    cores = lax.axis_size("col")
    grps = lax.axis_size("grp")
    rows, half = query_vectors.shape
    width = half * cores

    bf16 = jnp.bfloat16
    cot_parts = [cotangent] + others(cotangent, "col")
    residuals = [residual] + others(residual, "col")
    keys = [key_vectors] + others(key_vectors, "grp")
    values = [value_vectors] + others(value_vectors, "grp")
    weights = [output_weight] + others(output_weight, "col")
    cot = call(join_cores, jax.ShapeDtypeStruct((rows, width), bf16), 0, cot_parts)
    cot12 = send(cot, [(1, 0), (2, 0)])
    cot3x = send(cot, [(3, 0), (0, 1)])

    weights[0], residuals[0] = call(
        keep,
        [jax.ShapeDtypeStruct(a.shape, bf16) for a in (output_weight, residual)],
        0,
        [after(output_weight, cot), residual],
    )
    packed = call(
        functools.partial(attend, grps),
        jax.ShapeDtypeStruct((rows + GAIN_ROWS, half), bf16),
        2,
        [neighbor_ids, neighbor_count, norm_gain[None], after(query_vectors, weights[0])]
        + keys
        + values,
        [pltpu.VMEM((half // HEAD * grps, rows, rows), jnp.float32)],
        OWN_LIMIT,
    )
    stream, normed = call(
        functools.partial(project, cores),
        (
            jax.ShapeDtypeStruct((rows, half), jnp.float32),
            jax.ShapeDtypeStruct((rows, width), bf16),
        ),
        0,
        [packed] + others(packed, "col") + [after(weights[0], cot12)] + weights[1:] + residuals,
        [pltpu.VMEM((rows, width), jnp.float32), pltpu.VMEM((8, width), jnp.float32)],
    )

    norm12 = send(normed, [(1, 0), (2, 0)])
    norm3x = send(normed, [(3, 0), (0, 1)])
    cot12, cot3x = after(cot12, normed), after(cot3x, normed)
    cot_over12 = send(cot12, [(0, 1), (0, 1)])
    cot_swap12, cot_swap3x = swap(cot12), swap(cot3x)
    norm12, norm3x = call(
        keep, [jax.ShapeDtypeStruct((rows, width), bf16)] * 2, 0, [norm12, norm3x], cost=LARGE
    )
    norm12, norm3x, *_ = lax.optimization_barrier(
        (norm12, norm3x, cot_over12, cot_swap12, cot_swap3x)
    )
    over12 = send(norm12, [(0, 1), (0, 1)])
    third_block = call(
        pick, jax.ShapeDtypeStruct((rows, width), bf16), 0, [norm3x, cot_swap3x]
    )
    over3 = send(third_block, [(0, 1), (0, 1)])
    swap12, swap3x = swap(norm12), swap(norm3x)

    def pair(choices, blocks, shares=()):
        made = jax.ShapeDtypeStruct((2 * rows, width), bf16)
        return call(
            functools.partial(feed_forward, choices, bool(shares)),
            [made] * 4 + [jax.ShapeDtypeStruct((2 * rows, half), t) for t in shares],
            0,
            blocks + [up_weight, down_weight],
        )

    *group, mine, theirs = pair(
        (1, 2), [normed, swap3x, norm3x, cot, cot_swap3x, cot3x], (jnp.float32, bf16)
    )
    near = pair((1, 1), [norm12, swap12, cot12, cot_swap12])
    own_part, sent = call(
        add_halves,
        (
            jax.ShapeDtypeStruct((rows, half), jnp.float32),
            jax.ShapeDtypeStruct((rows, half), bf16),
        ),
        0,
        [mine, swap(theirs)],
    )
    rest = lax.ppermute(sent, "grp", [(0, 1), (1, 0)])
    panel = up_weight.shape[1]
    grads = (
        jax.ShapeDtypeStruct((width, panel), jnp.float32),
        jax.ShapeDtypeStruct((panel, width), jnp.float32),
    )
    sums = call(add_products, grads, 0, list(group) + list(near))
    over12, over3 = after(over12, sums[0]), after(over3, sums[0])
    swap_over, swap_over3 = swap(over12), swap(over3)
    over = pair((1, 1), [over12, swap_over, cot_over12, swap(cot_over12)])
    third = pair(
        (2, 2),
        [norm3x, swap3x, over3, swap_over3, cot3x, cot_swap3x, swap_over3, over3],
    )
    last = list(over) + list(third)
    parts = [stream, own_part, rest]
    return pl.pallas_call(
        finish_products,
        out_shape=(jax.ShapeDtypeStruct((rows, half), bf16),) + grads,
        in_specs=[pl.BlockSpec(memory_space=pltpu.VMEM)] * (5 + len(last)),
        out_specs=[pl.BlockSpec(memory_space=pl.ANY)] * 3,
        scratch_shapes=[
            pltpu.VMEM((rows, half), bf16),
            pltpu.VMEM((4, TILE, width), jnp.float32),
            pltpu.SemaphoreType.DMA((5,)),
        ],
        cost_estimate=SMALL,
        compiler_params=pltpu.CompilerParams(vmem_limit_bytes=16 * 2**20),
    )(*sums, *parts, *last)


def layer(*args):
    query_vectors, up_weight = args[0], args[8]
    patches, grps, cores = (lax.axis_size(a) for a in ("patch", "grp", "col"))
    tokens = query_vectors.shape[0] * grps * patches
    if (patches, grps, cores) == (4, 2, 2) and tokens <= 2 * up_weight.shape[1]:
        return gather_plan(*args)
    return shards(*args)


def solution(mesh):
    return jax.shard_map(
        layer,
        mesh=mesh,
        in_specs=(
            P(("parts", "patch", "grp"), "col"),
            P(("parts", "patch", "grp"), "col"),
            P(("parts", "patch", "grp"), "col"),
            P(("parts", "patch", "grp"), "col"),
            P(("parts", "patch", "grp"), None),
            P(("parts", "patch", "grp")),
            P("col", None),
            P("col"),
            P(None, ("grp", "col")),
            P(("grp", "col"), None),
            P(("parts", "patch", "grp"), "col"),
        ),
        out_specs=(
            P(("parts", "patch", "grp"), "col"),
            P("parts", ("grp", "col")),
            P(("parts", "grp", "col"), None),
        ),
        check_vma=False,
    )
```

```python
import functools

import jax
import jax.numpy as jnp
from jax import lax
from jax.experimental import pallas as pl
from jax.experimental.pallas import tpu as pltpu
from jax.sharding import PartitionSpec as P

HEAD = 64
D = 1024
BLK = 128


def spread_rows(part_rows):
    stacked = lax.all_gather(part_rows[None], ("grp", "col"), axis=0, tiled=True)
    grp_count = lax.axis_size("grp")
    col_count = lax.axis_size("col")
    row_count = part_rows.shape[0]
    half_width = part_rows.shape[1]
    arranged = stacked.reshape(grp_count, col_count, row_count, half_width).transpose(0, 2, 1, 3)
    return arranged.reshape(grp_count * row_count, col_count * half_width)


def shards(
    query_vectors,
    key_vectors,
    value_vectors,
    residual,
    neighbor_ids,
    neighbor_count,
    output_weight,
    norm_gain,
    up_weight,
    down_weight,
    cotangent,
):
    key_all, value_all = (
        lax.all_gather(key_vectors, "grp", axis=0, tiled=True),
        lax.all_gather(value_vectors, "grp", axis=0, tiled=True),
    )
    row_count = query_vectors.shape[0]
    local_heads = query_vectors.shape[1] // HEAD
    group_count = key_all.shape[0] // BLK
    column_ids = jnp.arange(group_count, dtype=jnp.int32)
    slot_ids = jnp.arange(neighbor_ids.shape[1], dtype=jnp.int32)
    listed = (neighbor_ids[:, :, None] == column_ids[None, None, :]) & (
        slot_ids[None, :, None] < neighbor_count[:, None, None]
    )
    allowed = jnp.any(listed, axis=1)
    token_mask = jnp.repeat(jnp.repeat(allowed, BLK, axis=0), BLK, axis=1)
    query_heads = query_vectors.reshape(row_count, local_heads, HEAD)
    key_heads = key_all.reshape(-1, local_heads, HEAD)
    value_heads = value_all.reshape(-1, local_heads, HEAD)
    scores = jnp.einsum(
        "qhd,khd->hqk", query_heads, key_heads, preferred_element_type=jnp.float32
    ) * HEAD ** (-0.5)
    scores = jnp.where(token_mask[None], scores, -1e30)
    largest = jnp.max(scores, axis=2, keepdims=True)
    weights = jnp.exp(scores - largest)
    probs = (weights / jnp.sum(weights, axis=2, keepdims=True)).astype(jnp.bfloat16)
    attended = jnp.einsum("hqk,khd->qhd", probs, value_heads, preferred_element_type=jnp.float32)
    attended = attended.astype(jnp.bfloat16).reshape(row_count, -1)
    projected = jnp.dot(attended, output_weight, preferred_element_type=jnp.float32)
    stream = residual.astype(jnp.float32) + lax.psum_scatter(
        projected.astype(jnp.bfloat16), "col", scatter_dimension=1, tiled=True
    ).astype(jnp.float32)
    first_sum, second_sum = lax.psum(
        (jnp.sum(stream, axis=1), jnp.sum(stream * stream, axis=1)), "col"
    )
    center = first_sum[:, None] / D
    shifted = stream - center
    spread_sq = second_sum[:, None] / D - center * center
    normed = (shifted * lax.rsqrt(spread_sq + 1e-05) * norm_gain[None, :]).astype(jnp.bfloat16)
    normed_rows = spread_rows(normed)
    pre = jnp.dot(normed_rows, up_weight, preferred_element_type=jnp.float32)
    hidden = jax.nn.gelu(pre).astype(jnp.bfloat16)
    grp_count = lax.axis_size("grp")
    col_count = lax.axis_size("col")
    partial_out = jnp.dot(hidden, down_weight, preferred_element_type=jnp.float32)
    half_width = partial_out.shape[1] // col_count
    partial_out = partial_out.reshape(grp_count, row_count, col_count, half_width).transpose(
        0, 2, 1, 3
    )
    partial_out = partial_out.reshape(grp_count * col_count * row_count, half_width)
    ff_out = lax.psum_scatter(
        partial_out.astype(jnp.bfloat16), ("grp", "col"), scatter_dimension=0, tiled=True
    ).astype(jnp.float32)
    layer_out = (stream + ff_out).astype(jnp.bfloat16)
    back_rows = spread_rows(cotangent)
    back_hidden = lax.dot_general(
        back_rows, down_weight, (((1,), (1,)), ((), ())), preferred_element_type=jnp.float32
    )
    _, gelu_back = jax.vjp(jax.nn.gelu, pre)
    back_pre = gelu_back(back_hidden)[0].astype(jnp.bfloat16)
    up_local = lax.dot_general(
        normed_rows, back_pre, (((0,), (0,)), ((), ())), preferred_element_type=jnp.float32
    )
    down_local = lax.dot_general(
        hidden, back_rows, (((0,), (0,)), ((), ())), preferred_element_type=jnp.float32
    )
    up_grad, down_grad = (
        lax.psum(up_local.astype(jnp.bfloat16), "patch").astype(jnp.float32),
        lax.psum(down_local.astype(jnp.bfloat16), "patch").astype(jnp.float32),
    )
    return (layer_out, up_grad, down_grad)


GAIN_ROWS = 16
TILE = 256
PANEL_TILE = 512
ROOT, CUBIC = 0.7978845608028654, 0.044715
OWN_LIMIT = 56 * 2**20


def shift(x, axis, k):
    n = lax.axis_size(axis)
    return lax.ppermute(x, axis, [(i, (i + k) % n) for i in range(n)])


def after(x, *others):
    return lax.optimization_barrier((x,) + others)[0]


def others(x, axis):
    n = lax.axis_size(axis)
    if n & (n - 1):
        return [shift(x, axis, k) for k in range(1, n)]
    return [lax.ppermute(x, axis, [(i, i ^ k) for i in range(n)]) for k in range(1, n)]


def member(axis, k):
    n = lax.axis_size(axis)
    me = lax.axis_index(axis)
    return (me - k + n) % n if n & (n - 1) else me ^ k


def one_head(query, lane, head):
    return jnp.where((lane < HEAD) == (head == 0), query, jnp.zeros_like(query))


def pair_scores(query, key):
    return lax.dot_general(
        query, key, (((1,), (1,)), ((), ())), preferred_element_type=jnp.float32
    ) * HEAD ** (-0.5)


def core_columns(j, half):
    return pl.ds(pl.multiple_of(member("col", j) * half, half), half)


def join_cores(*refs):
    parts, out_ref = refs[:-1], refs[-1]
    half = parts[0].shape[1]
    for j, part in enumerate(parts):
        out_ref[:, core_columns(j, half)] = part[...]


def keep(*refs):
    count = len(refs) // 2
    for source, target in zip(refs[:count], refs[count:]):
        target[...] = source[...]


def keep_and_pick(one_ref, two_ref, other_ref, kept_one_ref, kept_two_ref, picked_ref):
    kept_one_ref[...] = one_ref[...]
    kept_two_ref[...] = two_ref[...]
    picked_ref[...] = jnp.where(lax.axis_index("col") == 0, other_ref[...], one_ref[...])


def add_halves(mine_ref, other_ref, own_ref, sent_ref):
    rows = own_ref.shape[0]
    total = mine_ref[...] + other_ref[...].astype(jnp.float32)
    own_ref[...] = total[:rows]
    sent_ref[...] = total[rows:].astype(sent_ref.dtype)


def gelu_and_slope(pre):
    square = pre * pre
    curve = jnp.tanh(ROOT * (pre + CUBIC * (square * pre)))
    half = 0.5 * (1.0 + curve)
    slope = half + 0.5 * pre * (1.0 - curve * curve) * (ROOT * (1.0 + 3.0 * CUBIC * square))
    return pre * half, slope


def feed_forward(choices, share, *refs):
    count = 2 * sum(choices)
    blocks, (up_ref, down_ref), outs = refs[:count], refs[count : count + 2], refs[count + 2 :]
    rows_ref, back_pre_ref, hidden_ref, back_ref = outs[:4]
    first = lax.axis_index("col") == 0
    at = 0
    for out_ref in (rows_ref, back_ref):
        for i, width in enumerate(choices):
            rows = blocks[at].shape[0]
            block = blocks[at][...]
            if width == 2:
                block = jnp.where(first, block, blocks[at + 1][...])
            out_ref[pl.ds(i * rows, rows), :] = block
            at += width
    rows, back = rows_ref[...], back_ref[...]
    for start in range(0, up_ref.shape[1], PANEL_TILE):
        tile = pl.ds(start, PANEL_TILE)
        pre = jnp.dot(rows, up_ref[:, tile], preferred_element_type=jnp.float32)
        back_hidden = lax.dot_general(
            back, down_ref[tile, :], (((1,), (1,)), ((), ())), preferred_element_type=jnp.float32
        )
        hidden, slope = gelu_and_slope(pre)
        hidden_ref[:, tile] = hidden.astype(jnp.bfloat16)
        back_pre_ref[:, tile] = (back_hidden * slope).astype(jnp.bfloat16)
    if share:
        for j, out_ref in enumerate(outs[4:]):
            part = jnp.dot(
                hidden_ref[...],
                down_ref[:, core_columns(j, out_ref.shape[1])],
                preferred_element_type=jnp.float32,
            )
            out_ref[...] = part.astype(out_ref.dtype)


def attend(grps, ids_ref, count_ref, gain_ref, query_ref, *refs):
    seen = []
    for k in range(grps):
        listed = [
            (ids_ref[0, m] == member("grp", k)) & (m < count_ref[0]) for m in range(ids_ref.shape[1])
        ]
        seen.append(functools.reduce(jnp.logical_or, listed))
    keys, values, (out_ref, score_ref) = refs[:grps], refs[grps : 2 * grps], refs[2 * grps :]
    rows, half = query_ref.shape
    heads = half // HEAD
    lane = lax.broadcasted_iota(jnp.int32, (rows, 2 * HEAD), 1)
    for head in range(heads):
        cols = pl.ds(head // 2 * 2 * HEAD, 2 * HEAD)
        query = one_head(query_ref[:, cols], lane, head % 2)
        for k in range(grps):
            part = pair_scores(query, keys[k][:, cols])
            score_ref[head * grps + k] = jnp.where(seen[k], part, -1e30)
    for pair in range(heads // 2):
        cols = pl.ds(pair * 2 * HEAD, 2 * HEAD)
        value = [ref[:, cols] for ref in values]
        found = []
        for head in (2 * pair, 2 * pair + 1):
            scores = [score_ref[head * grps + k] for k in range(grps)]
            largest = scores[0]
            for part in scores[1:]:
                largest = jnp.maximum(largest, part)
            largest = jnp.max(largest, axis=1, keepdims=True)
            weights = [jnp.exp(part - largest) for part in scores]
            total = weights[0]
            for part in weights[1:]:
                total = total + part
            total = jnp.sum(total, axis=1, keepdims=True)
            result = 0.0
            for k in range(grps):
                probs = (weights[k] / total).astype(jnp.bfloat16)
                result = result + jnp.dot(probs, value[k], preferred_element_type=jnp.float32)
            found.append(result)
        out_ref[pl.ds(0, rows), cols] = jnp.where(lane < HEAD, found[0], found[1]).astype(
            jnp.bfloat16
        )
    gain = gain_ref[...]
    high = gain.astype(jnp.bfloat16).astype(jnp.float32)
    middle = (gain - high).astype(jnp.bfloat16).astype(jnp.float32)
    low = gain - high - middle
    row = lax.broadcasted_iota(jnp.int32, (GAIN_ROWS, half), 0)
    parts = jnp.where(
        row == 0, high, jnp.where(row == 1, middle, jnp.where(row == 2, low, 0.0))
    )
    out_ref[pl.ds(rows, GAIN_ROWS), :] = parts.astype(jnp.bfloat16)


def project(cores, *refs):
    packs, weights, residuals = refs[:cores], refs[cores : 2 * cores], refs[2 * cores : 3 * cores]
    stream_ref, normed_ref, full, gain = refs[3 * cores :]
    rows, half = stream_ref.shape
    width = half * cores
    full[...] = sum(
        jnp.dot(pack[pl.ds(0, rows), :], weight[...], preferred_element_type=jnp.float32)
        for pack, weight in zip(packs, weights)
    )
    for j, pack in enumerate(packs):
        cols = core_columns(j, half)
        part = full[:, cols] + residuals[j][...].astype(jnp.float32)
        full[:, cols] = part
        if j == 0:
            stream_ref[...] = part
        gains = pack[pl.ds(rows, GAIN_ROWS), :].astype(jnp.float32)
        gain[0:1, cols] = (gains[1:2] + gains[2:3]) + gains[0:1]
    stream = full[...]
    center = jnp.sum(stream, axis=1, keepdims=True) / width
    shifted = stream - center
    spread_sq = jnp.sum(shifted * shifted, axis=1, keepdims=True) / width
    normed_ref[...] = (shifted * lax.rsqrt(spread_sq + 1e-05) * gain[0:1, :]).astype(jnp.bfloat16)


def add_products(*refs):
    pairs, (up_ref, down_ref) = refs[:-2], refs[-2:]
    count = len(pairs) // 4
    for start in range(0, up_ref.shape[0], TILE):
        tile = pl.ds(start, TILE)
        for k, out_ref in ((0, up_ref), (2, down_ref)):
            out_ref[tile, :] = sum(
                lax.dot_general(
                    pairs[4 * i + k][:, tile],
                    pairs[4 * i + k + 1][...],
                    (((0,), (0,)), ((), ())),
                    preferred_element_type=jnp.float32,
                )
                for i in range(count)
            )


def finish_products(*refs):
    up_sum, down_sum, stream, own_part, other_part = refs[:5]
    layer_ref, up_ref, down_ref, layer, buffer, sems = refs[-6:]
    pairs = refs[5:-6]
    count = len(pairs) // 4
    total = stream[...] + own_part[...] + other_part[...].astype(jnp.float32)
    layer[...] = total.astype(jnp.bfloat16)
    layer_copy = pltpu.make_async_copy(layer, layer_ref, sems.at[buffer.shape[0]])
    layer_copy.start()
    copies = []
    for start in range(0, up_ref.shape[0], TILE):
        tile = pl.ds(start, TILE)
        for k, sum_ref, out_ref in ((0, up_sum, up_ref), (2, down_sum, down_ref)):
            slot = len(copies) % buffer.shape[0]
            if len(copies) >= buffer.shape[0]:
                copies[-buffer.shape[0]].wait()
            buffer[slot] = sum_ref[tile, :] + sum(
                lax.dot_general(
                    pairs[4 * i + k][:, tile],
                    pairs[4 * i + k + 1][...],
                    (((0,), (0,)), ((), ())),
                    preferred_element_type=jnp.float32,
                )
                for i in range(count)
            )
            copies.append(
                pltpu.make_async_copy(buffer.at[slot], out_ref.at[tile], sems.at[slot])
            )
            copies[-1].start()
    for copy in copies[-buffer.shape[0] :] + [layer_copy]:
        copy.wait()


SMALL = pl.CostEstimate(flops=1, bytes_accessed=1, transcendentals=0)
LARGE = pl.CostEstimate(flops=10**8, bytes_accessed=1, transcendentals=0)


def call(kernel, out_shape, smem, args, scratch=(), limit=16 * 2**20, cost=SMALL):
    return pl.pallas_call(
        kernel,
        out_shape=out_shape,
        in_specs=[pl.BlockSpec(memory_space=pltpu.SMEM)] * smem
        + [pl.BlockSpec(memory_space=pltpu.VMEM)] * (len(args) - smem),
        scratch_shapes=scratch,
        cost_estimate=cost,
        compiler_params=pltpu.CompilerParams(vmem_limit_bytes=limit),
    )(*args)


def send(x, routes):
    patches, grps, cores = (lax.axis_size(a) for a in ("patch", "grp", "col"))
    pairs = []
    for p in range(patches):
        for g in range(grps):
            for c, route in enumerate(routes):
                if route is not None:
                    to = ((p ^ route[0]) * grps + (g ^ route[1])) * cores + c
                    pairs.append(((p * grps + g) * cores + c, to))
    return lax.ppermute(x, ("patch", "grp", "col"), pairs)


def swap(x):
    return lax.ppermute(x, "col", [(0, 1), (1, 0)])


def gather_plan(
    query_vectors,
    key_vectors,
    value_vectors,
    residual,
    neighbor_ids,
    neighbor_count,
    output_weight,
    norm_gain,
    up_weight,
    down_weight,
    cotangent,
):
    cores = lax.axis_size("col")
    grps = lax.axis_size("grp")
    rows, half = query_vectors.shape
    width = half * cores

    bf16 = jnp.bfloat16
    cot_parts = [cotangent] + others(cotangent, "col")
    residuals = [residual] + others(residual, "col")
    keys = [key_vectors] + others(key_vectors, "grp")
    values = [value_vectors] + others(value_vectors, "grp")
    weights = [output_weight] + others(output_weight, "col")
    cot = call(join_cores, jax.ShapeDtypeStruct((rows, width), bf16), 0, cot_parts)
    cot12 = send(cot, [(1, 0), (2, 0)])
    cot3x = send(cot, [(3, 0), (0, 1)])

    weights[0], residuals[0] = call(
        keep,
        [jax.ShapeDtypeStruct(a.shape, bf16) for a in (output_weight, residual)],
        0,
        [after(output_weight, cot), residual],
    )
    packed = call(
        functools.partial(attend, grps),
        jax.ShapeDtypeStruct((rows + GAIN_ROWS, half), bf16),
        2,
        [neighbor_ids, neighbor_count, norm_gain[None], after(query_vectors, weights[0])]
        + keys
        + values,
        [pltpu.VMEM((half // HEAD * grps, rows, rows), jnp.float32)],
        OWN_LIMIT,
    )
    stream, normed = call(
        functools.partial(project, cores),
        (
            jax.ShapeDtypeStruct((rows, half), jnp.float32),
            jax.ShapeDtypeStruct((rows, width), bf16),
        ),
        0,
        [packed] + others(packed, "col") + [after(weights[0], cot12)] + weights[1:] + residuals,
        [pltpu.VMEM((rows, width), jnp.float32), pltpu.VMEM((8, width), jnp.float32)],
    )

    norm12 = send(normed, [(1, 0), (2, 0)])
    norm3x = send(normed, [(3, 0), (0, 1)])
    cot12, cot3x = after(cot12, normed), after(cot3x, normed)
    cot_over12 = send(cot12, [(0, 1), (0, 1)])
    cot_swap12, cot_swap3x = swap(cot12), swap(cot3x)
    norm12, norm3x, picked = call(
        keep_and_pick,
        [jax.ShapeDtypeStruct((rows, width), bf16)] * 3,
        0,
        [norm12, norm3x, cot3x],
        cost=LARGE,
    )
    norm12, norm3x, picked, *_ = lax.optimization_barrier(
        (norm12, norm3x, picked, cot_over12, cot_swap12)
    )
    far = send(norm3x, [(0, 1), (1, 0)])
    mixed = send(picked, [(0, 1), (0, 1)])
    swap12, swap3x = swap(norm12), swap(norm3x)

    def pair(choices, blocks, shares=()):
        made = jax.ShapeDtypeStruct((2 * rows, width), bf16)
        return call(
            functools.partial(feed_forward, choices, bool(shares)),
            [made] * 4 + [jax.ShapeDtypeStruct((2 * rows, half), t) for t in shares],
            0,
            blocks + [up_weight, down_weight],
        )

    *group, mine, theirs = pair(
        (1, 2), [normed, swap3x, norm3x, cot, cot_swap3x, cot3x], (jnp.float32, bf16)
    )
    near = pair((1, 1), [norm12, swap12, cot12, cot_swap12])
    own_part, sent = call(
        add_halves,
        (
            jax.ShapeDtypeStruct((rows, half), jnp.float32),
            jax.ShapeDtypeStruct((rows, half), bf16),
        ),
        0,
        [mine, swap(theirs)],
    )
    rest = lax.ppermute(sent, "grp", [(0, 1), (1, 0)])
    panel = up_weight.shape[1]
    grads = (
        jax.ShapeDtypeStruct((width, panel), jnp.float32),
        jax.ShapeDtypeStruct((panel, width), jnp.float32),
    )
    sums = call(add_products, grads, 0, list(group) + list(near))
    far, mixed = after(far, sums[0]), after(mixed, sums[0])
    swap_far, swap_mixed = swap(far), swap(mixed)
    cot_swap_over = swap(cot_over12)
    over = pair(
        (2, 2),
        [swap_far, far, swap_mixed, mixed]
        + [cot_over12, cot_swap_over, cot_swap_over, cot_over12],
    )
    third = pair(
        (2, 2), [norm3x, swap3x, far, swap_far, cot3x, cot_swap3x, mixed, swap_mixed]
    )
    last = list(over) + list(third)
    parts = [stream, own_part, rest]
    return pl.pallas_call(
        finish_products,
        out_shape=(jax.ShapeDtypeStruct((rows, half), bf16),) + grads,
        in_specs=[pl.BlockSpec(memory_space=pltpu.VMEM)] * (5 + len(last)),
        out_specs=[pl.BlockSpec(memory_space=pl.ANY)] * 3,
        scratch_shapes=[
            pltpu.VMEM((rows, half), bf16),
            pltpu.VMEM((4, TILE, width), jnp.float32),
            pltpu.SemaphoreType.DMA((5,)),
        ],
        cost_estimate=SMALL,
        compiler_params=pltpu.CompilerParams(vmem_limit_bytes=16 * 2**20),
    )(*sums, *parts, *last)


def layer(*args):
    query_vectors, up_weight = args[0], args[8]
    patches, grps, cores = (lax.axis_size(a) for a in ("patch", "grp", "col"))
    tokens = query_vectors.shape[0] * grps * patches
    if (patches, grps, cores) == (4, 2, 2) and tokens <= 2 * up_weight.shape[1]:
        return gather_plan(*args)
    return shards(*args)


def solution(mesh):
    return jax.shard_map(
        layer,
        mesh=mesh,
        in_specs=(
            P(("parts", "patch", "grp"), "col"),
            P(("parts", "patch", "grp"), "col"),
            P(("parts", "patch", "grp"), "col"),
            P(("parts", "patch", "grp"), "col"),
            P(("parts", "patch", "grp"), None),
            P(("parts", "patch", "grp")),
            P("col", None),
            P("col"),
            P(None, ("grp", "col")),
            P(("grp", "col"), None),
            P(("parts", "patch", "grp"), "col"),
        ),
        out_specs=(
            P(("parts", "patch", "grp"), "col"),
            P("parts", ("grp", "col")),
            P(("parts", "grp", "col"), None),
        ),
        check_vma=False,
    )
```

```python
import functools

import jax
import jax.numpy as jnp
from jax import lax
from jax.experimental import pallas as pl
from jax.experimental.pallas import tpu as pltpu
from jax.sharding import PartitionSpec as P

HEAD = 64
D = 1024
BLK = 128


def spread_rows(part_rows):
    stacked = lax.all_gather(part_rows[None], ("grp", "col"), axis=0, tiled=True)
    grp_count = lax.axis_size("grp")
    col_count = lax.axis_size("col")
    row_count = part_rows.shape[0]
    half_width = part_rows.shape[1]
    arranged = stacked.reshape(grp_count, col_count, row_count, half_width).transpose(0, 2, 1, 3)
    return arranged.reshape(grp_count * row_count, col_count * half_width)


def shards(
    query_vectors,
    key_vectors,
    value_vectors,
    residual,
    neighbor_ids,
    neighbor_count,
    output_weight,
    norm_gain,
    up_weight,
    down_weight,
    cotangent,
):
    key_all, value_all = (
        lax.all_gather(key_vectors, "grp", axis=0, tiled=True),
        lax.all_gather(value_vectors, "grp", axis=0, tiled=True),
    )
    row_count = query_vectors.shape[0]
    local_heads = query_vectors.shape[1] // HEAD
    group_count = key_all.shape[0] // BLK
    column_ids = jnp.arange(group_count, dtype=jnp.int32)
    slot_ids = jnp.arange(neighbor_ids.shape[1], dtype=jnp.int32)
    listed = (neighbor_ids[:, :, None] == column_ids[None, None, :]) & (
        slot_ids[None, :, None] < neighbor_count[:, None, None]
    )
    allowed = jnp.any(listed, axis=1)
    token_mask = jnp.repeat(jnp.repeat(allowed, BLK, axis=0), BLK, axis=1)
    query_heads = query_vectors.reshape(row_count, local_heads, HEAD)
    key_heads = key_all.reshape(-1, local_heads, HEAD)
    value_heads = value_all.reshape(-1, local_heads, HEAD)
    scores = jnp.einsum(
        "qhd,khd->hqk", query_heads, key_heads, preferred_element_type=jnp.float32
    ) * HEAD ** (-0.5)
    scores = jnp.where(token_mask[None], scores, -1e30)
    largest = jnp.max(scores, axis=2, keepdims=True)
    weights = jnp.exp(scores - largest)
    probs = (weights / jnp.sum(weights, axis=2, keepdims=True)).astype(jnp.bfloat16)
    attended = jnp.einsum("hqk,khd->qhd", probs, value_heads, preferred_element_type=jnp.float32)
    attended = attended.astype(jnp.bfloat16).reshape(row_count, -1)
    projected = jnp.dot(attended, output_weight, preferred_element_type=jnp.float32)
    stream = residual.astype(jnp.float32) + lax.psum_scatter(
        projected.astype(jnp.bfloat16), "col", scatter_dimension=1, tiled=True
    ).astype(jnp.float32)
    first_sum, second_sum = lax.psum(
        (jnp.sum(stream, axis=1), jnp.sum(stream * stream, axis=1)), "col"
    )
    center = first_sum[:, None] / D
    shifted = stream - center
    spread_sq = second_sum[:, None] / D - center * center
    normed = (shifted * lax.rsqrt(spread_sq + 1e-05) * norm_gain[None, :]).astype(jnp.bfloat16)
    normed_rows = spread_rows(normed)
    pre = jnp.dot(normed_rows, up_weight, preferred_element_type=jnp.float32)
    hidden = jax.nn.gelu(pre).astype(jnp.bfloat16)
    grp_count = lax.axis_size("grp")
    col_count = lax.axis_size("col")
    partial_out = jnp.dot(hidden, down_weight, preferred_element_type=jnp.float32)
    half_width = partial_out.shape[1] // col_count
    partial_out = partial_out.reshape(grp_count, row_count, col_count, half_width).transpose(
        0, 2, 1, 3
    )
    partial_out = partial_out.reshape(grp_count * col_count * row_count, half_width)
    ff_out = lax.psum_scatter(
        partial_out.astype(jnp.bfloat16), ("grp", "col"), scatter_dimension=0, tiled=True
    ).astype(jnp.float32)
    layer_out = (stream + ff_out).astype(jnp.bfloat16)
    back_rows = spread_rows(cotangent)
    back_hidden = lax.dot_general(
        back_rows, down_weight, (((1,), (1,)), ((), ())), preferred_element_type=jnp.float32
    )
    _, gelu_back = jax.vjp(jax.nn.gelu, pre)
    back_pre = gelu_back(back_hidden)[0].astype(jnp.bfloat16)
    up_local = lax.dot_general(
        normed_rows, back_pre, (((0,), (0,)), ((), ())), preferred_element_type=jnp.float32
    )
    down_local = lax.dot_general(
        hidden, back_rows, (((0,), (0,)), ((), ())), preferred_element_type=jnp.float32
    )
    up_grad, down_grad = (
        lax.psum(up_local.astype(jnp.bfloat16), "patch").astype(jnp.float32),
        lax.psum(down_local.astype(jnp.bfloat16), "patch").astype(jnp.float32),
    )
    return (layer_out, up_grad, down_grad)


GAIN_ROWS = 16
TILE = 256
PANEL_TILE = 512
ROOT, CUBIC = 0.7978845608028654, 0.044715
OWN_LIMIT = 56 * 2**20


def shift(x, axis, k):
    n = lax.axis_size(axis)
    return lax.ppermute(x, axis, [(i, (i + k) % n) for i in range(n)])


def after(x, *others):
    return lax.optimization_barrier((x,) + others)[0]


def others(x, axis):
    n = lax.axis_size(axis)
    if n & (n - 1):
        return [shift(x, axis, k) for k in range(1, n)]
    return [lax.ppermute(x, axis, [(i, i ^ k) for i in range(n)]) for k in range(1, n)]


def member(axis, k):
    n = lax.axis_size(axis)
    me = lax.axis_index(axis)
    return (me - k + n) % n if n & (n - 1) else me ^ k


def one_head(query, lane, head):
    return jnp.where((lane < HEAD) == (head == 0), query, jnp.zeros_like(query))


def pair_scores(query, key):
    return lax.dot_general(
        query, key, (((1,), (1,)), ((), ())), preferred_element_type=jnp.float32
    ) * HEAD ** (-0.5)


def core_columns(j, half):
    return pl.ds(pl.multiple_of(member("col", j) * half, half), half)


def join_cores(*refs):
    parts, out_ref = refs[:-1], refs[-1]
    half = parts[0].shape[1]
    for j, part in enumerate(parts):
        out_ref[:, core_columns(j, half)] = part[...]


def keep(*refs):
    count = len(refs) // 2
    for source, target in zip(refs[:count], refs[count:]):
        target[...] = source[...]


def keep_and_pick(one_ref, two_ref, other_ref, kept_one_ref, kept_two_ref, picked_ref):
    kept_one_ref[...] = one_ref[...]
    kept_two_ref[...] = two_ref[...]
    picked_ref[...] = jnp.where(lax.axis_index("col") == 0, other_ref[...], one_ref[...])


def add_halves(mine_ref, other_ref, own_ref, sent_ref):
    rows = own_ref.shape[0]
    total = mine_ref[...] + other_ref[...].astype(jnp.float32)
    own_ref[...] = total[:rows]
    sent_ref[...] = total[rows:].astype(sent_ref.dtype)


def gelu_and_slope(pre):
    square = pre * pre
    curve = jnp.tanh(ROOT * (pre + CUBIC * (square * pre)))
    half = 0.5 * (1.0 + curve)
    slope = half + 0.5 * pre * (1.0 - curve * curve) * (ROOT * (1.0 + 3.0 * CUBIC * square))
    return pre * half, slope


def add_layer(stream_ref, own_ref, other_ref, out_ref):
    total = stream_ref[...] + own_ref[...] + other_ref[...].astype(jnp.float32)
    out_ref[...] = total.astype(out_ref.dtype)


def feed_forward(choices, share, *refs):
    count = 2 * sum(choices)
    blocks, (up_ref, down_ref), outs = refs[:count], refs[count : count + 2], refs[count + 2 :]
    rows_ref, back_pre_ref, hidden_ref, back_ref = outs[:4]
    first = lax.axis_index("col") == 0
    at = 0
    for out_ref in (rows_ref, back_ref):
        for i, width in enumerate(choices):
            rows = blocks[at].shape[0]
            block = blocks[at][...]
            if width == 2:
                block = jnp.where(first, block, blocks[at + 1][...])
            out_ref[pl.ds(i * rows, rows), :] = block
            at += width
    rows, back = rows_ref[...], back_ref[...]
    for start in range(0, up_ref.shape[1], PANEL_TILE):
        tile = pl.ds(start, PANEL_TILE)
        pre = jnp.dot(rows, up_ref[:, tile], preferred_element_type=jnp.float32)
        back_hidden = lax.dot_general(
            back, down_ref[tile, :], (((1,), (1,)), ((), ())), preferred_element_type=jnp.float32
        )
        hidden, slope = gelu_and_slope(pre)
        hidden_ref[:, tile] = hidden.astype(jnp.bfloat16)
        back_pre_ref[:, tile] = (back_hidden * slope).astype(jnp.bfloat16)
    if share:
        for j, out_ref in enumerate(outs[4:]):
            part = jnp.dot(
                hidden_ref[...],
                down_ref[:, core_columns(j, out_ref.shape[1])],
                preferred_element_type=jnp.float32,
            )
            out_ref[...] = part.astype(out_ref.dtype)


def attend(grps, ids_ref, count_ref, gain_ref, query_ref, *refs):
    seen = []
    for k in range(grps):
        listed = [
            (ids_ref[0, m] == member("grp", k)) & (m < count_ref[0]) for m in range(ids_ref.shape[1])
        ]
        seen.append(functools.reduce(jnp.logical_or, listed))
    keys, values, (out_ref, score_ref) = refs[:grps], refs[grps : 2 * grps], refs[2 * grps :]
    rows, half = query_ref.shape
    heads = half // HEAD
    lane = lax.broadcasted_iota(jnp.int32, (rows, 2 * HEAD), 1)
    for head in range(heads):
        cols = pl.ds(head // 2 * 2 * HEAD, 2 * HEAD)
        query = one_head(query_ref[:, cols], lane, head % 2)
        for k in range(grps):
            part = pair_scores(query, keys[k][:, cols])
            score_ref[head * grps + k] = jnp.where(seen[k], part, -1e30)
    for pair in range(heads // 2):
        cols = pl.ds(pair * 2 * HEAD, 2 * HEAD)
        value = [ref[:, cols] for ref in values]
        found = []
        for head in (2 * pair, 2 * pair + 1):
            scores = [score_ref[head * grps + k] for k in range(grps)]
            largest = scores[0]
            for part in scores[1:]:
                largest = jnp.maximum(largest, part)
            largest = jnp.max(largest, axis=1, keepdims=True)
            weights = [jnp.exp(part - largest) for part in scores]
            total = weights[0]
            for part in weights[1:]:
                total = total + part
            total = jnp.sum(total, axis=1, keepdims=True)
            result = 0.0
            for k in range(grps):
                probs = (weights[k] / total).astype(jnp.bfloat16)
                result = result + jnp.dot(probs, value[k], preferred_element_type=jnp.float32)
            found.append(result)
        out_ref[pl.ds(0, rows), cols] = jnp.where(lane < HEAD, found[0], found[1]).astype(
            jnp.bfloat16
        )
    gain = gain_ref[...]
    high = gain.astype(jnp.bfloat16).astype(jnp.float32)
    middle = (gain - high).astype(jnp.bfloat16).astype(jnp.float32)
    low = gain - high - middle
    row = lax.broadcasted_iota(jnp.int32, (GAIN_ROWS, half), 0)
    parts = jnp.where(
        row == 0, high, jnp.where(row == 1, middle, jnp.where(row == 2, low, 0.0))
    )
    out_ref[pl.ds(rows, GAIN_ROWS), :] = parts.astype(jnp.bfloat16)


def project(cores, *refs):
    packs, weights, residuals = refs[:cores], refs[cores : 2 * cores], refs[2 * cores : 3 * cores]
    stream_ref, normed_ref, full, gain = refs[3 * cores :]
    rows, half = stream_ref.shape
    width = half * cores
    full[...] = sum(
        jnp.dot(pack[pl.ds(0, rows), :], weight[...], preferred_element_type=jnp.float32)
        for pack, weight in zip(packs, weights)
    )
    for j, pack in enumerate(packs):
        cols = core_columns(j, half)
        part = full[:, cols] + residuals[j][...].astype(jnp.float32)
        full[:, cols] = part
        if j == 0:
            stream_ref[...] = part
        gains = pack[pl.ds(rows, GAIN_ROWS), :].astype(jnp.float32)
        gain[0:1, cols] = (gains[1:2] + gains[2:3]) + gains[0:1]
    stream = full[...]
    center = jnp.sum(stream, axis=1, keepdims=True) / width
    shifted = stream - center
    spread_sq = jnp.sum(shifted * shifted, axis=1, keepdims=True) / width
    normed_ref[...] = (shifted * lax.rsqrt(spread_sq + 1e-05) * gain[0:1, :]).astype(jnp.bfloat16)


def add_products(*refs):
    pairs, (up_ref, down_ref) = refs[:-2], refs[-2:]
    count = len(pairs) // 4
    for start in range(0, up_ref.shape[0], TILE):
        tile = pl.ds(start, TILE)
        for k, out_ref in ((0, up_ref), (2, down_ref)):
            out_ref[tile, :] = sum(
                lax.dot_general(
                    pairs[4 * i + k][:, tile],
                    pairs[4 * i + k + 1][...],
                    (((0,), (0,)), ((), ())),
                    preferred_element_type=jnp.float32,
                )
                for i in range(count)
            )


def finish_products(*refs):
    up_sum, down_sum = refs[:2]
    up_ref, down_ref, buffer, sems = refs[-4:]
    pairs = refs[2:-4]
    count = len(pairs) // 4
    copies = []
    for start in range(0, up_ref.shape[0], TILE):
        tile = pl.ds(start, TILE)
        for k, sum_ref, out_ref in ((0, up_sum, up_ref), (2, down_sum, down_ref)):
            slot = len(copies) % buffer.shape[0]
            if len(copies) >= buffer.shape[0]:
                copies[-buffer.shape[0]].wait()
            buffer[slot] = sum_ref[tile, :] + sum(
                lax.dot_general(
                    pairs[4 * i + k][:, tile],
                    pairs[4 * i + k + 1][...],
                    (((0,), (0,)), ((), ())),
                    preferred_element_type=jnp.float32,
                )
                for i in range(count)
            )
            copies.append(
                pltpu.make_async_copy(buffer.at[slot], out_ref.at[tile], sems.at[slot])
            )
            copies[-1].start()
    for copy in copies[-buffer.shape[0] :]:
        copy.wait()


SMALL = pl.CostEstimate(flops=1, bytes_accessed=1, transcendentals=0)
LARGE = pl.CostEstimate(flops=10**8, bytes_accessed=1, transcendentals=0)


def call(kernel, out_shape, smem, args, scratch=(), limit=16 * 2**20, cost=SMALL):
    return pl.pallas_call(
        kernel,
        out_shape=out_shape,
        in_specs=[pl.BlockSpec(memory_space=pltpu.SMEM)] * smem
        + [pl.BlockSpec(memory_space=pltpu.VMEM)] * (len(args) - smem),
        scratch_shapes=scratch,
        cost_estimate=cost,
        compiler_params=pltpu.CompilerParams(vmem_limit_bytes=limit),
    )(*args)


def send(x, routes):
    patches, grps, cores = (lax.axis_size(a) for a in ("patch", "grp", "col"))
    pairs = []
    for p in range(patches):
        for g in range(grps):
            for c, route in enumerate(routes):
                if route is not None:
                    to = ((p ^ route[0]) * grps + (g ^ route[1])) * cores + c
                    pairs.append(((p * grps + g) * cores + c, to))
    return lax.ppermute(x, ("patch", "grp", "col"), pairs)


def swap(x):
    return lax.ppermute(x, "col", [(0, 1), (1, 0)])


def gather_plan(
    query_vectors,
    key_vectors,
    value_vectors,
    residual,
    neighbor_ids,
    neighbor_count,
    output_weight,
    norm_gain,
    up_weight,
    down_weight,
    cotangent,
):
    cores = lax.axis_size("col")
    grps = lax.axis_size("grp")
    rows, half = query_vectors.shape
    width = half * cores

    bf16 = jnp.bfloat16
    cot_parts = [cotangent] + others(cotangent, "col")
    residuals = [residual] + others(residual, "col")
    keys = [key_vectors] + others(key_vectors, "grp")
    values = [value_vectors] + others(value_vectors, "grp")
    weights = [output_weight] + others(output_weight, "col")
    cot = call(join_cores, jax.ShapeDtypeStruct((rows, width), bf16), 0, cot_parts)
    cot12 = send(cot, [(1, 0), (2, 0)])
    cot3x = send(cot, [(3, 0), (0, 1)])

    weights[0], residuals[0] = call(
        keep,
        [jax.ShapeDtypeStruct(a.shape, bf16) for a in (output_weight, residual)],
        0,
        [after(output_weight, cot), residual],
    )
    packed = call(
        functools.partial(attend, grps),
        jax.ShapeDtypeStruct((rows + GAIN_ROWS, half), bf16),
        2,
        [neighbor_ids, neighbor_count, norm_gain[None], after(query_vectors, weights[0])]
        + keys
        + values,
        [pltpu.VMEM((half // HEAD * grps, rows, rows), jnp.float32)],
        OWN_LIMIT,
    )
    stream, normed = call(
        functools.partial(project, cores),
        (
            jax.ShapeDtypeStruct((rows, half), jnp.float32),
            jax.ShapeDtypeStruct((rows, width), bf16),
        ),
        0,
        [packed] + others(packed, "col") + [after(weights[0], cot12)] + weights[1:] + residuals,
        [pltpu.VMEM((rows, width), jnp.float32), pltpu.VMEM((8, width), jnp.float32)],
    )

    norm12 = send(normed, [(1, 0), (2, 0)])
    norm3x = send(normed, [(3, 0), (0, 1)])
    cot12, cot3x = after(cot12, normed), after(cot3x, normed)
    cot_over12 = send(cot12, [(0, 1), (0, 1)])
    cot_swap12, cot_swap3x = swap(cot12), swap(cot3x)
    norm12, norm3x, picked = call(
        keep_and_pick,
        [jax.ShapeDtypeStruct((rows, width), bf16)] * 3,
        0,
        [norm12, norm3x, cot3x],
        cost=LARGE,
    )
    norm12, norm3x, picked, *_ = lax.optimization_barrier(
        (norm12, norm3x, picked, cot_over12, cot_swap12)
    )
    far = send(norm3x, [(0, 1), (1, 0)])
    mixed = send(picked, [(0, 1), (0, 1)])
    swap12, swap3x = swap(norm12), swap(norm3x)

    def pair(choices, blocks, shares=()):
        made = jax.ShapeDtypeStruct((len(choices) * rows, width), bf16)
        return call(
            functools.partial(feed_forward, choices, bool(shares)),
            [made] * 4 + [jax.ShapeDtypeStruct((2 * rows, half), t) for t in shares],
            0,
            blocks + [up_weight, down_weight],
        )

    *group, mine, theirs = pair(
        (1, 2), [normed, swap3x, norm3x, cot, cot_swap3x, cot3x], (jnp.float32, bf16)
    )
    near = pair((1, 1), [norm12, swap12, cot12, cot_swap12])
    own_part, sent = call(
        add_halves,
        (
            jax.ShapeDtypeStruct((rows, half), jnp.float32),
            jax.ShapeDtypeStruct((rows, half), bf16),
        ),
        0,
        [mine, swap(theirs)],
    )
    rest = lax.ppermute(sent, "grp", [(0, 1), (1, 0)])
    panel = up_weight.shape[1]
    grads = (
        jax.ShapeDtypeStruct((width, panel), jnp.float32),
        jax.ShapeDtypeStruct((panel, width), jnp.float32),
    )
    sums = call(add_products, grads, 0, list(group) + list(near))
    far, mixed = after(far, sums[0]), after(mixed, sums[0])
    swap_far, swap_mixed = swap(far), swap(mixed)
    cot_swap_over = swap(cot_over12)
    last = pair(
        (2, 2, 2, 2),
        [swap_far, far, swap_mixed, mixed, norm3x, swap3x, far, swap_far]
        + [cot_over12, cot_swap_over, cot_swap_over, cot_over12]
        + [cot3x, cot_swap3x, mixed, swap_mixed],
    )
    up_grad, down_grad = pl.pallas_call(
        finish_products,
        out_shape=grads,
        in_specs=[pl.BlockSpec(memory_space=pltpu.VMEM)] * (2 + len(last)),
        out_specs=[pl.BlockSpec(memory_space=pl.ANY)] * 2,
        scratch_shapes=[
            pltpu.VMEM((8, TILE, width), jnp.float32),
            pltpu.SemaphoreType.DMA((8,)),
        ],
        cost_estimate=SMALL,
        compiler_params=pltpu.CompilerParams(vmem_limit_bytes=16 * 2**20),
    )(*sums, *last)
    layer_out = call(
        add_layer,
        jax.ShapeDtypeStruct((rows, half), bf16),
        0,
        [stream, own_part, after(rest, up_grad)],
    )
    return (layer_out, up_grad, down_grad)


def layer(*args):
    query_vectors, up_weight = args[0], args[8]
    patches, grps, cores = (lax.axis_size(a) for a in ("patch", "grp", "col"))
    tokens = query_vectors.shape[0] * grps * patches
    if (patches, grps, cores) == (4, 2, 2) and tokens <= 2 * up_weight.shape[1]:
        return gather_plan(*args)
    return shards(*args)


def solution(mesh):
    return jax.shard_map(
        layer,
        mesh=mesh,
        in_specs=(
            P(("parts", "patch", "grp"), "col"),
            P(("parts", "patch", "grp"), "col"),
            P(("parts", "patch", "grp"), "col"),
            P(("parts", "patch", "grp"), "col"),
            P(("parts", "patch", "grp"), None),
            P(("parts", "patch", "grp")),
            P("col", None),
            P("col"),
            P(None, ("grp", "col")),
            P(("grp", "col"), None),
            P(("parts", "patch", "grp"), "col"),
        ),
        out_specs=(
            P(("parts", "patch", "grp"), "col"),
            P("parts", ("grp", "col")),
            P(("parts", "grp", "col"), None),
        ),
        check_vma=False,
    )
```

```python
import functools

import jax
import jax.numpy as jnp
from jax import lax
from jax.experimental import pallas as pl
from jax.experimental.pallas import tpu as pltpu
from jax.sharding import PartitionSpec as P

HEAD = 64
D = 1024
BLK = 128


def spread_rows(part_rows):
    stacked = lax.all_gather(part_rows[None], ("grp", "col"), axis=0, tiled=True)
    grp_count = lax.axis_size("grp")
    col_count = lax.axis_size("col")
    row_count = part_rows.shape[0]
    half_width = part_rows.shape[1]
    arranged = stacked.reshape(grp_count, col_count, row_count, half_width).transpose(0, 2, 1, 3)
    return arranged.reshape(grp_count * row_count, col_count * half_width)


def shards(
    query_vectors,
    key_vectors,
    value_vectors,
    residual,
    neighbor_ids,
    neighbor_count,
    output_weight,
    norm_gain,
    up_weight,
    down_weight,
    cotangent,
):
    key_all, value_all = (
        lax.all_gather(key_vectors, "grp", axis=0, tiled=True),
        lax.all_gather(value_vectors, "grp", axis=0, tiled=True),
    )
    row_count = query_vectors.shape[0]
    local_heads = query_vectors.shape[1] // HEAD
    group_count = key_all.shape[0] // BLK
    column_ids = jnp.arange(group_count, dtype=jnp.int32)
    slot_ids = jnp.arange(neighbor_ids.shape[1], dtype=jnp.int32)
    listed = (neighbor_ids[:, :, None] == column_ids[None, None, :]) & (
        slot_ids[None, :, None] < neighbor_count[:, None, None]
    )
    allowed = jnp.any(listed, axis=1)
    token_mask = jnp.repeat(jnp.repeat(allowed, BLK, axis=0), BLK, axis=1)
    query_heads = query_vectors.reshape(row_count, local_heads, HEAD)
    key_heads = key_all.reshape(-1, local_heads, HEAD)
    value_heads = value_all.reshape(-1, local_heads, HEAD)
    scores = jnp.einsum(
        "qhd,khd->hqk", query_heads, key_heads, preferred_element_type=jnp.float32
    ) * HEAD ** (-0.5)
    scores = jnp.where(token_mask[None], scores, -1e30)
    largest = jnp.max(scores, axis=2, keepdims=True)
    weights = jnp.exp(scores - largest)
    probs = (weights / jnp.sum(weights, axis=2, keepdims=True)).astype(jnp.bfloat16)
    attended = jnp.einsum("hqk,khd->qhd", probs, value_heads, preferred_element_type=jnp.float32)
    attended = attended.astype(jnp.bfloat16).reshape(row_count, -1)
    projected = jnp.dot(attended, output_weight, preferred_element_type=jnp.float32)
    stream = residual.astype(jnp.float32) + lax.psum_scatter(
        projected.astype(jnp.bfloat16), "col", scatter_dimension=1, tiled=True
    ).astype(jnp.float32)
    first_sum, second_sum = lax.psum(
        (jnp.sum(stream, axis=1), jnp.sum(stream * stream, axis=1)), "col"
    )
    center = first_sum[:, None] / D
    shifted = stream - center
    spread_sq = second_sum[:, None] / D - center * center
    normed = (shifted * lax.rsqrt(spread_sq + 1e-05) * norm_gain[None, :]).astype(jnp.bfloat16)
    normed_rows = spread_rows(normed)
    pre = jnp.dot(normed_rows, up_weight, preferred_element_type=jnp.float32)
    hidden = jax.nn.gelu(pre).astype(jnp.bfloat16)
    grp_count = lax.axis_size("grp")
    col_count = lax.axis_size("col")
    partial_out = jnp.dot(hidden, down_weight, preferred_element_type=jnp.float32)
    half_width = partial_out.shape[1] // col_count
    partial_out = partial_out.reshape(grp_count, row_count, col_count, half_width).transpose(
        0, 2, 1, 3
    )
    partial_out = partial_out.reshape(grp_count * col_count * row_count, half_width)
    ff_out = lax.psum_scatter(
        partial_out.astype(jnp.bfloat16), ("grp", "col"), scatter_dimension=0, tiled=True
    ).astype(jnp.float32)
    layer_out = (stream + ff_out).astype(jnp.bfloat16)
    back_rows = spread_rows(cotangent)
    back_hidden = lax.dot_general(
        back_rows, down_weight, (((1,), (1,)), ((), ())), preferred_element_type=jnp.float32
    )
    _, gelu_back = jax.vjp(jax.nn.gelu, pre)
    back_pre = gelu_back(back_hidden)[0].astype(jnp.bfloat16)
    up_local = lax.dot_general(
        normed_rows, back_pre, (((0,), (0,)), ((), ())), preferred_element_type=jnp.float32
    )
    down_local = lax.dot_general(
        hidden, back_rows, (((0,), (0,)), ((), ())), preferred_element_type=jnp.float32
    )
    up_grad, down_grad = (
        lax.psum(up_local.astype(jnp.bfloat16), "patch").astype(jnp.float32),
        lax.psum(down_local.astype(jnp.bfloat16), "patch").astype(jnp.float32),
    )
    return (layer_out, up_grad, down_grad)


GAIN_ROWS = 16
TILE = 256
PANEL_TILE = 512
ROOT, CUBIC = 0.7978845608028654, 0.044715
OWN_LIMIT = 54 * 2**20


def shift(x, axis, k):
    n = lax.axis_size(axis)
    return lax.ppermute(x, axis, [(i, (i + k) % n) for i in range(n)])


def after(x, *others):
    return lax.optimization_barrier((x,) + others)[0]


def others(x, axis):
    n = lax.axis_size(axis)
    if n & (n - 1):
        return [shift(x, axis, k) for k in range(1, n)]
    return [lax.ppermute(x, axis, [(i, i ^ k) for i in range(n)]) for k in range(1, n)]


def member(axis, k):
    n = lax.axis_size(axis)
    me = lax.axis_index(axis)
    return (me - k + n) % n if n & (n - 1) else me ^ k


def one_head(query, lane, head):
    return jnp.where((lane < HEAD) == (head == 0), query, jnp.zeros_like(query))


def pair_scores(query, key):
    return lax.dot_general(
        query, key, (((1,), (1,)), ((), ())), preferred_element_type=jnp.float32
    ) * HEAD ** (-0.5)


def core_columns(j, half):
    return pl.ds(pl.multiple_of(member("col", j) * half, half), half)


def join_cores(*refs):
    parts, out_ref = refs[:-1], refs[-1]
    half = parts[0].shape[1]
    for j, part in enumerate(parts):
        out_ref[:, core_columns(j, half)] = part[...]


def keep(*refs):
    count = len(refs) // 2
    for source, target in zip(refs[:count], refs[count:]):
        target[...] = source[...]


def keep_and_pick(one_ref, two_ref, other_ref, kept_one_ref, kept_two_ref, picked_ref):
    kept_one_ref[...] = one_ref[...]
    kept_two_ref[...] = two_ref[...]
    picked_ref[...] = jnp.where(lax.axis_index("col") == 0, other_ref[...], one_ref[...])


def add_halves(mine_ref, other_ref, own_ref, sent_ref):
    rows = own_ref.shape[0]
    total = mine_ref[...] + other_ref[...].astype(jnp.float32)
    own_ref[...] = total[:rows]
    sent_ref[...] = total[rows:].astype(sent_ref.dtype)


def gelu_and_slope(pre):
    square = pre * pre
    curve = jnp.tanh(ROOT * (pre + CUBIC * (square * pre)))
    half = 0.5 * (1.0 + curve)
    slope = half + 0.5 * pre * (1.0 - curve * curve) * (ROOT * (1.0 + 3.0 * CUBIC * square))
    return pre * half, slope


def add_layer(stream_ref, own_ref, other_ref, out_ref):
    total = stream_ref[...] + own_ref[...] + other_ref[...].astype(jnp.float32)
    out_ref[...] = total.astype(out_ref.dtype)


def feed_forward(choices, share, *refs):
    count = 2 * sum(choices)
    blocks, (up_ref, down_ref), outs = refs[:count], refs[count : count + 2], refs[count + 2 :]
    rows_ref, back_pre_ref, hidden_ref, back_ref = outs[:4]
    first = lax.axis_index("col") == 0
    at = 0
    for out_ref in (rows_ref, back_ref):
        for i, width in enumerate(choices):
            rows = blocks[at].shape[0]
            block = blocks[at][...]
            if width == 2:
                block = jnp.where(first, block, blocks[at + 1][...])
            out_ref[pl.ds(i * rows, rows), :] = block
            at += width
    rows, back = rows_ref[...], back_ref[...]
    for start in range(0, up_ref.shape[1], PANEL_TILE):
        tile = pl.ds(start, PANEL_TILE)
        pre = jnp.dot(rows, up_ref[:, tile], preferred_element_type=jnp.float32)
        back_hidden = lax.dot_general(
            back, down_ref[tile, :], (((1,), (1,)), ((), ())), preferred_element_type=jnp.float32
        )
        hidden, slope = gelu_and_slope(pre)
        hidden_ref[:, tile] = hidden.astype(jnp.bfloat16)
        back_pre_ref[:, tile] = (back_hidden * slope).astype(jnp.bfloat16)
    if share:
        for j, out_ref in enumerate(outs[4:]):
            part = jnp.dot(
                hidden_ref[...],
                down_ref[:, core_columns(j, out_ref.shape[1])],
                preferred_element_type=jnp.float32,
            )
            out_ref[...] = part.astype(out_ref.dtype)


def attend(grps, ids_ref, count_ref, gain_ref, query_ref, *refs):
    seen = []
    for k in range(grps):
        listed = [
            (ids_ref[0, m] == member("grp", k)) & (m < count_ref[0]) for m in range(ids_ref.shape[1])
        ]
        seen.append(functools.reduce(jnp.logical_or, listed))
    keys, values, (out_ref, score_ref) = refs[:grps], refs[grps : 2 * grps], refs[2 * grps :]
    rows, half = query_ref.shape
    heads = half // HEAD
    lane = lax.broadcasted_iota(jnp.int32, (rows, 2 * HEAD), 1)
    for head in range(heads):
        cols = pl.ds(head // 2 * 2 * HEAD, 2 * HEAD)
        query = one_head(query_ref[:, cols], lane, head % 2)
        for k in range(grps):
            part = pair_scores(query, keys[k][:, cols])
            score_ref[head * grps + k] = jnp.where(seen[k], part, -1e30)
    for pair in range(heads // 2):
        cols = pl.ds(pair * 2 * HEAD, 2 * HEAD)
        value = [ref[:, cols] for ref in values]
        found = []
        for head in (2 * pair, 2 * pair + 1):
            scores = [score_ref[head * grps + k] for k in range(grps)]
            largest = scores[0]
            for part in scores[1:]:
                largest = jnp.maximum(largest, part)
            largest = jnp.max(largest, axis=1, keepdims=True)
            weights = [jnp.exp(part - largest) for part in scores]
            total = weights[0]
            for part in weights[1:]:
                total = total + part
            total = jnp.sum(total, axis=1, keepdims=True)
            result = 0.0
            for k in range(grps):
                probs = (weights[k] / total).astype(jnp.bfloat16)
                result = result + jnp.dot(probs, value[k], preferred_element_type=jnp.float32)
            found.append(result)
        out_ref[pl.ds(0, rows), cols] = jnp.where(lane < HEAD, found[0], found[1]).astype(
            jnp.bfloat16
        )
    gain = gain_ref[...]
    high = gain.astype(jnp.bfloat16).astype(jnp.float32)
    middle = (gain - high).astype(jnp.bfloat16).astype(jnp.float32)
    low = gain - high - middle
    row = lax.broadcasted_iota(jnp.int32, (GAIN_ROWS, half), 0)
    parts = jnp.where(
        row == 0, high, jnp.where(row == 1, middle, jnp.where(row == 2, low, 0.0))
    )
    out_ref[pl.ds(rows, GAIN_ROWS), :] = parts.astype(jnp.bfloat16)


def project(cores, *refs):
    packs, weights, residuals = refs[:cores], refs[cores : 2 * cores], refs[2 * cores : 3 * cores]
    stream_ref, normed_ref, full, gain = refs[3 * cores :]
    rows, half = stream_ref.shape
    width = half * cores
    full[...] = sum(
        jnp.dot(pack[pl.ds(0, rows), :], weight[...], preferred_element_type=jnp.float32)
        for pack, weight in zip(packs, weights)
    )
    for j, pack in enumerate(packs):
        cols = core_columns(j, half)
        part = full[:, cols] + residuals[j][...].astype(jnp.float32)
        full[:, cols] = part
        if j == 0:
            stream_ref[...] = part
        gains = pack[pl.ds(rows, GAIN_ROWS), :].astype(jnp.float32)
        gain[0:1, cols] = (gains[1:2] + gains[2:3]) + gains[0:1]
    stream = full[...]
    center = jnp.sum(stream, axis=1, keepdims=True) / width
    shifted = stream - center
    spread_sq = jnp.sum(shifted * shifted, axis=1, keepdims=True) / width
    normed_ref[...] = (shifted * lax.rsqrt(spread_sq + 1e-05) * gain[0:1, :]).astype(jnp.bfloat16)


def add_products(*refs):
    pairs, (up_ref, down_ref) = refs[:-2], refs[-2:]
    count = len(pairs) // 4
    for start in range(0, up_ref.shape[0], TILE):
        tile = pl.ds(start, TILE)
        for k, out_ref in ((0, up_ref), (2, down_ref)):
            out_ref[tile, :] = sum(
                lax.dot_general(
                    pairs[4 * i + k][:, tile],
                    pairs[4 * i + k + 1][...],
                    (((0,), (0,)), ((), ())),
                    preferred_element_type=jnp.float32,
                )
                for i in range(count)
            )


def finish_products(*refs):
    up_sum, down_sum = refs[:2]
    up_ref, down_ref, buffer, sems = refs[-4:]
    pairs = refs[2:-4]
    count = len(pairs) // 4
    copies = []
    for start in range(0, up_ref.shape[0], TILE):
        tile = pl.ds(start, TILE)
        for k, sum_ref, out_ref in ((0, up_sum, up_ref), (2, down_sum, down_ref)):
            slot = len(copies) % buffer.shape[0]
            if len(copies) >= buffer.shape[0]:
                copies[-buffer.shape[0]].wait()
            buffer[slot] = sum_ref[tile, :] + sum(
                lax.dot_general(
                    pairs[4 * i + k][:, tile],
                    pairs[4 * i + k + 1][...],
                    (((0,), (0,)), ((), ())),
                    preferred_element_type=jnp.float32,
                )
                for i in range(count)
            )
            copies.append(
                pltpu.make_async_copy(buffer.at[slot], out_ref.at[tile], sems.at[slot])
            )
            copies[-1].start()
    for copy in copies[-buffer.shape[0] :]:
        copy.wait()


SMALL = pl.CostEstimate(flops=1, bytes_accessed=1, transcendentals=0)
LARGE = pl.CostEstimate(flops=10**9, bytes_accessed=1, transcendentals=0)


def call(kernel, out_shape, smem, args, scratch=(), limit=16 * 2**20, cost=SMALL):
    return pl.pallas_call(
        kernel,
        out_shape=out_shape,
        in_specs=[pl.BlockSpec(memory_space=pltpu.SMEM)] * smem
        + [pl.BlockSpec(memory_space=pltpu.VMEM)] * (len(args) - smem),
        scratch_shapes=scratch,
        cost_estimate=cost,
        compiler_params=pltpu.CompilerParams(vmem_limit_bytes=limit),
    )(*args)


def send(x, routes):
    patches, grps, cores = (lax.axis_size(a) for a in ("patch", "grp", "col"))
    pairs = []
    for p in range(patches):
        for g in range(grps):
            for c, route in enumerate(routes):
                if route is not None:
                    to = ((p ^ route[0]) * grps + (g ^ route[1])) * cores + c
                    pairs.append(((p * grps + g) * cores + c, to))
    return lax.ppermute(x, ("patch", "grp", "col"), pairs)


def swap(x):
    return lax.ppermute(x, "col", [(0, 1), (1, 0)])


def gather_plan(
    query_vectors,
    key_vectors,
    value_vectors,
    residual,
    neighbor_ids,
    neighbor_count,
    output_weight,
    norm_gain,
    up_weight,
    down_weight,
    cotangent,
):
    cores = lax.axis_size("col")
    grps = lax.axis_size("grp")
    rows, half = query_vectors.shape
    width = half * cores

    bf16 = jnp.bfloat16
    cot_parts = [cotangent] + others(cotangent, "col")
    residuals = [residual] + others(residual, "col")
    keys = [key_vectors] + others(key_vectors, "grp")
    values = [value_vectors] + others(value_vectors, "grp")
    weights = [output_weight] + others(output_weight, "col")
    cot = call(join_cores, jax.ShapeDtypeStruct((rows, width), bf16), 0, cot_parts)
    cot12 = send(cot, [(1, 0), (2, 0)])
    cot3x = send(cot, [(3, 0), (0, 1)])

    weights[0], residuals[0] = call(
        keep,
        [jax.ShapeDtypeStruct(a.shape, bf16) for a in (output_weight, residual)],
        0,
        [after(output_weight, cot), residual],
    )
    packed = call(
        functools.partial(attend, grps),
        jax.ShapeDtypeStruct((rows + GAIN_ROWS, half), bf16),
        2,
        [neighbor_ids, neighbor_count, norm_gain[None], after(query_vectors, weights[0])]
        + keys
        + values,
        [pltpu.VMEM((half // HEAD * grps, rows, rows), jnp.float32)],
        OWN_LIMIT,
    )
    stream, normed = call(
        functools.partial(project, cores),
        (
            jax.ShapeDtypeStruct((rows, half), jnp.float32),
            jax.ShapeDtypeStruct((rows, width), bf16),
        ),
        0,
        [packed] + others(packed, "col") + [after(weights[0], cot12)] + weights[1:] + residuals,
        [pltpu.VMEM((rows, width), jnp.float32), pltpu.VMEM((8, width), jnp.float32)],
    )

    norm12 = send(normed, [(1, 0), (2, 0)])
    norm3x = send(normed, [(3, 0), (0, 1)])
    cot12, cot3x = after(cot12, normed), after(cot3x, normed)
    cot_over12 = send(cot12, [(0, 1), (0, 1)])
    cot_swap12, cot_swap3x = swap(cot12), swap(cot3x)
    norm12, norm3x, picked = call(
        keep_and_pick,
        [jax.ShapeDtypeStruct((rows, width), bf16)] * 3,
        0,
        [norm12, norm3x, cot3x],
        cost=LARGE,
    )
    norm12, norm3x, picked, *_ = lax.optimization_barrier(
        (norm12, norm3x, picked, cot_over12, cot_swap12)
    )
    far = send(norm3x, [(0, 1), (1, 0)])
    mixed = send(picked, [(0, 1), (0, 1)])
    swap12, swap3x = swap(norm12), swap(norm3x)

    def pair(choices, blocks, shares=()):
        made = jax.ShapeDtypeStruct((len(choices) * rows, width), bf16)
        return call(
            functools.partial(feed_forward, choices, bool(shares)),
            [made] * 4 + [jax.ShapeDtypeStruct((2 * rows, half), t) for t in shares],
            0,
            blocks + [up_weight, down_weight],
        )

    *group, mine, theirs = pair(
        (1, 2), [normed, swap3x, norm3x, cot, cot_swap3x, cot3x], (jnp.float32, bf16)
    )
    near = pair((1, 1), [norm12, swap12, cot12, cot_swap12])
    own_part, sent = call(
        add_halves,
        (
            jax.ShapeDtypeStruct((rows, half), jnp.float32),
            jax.ShapeDtypeStruct((rows, half), bf16),
        ),
        0,
        [mine, swap(theirs)],
    )
    rest = lax.ppermute(sent, "grp", [(0, 1), (1, 0)])
    panel = up_weight.shape[1]
    grads = (
        jax.ShapeDtypeStruct((width, panel), jnp.float32),
        jax.ShapeDtypeStruct((panel, width), jnp.float32),
    )
    sums = call(add_products, grads, 0, list(group) + list(near))
    far, mixed = after(far, sums[0]), after(mixed, sums[0])
    swap_far, swap_mixed = swap(far), swap(mixed)
    cot_swap_over = swap(cot_over12)
    last = pair(
        (2, 2, 2, 2),
        [swap_far, far, swap_mixed, mixed, norm3x, swap3x, far, swap_far]
        + [cot_over12, cot_swap_over, cot_swap_over, cot_over12]
        + [cot3x, cot_swap3x, mixed, swap_mixed],
    )
    up_grad, down_grad = pl.pallas_call(
        finish_products,
        out_shape=grads,
        in_specs=[pl.BlockSpec(memory_space=pltpu.VMEM)] * (2 + len(last)),
        out_specs=[pl.BlockSpec(memory_space=pl.ANY)] * 2,
        scratch_shapes=[
            pltpu.VMEM((8, TILE, width), jnp.float32),
            pltpu.SemaphoreType.DMA((8,)),
        ],
        cost_estimate=SMALL,
        compiler_params=pltpu.CompilerParams(vmem_limit_bytes=16 * 2**20),
    )(*sums, *last)
    layer_out = call(
        add_layer,
        jax.ShapeDtypeStruct((rows, half), bf16),
        0,
        [stream, own_part, after(rest, up_grad)],
    )
    return (layer_out, up_grad, down_grad)


def layer(*args):
    query_vectors, up_weight = args[0], args[8]
    patches, grps, cores = (lax.axis_size(a) for a in ("patch", "grp", "col"))
    tokens = query_vectors.shape[0] * grps * patches
    if (patches, grps, cores) == (4, 2, 2) and tokens <= 2 * up_weight.shape[1]:
        return gather_plan(*args)
    return shards(*args)


def solution(mesh):
    return jax.shard_map(
        layer,
        mesh=mesh,
        in_specs=(
            P(("parts", "patch", "grp"), "col"),
            P(("parts", "patch", "grp"), "col"),
            P(("parts", "patch", "grp"), "col"),
            P(("parts", "patch", "grp"), "col"),
            P(("parts", "patch", "grp"), None),
            P(("parts", "patch", "grp")),
            P("col", None),
            P("col"),
            P(None, ("grp", "col")),
            P(("grp", "col"), None),
            P(("parts", "patch", "grp"), "col"),
        ),
        out_specs=(
            P(("parts", "patch", "grp"), "col"),
            P("parts", ("grp", "col")),
            P(("parts", "grp", "col"), None),
        ),
        check_vma=False,
    )
```
